32 devices in a mesh: groups: 2 (over y), px: 16 (over z, x, core).
Axes of the slice: x: 2, y: 2, z: 4, core: 2. Of those that a mesh axis runs over, the one named last changes fastest.
Arguments:
- right_side: float32 [262144], P(('groups', 'px')), parts along dimension 0, may hold values from -36 to 36
- self_term: float32 [262144], P(('groups', 'px')), parts along dimension 0, may hold values from 1 to 4
- proj_tiles: float32 [4096, 64, 128], P(('groups', 'px')), parts along dimension 0, may hold values from -0.75 to 0.75
- owner_dev: int32 [4096, 1], P(('groups', 'px')), parts along dimension 0, may hold values from 0 to 15; in each aligned block of 128 rows (0 to 127, 128 to 255, ...) at most 16 rows name the same one
- cube_slot: int32 [4096], P(('groups', 'px')), parts along dimension 0, may hold values from 0 to 8191
- near_src: int32 [4096, 2], P(('groups', 'px')), parts along dimension 0, may hold values from 0 to 191
- near_tiles: float32 [4096, 64, 128], P(('groups', 'px')), parts along dimension 0, may hold values from -0.5 to 0.5
- kernel_hat: float32 [256, 256, 256], P(None, 'px'), may hold values from 0.2 to 2, as said below
Outputs:
- solution: float32 [262144], P(('groups', 'px')), parts along dimension 0
- residual: float32 [262144], P(('groups', 'px')), parts along dimension 0
The draws below stay inside these ranges and needn't reach their ends.
There are 2 independent parts, one for each index of `groups`. The reference program is written for one: setup_inputs(seed, part) draws one part's arguments, and reference() takes and returns one part's arrays. A program takes and returns all parts, laid end to end along the dimension named above; an argument that names none is the same for every part. Nothing has to cross between parts.
Inputs may be any that keep to these rules, and one draw needn't show every extreme that they name: `owner_dev`: among the blocks of one device at most 16 have the same owner, and some device has 16 blocks of one owner. kernel_hat at frequency (k0, k1, k2) equals kernel_hat at ((-k0) mod 256, (-k1) mod 256, (-k2) mod 256).
All inputs are finite; a program needn't handle non-finite values.
Results may differ from the reference program's by a relative error of at most 0.0002.
Values sent between devices are 32-bit elements; how exact they have to be, the bound alone decides.
No kernel may reach another device: no remote copies, remote signals or barrier semaphores. Data moves between devices by JAX's collectives and lax.ppermute only.
A program may use at most 256 MiB of HBM per device.

```python
import math
import jax
import jax.numpy as jnp
import numpy as np
from jax import lax

G = 256
B_DEV = 128
NEAR = 2
RIM = 32
CAP = 16
BLOCKS = 2048
PANELS = 131072
CUBES_DEV = 8192
N_PX = 16


def draw_right_side(key, part):
    key = jax.random.fold_in(key, 11)
    key_scale, key_value = jax.random.split(key)
    position = jnp.arange(PANELS, dtype=jnp.float32) / float(PANELS)
    rising = 1.0 + 2.0 * position
    spread = 0.3 * jnp.exp(math.log(10.0) * jax.random.uniform(key_scale, (PANELS,), jnp.float32))
    values = jnp.clip(jax.random.normal(key_value, (PANELS,), jnp.float32), -4.0, 4.0)
    return spread * rising * values


def draw_kernel_hat(key, part):
    key = jax.random.fold_in(key, 23)
    samples = jnp.exp(jax.random.uniform(key, (G, G, G), jnp.float32, math.log(0.2), math.log(2.0)))
    mirrored = jnp.roll(jnp.flip(samples, (0, 1, 2)), 1, (0, 1, 2))
    return 0.5 * (samples + mirrored)


def place_ends(values, rng, smallest, largest):
    shape = values.shape
    place = [jax.random.randint(jax.random.fold_in(rng, axis), (), 0, shape[axis]) for axis in range(len(shape))]
    values = values.at[tuple(place)].set(smallest)
    longest = shape.index(max(shape))
    place[longest] = (place[longest] + 1) % shape[longest]
    return values.at[tuple(place)].set(largest)


def level_of(rng, shape, cuts, low, top_value):
    factor_of, own = 1.0, jax.random.fold_in(rng, 6)
    for axis_at, blocks in cuts:
        heights = jnp.exp(jax.random.uniform(jax.random.fold_in(own, axis_at), (blocks,), jnp.float32, low / len(cuts), top_value / len(cuts)))
        factor_of = factor_of * jnp.repeat(heights, shape[axis_at] // blocks).reshape([-1 if axis == axis_at else 1 for axis in range(len(shape))])
    return factor_of


def shared_out(key, own, number, rows, amount, top, most, slope):
    order = jax.random.permutation(key, amount)
    heavy_load, ordinary = load_shares(amount, rows * top, most, slope, True), load_shares(amount, rows * top, most, slope, False)
    places = jnp.arange(amount)

    def named(sizes, rotation):
        used = int((sizes > 0).sum())
        fixed = max(1, used // 4)
        shifted = fixed + (places - fixed + rotation * (used - fixed)) % max(1, amount - fixed)
        return jnp.zeros((amount,), jnp.int32).at[order[jnp.where(places < fixed, places, shifted)]].set(jnp.asarray(sizes, jnp.int32))

    sizes = jnp.where(number % 4 == 0, named(heavy_load, number // 4), named(ordinary, number - number // 4 - 1))
    mixed = jax.random.permutation(jax.random.fold_in(own, 3), amount)
    giver, receiver = mixed[0:amount // 2 * 2:2], mixed[1:amount // 2 * 2:2]
    slack = jnp.minimum(sizes[giver] - 1, most - sizes[receiver]) // 2
    slack = jnp.where((giver == order[0]) | (receiver == order[0]) | (sizes[receiver] == 0), 0, jnp.maximum(slack, 0))
    shifted = jax.random.randint(jax.random.fold_in(own, 4), (amount // 2,), 0, 1 << 20) % (slack + 1)
    sizes = sizes.at[giver].add(-shifted).at[receiver].add(shifted)
    members = jnp.searchsorted(jnp.cumsum(sizes), jnp.arange(rows * top), side="right").astype(jnp.int32)
    grid = members.reshape(top, rows).T
    grid = grid[jax.random.permutation(jax.random.fold_in(own, 1), rows)]
    rotation = jax.random.randint(jax.random.fold_in(own, 2), (rows, 1), 0, top)
    return jnp.take_along_axis(grid, (jnp.arange(top)[None, :] + rotation) % top, axis=1)


def load_shares(count, total, limit, skew, full):
    loads = [(1 << 20) // math.isqrt(standing ** skew) + 1 for standing in range(1, count + 1)]
    largest = limit if full else min(limit, max(-(-total // count), total * loads[0] // sum(loads)))
    least = 1 if total - largest >= count - 1 else 0
    counts, spare = [largest] + [least] * (count - 1), total - largest - least * (count - 1)
    while spare > 0:
        free = [i for i in range(1, count) if counts[i] < largest] or [i for i in range(1, count) if counts[i] < limit]
        pool, left = sum([loads[i] for i in free]), spare
        for i in free:
            addition = min(limit - counts[i], max(1, left * loads[i] // pool), spare)
            counts[i] = counts[i] + addition
            spare = spare - addition
    return np.array(counts)


def normal_values(stream_key, dims, scale, limit, cuts=(), kind=jnp.bfloat16):
    values = jax.random.normal(stream_key, dims, jnp.float32) * scale
    if len(cuts) > 0:
        values = level_of(stream_key, dims, cuts, -0.22, 0.18) * values
    return jnp.clip(values, min=-limit, max=limit).astype(kind)


def setup_inputs(seed: int = 0, part: int = 0) -> dict:
    streams_of = jax.random.split(jax.random.key(seed), 9)
    part_splits = jax.random.split(jax.random.fold_in(streams_of[8], part), 9)
    right_side = draw_right_side(jax.random.fold_in(jax.random.fold_in(streams_of[8], part), 71), part)
    self_term = jnp.clip(jnp.exp(math.log(4.0) - 1.3862944 * jax.random.uniform(part_splits[1], (PANELS,), jnp.float32) ** level_of(part_splits[1], (PANELS,), ((0, 16),), -0.2, 0.2)), 1.0, 4.0)
    proj_tiles = normal_values(part_splits[2], (BLOCKS, 64, 128), 64 ** -0.5, 0.75, ((0, 16),), jnp.float32)
    owner_dev_keys = jax.random.split(jax.random.fold_in(part_splits[3], 1), BLOCKS // B_DEV)
    owner_dev_turns = jax.random.permutation(jax.random.fold_in(part_splits[3], 3), BLOCKS // B_DEV)
    owner_dev = jax.vmap(lambda own, number: shared_out(jax.random.fold_in(part_splits[3], 2), own, number, B_DEV, N_PX, 1, CAP, 2))(owner_dev_keys, owner_dev_turns).reshape((BLOCKS, 1))
    cube_slot = place_ends(jax.random.randint(part_splits[4], (BLOCKS,), 0, CUBES_DEV), jax.random.fold_in(part_splits[4], 1), 0, CUBES_DEV - 1).astype(jnp.int32)
    near_src = place_ends(jax.random.randint(part_splits[5], (BLOCKS, NEAR), 0, B_DEV + 2 * RIM), jax.random.fold_in(part_splits[5], 1), 0, (B_DEV + 2 * RIM) - 1).astype(jnp.int32)
    near_tiles = normal_values(part_splits[6], (BLOCKS, 64, NEAR * 64), (64 * NEAR) ** -0.5, 0.5, ((0, 16),), jnp.float32)
    kernel_hat = draw_kernel_hat(jax.random.fold_in(streams_of[8], 71), part)
    return dict(right_side=right_side, self_term=self_term, proj_tiles=proj_tiles, owner_dev=owner_dev, cube_slot=cube_slot, near_src=near_src, near_tiles=near_tiles, kernel_hat=kernel_hat)


def product(pattern, matrix, second):
    return jnp.einsum(pattern, matrix, second, precision=lax.Precision.HIGHEST)

def cube_layout(volume):
    planes = volume.shape[0]
    extent = volume.shape[1]
    shaped = volume.reshape(planes, extent // 8, 8, extent // 16, 16)
    return shaped.transpose(0, 1, 3, 2, 4).reshape(planes * (extent // 8) * (extent // 16), 128)

def grid_layout(cubed, planes, extent):
    shaped = cubed.reshape(planes, extent // 8, extent // 16, 8, 16)
    return shaped.transpose(0, 1, 3, 2, 4).reshape(planes, extent, extent)

def reference(right_side, self_term, proj_tiles, owner_dev, cube_slot, near_src, near_tiles, kernel_hat):
    cube_index = (owner_dev[:, 0] * CUBES_DEV + cube_slot).astype(jnp.int32)
    block_base = jnp.arange(BLOCKS, dtype=jnp.int32) // B_DEV * B_DEV
    source_rows = (block_base[:, None] + near_src).astype(jnp.int32)
    self_local = self_term.reshape(BLOCKS, 64)

    def operator(values):
        charges = product('bpc,bp->bc', proj_tiles, values)
        cubed = jnp.zeros((G * (G // 8) * (G // 16), 128), jnp.float32).at[cube_index].add(charges)
        charge_grid = grid_layout(cubed, G, G)
        spectrum = jnp.fft.fftn(charge_grid)
        far_grid = jnp.real(jnp.fft.ifftn(spectrum * kernel_hat)).astype(jnp.float32)
        picked = cube_layout(far_grid)[cube_index]
        far_part = product('bpc,bc->bp', proj_tiles, picked)
        padded = jnp.pad(values, ((RIM, RIM), (0, 0)))
        sources = padded[source_rows].reshape(BLOCKS, NEAR * 64)
        near_part = product('bpj,bj->bp', near_tiles, sources)
        return self_local * values + near_part + far_part
    rhs_blocks = right_side.reshape(BLOCKS, 64)
    initial_norm = jnp.sqrt(jnp.sum(rhs_blocks * rhs_blocks))
    basis_one = rhs_blocks / initial_norm
    image_one = operator(basis_one)
    diag_one = jnp.sum(basis_one * image_one)
    rest_one = image_one - diag_one * basis_one
    sub_one = jnp.sqrt(jnp.sum(rest_one * rest_one))
    basis_two = rest_one / sub_one
    image_two = operator(basis_two)
    upper_two = jnp.sum(basis_one * image_two)
    diag_two = jnp.sum(basis_two * image_two)
    rest_two = image_two - upper_two * basis_one - diag_two * basis_two
    sub_two_sq = jnp.sum(rest_two * rest_two)
    gram_one = diag_one * diag_one + sub_one * sub_one
    gram_cross = diag_one * upper_two + sub_one * diag_two
    gram_two = upper_two * upper_two + diag_two * diag_two + sub_two_sq
    determinant = gram_one * gram_two - gram_cross * gram_cross
    weight_one = initial_norm * (diag_one * gram_two - upper_two * gram_cross) / determinant
    weight_two = initial_norm * (upper_two * gram_one - diag_one * gram_cross) / determinant
    solution = weight_one * basis_one + weight_two * basis_two
    residual = rhs_blocks - weight_one * image_one - weight_two * image_two
    return (solution.reshape(PANELS), residual.reshape(PANELS))
```

```python
import functools
import jax
import jax.numpy as jnp
import numpy as np
from jax import lax
from jax.experimental import pallas as pl
from jax.experimental.pallas import tpu as pltpu
from jax.sharding import PartitionSpec as P

LANES = 128
CUBE_ROWS = 8
CUBE_COLS = 16


def split(value):
    high = value.astype(jnp.bfloat16)
    low = (value - high.astype(jnp.float32)).astype(jnp.bfloat16)
    return high, low


def split_table(table):
    if isinstance(table, np.ndarray):
        table = table.astype(np.float32)
        high = table.astype(jnp.bfloat16)
        return jnp.asarray(high), jnp.asarray((table - high.astype(np.float32)).astype(jnp.bfloat16))
    high = lax.reduce_precision(table, 8, 7)
    return high.astype(jnp.bfloat16), (table - high).astype(jnp.bfloat16)


def dot_in(left, right):
    return jnp.dot(left, right, preferred_element_type=jnp.float32)


def dot_three(left, right):
    left_high, left_low = left
    right_high, right_low = right
    return dot_in(left_high, right_high) + (
        dot_in(left_low, right_high) + dot_in(left_high, right_low)
    )


def partner_steps(members):
    steps = [1 << i for i in range(members.bit_length() - 1)]
    return steps[2:] + steps[1:2] + steps[:1]


def exchange(value, step):
    members = lax.axis_size("px")
    return lax.ppermute(value, "px", [(i, i ^ step) for i in range(members)])


def gather_pieces(piece):
    pieces = piece
    for step in partner_steps(lax.axis_size("px")):
        pieces = jnp.concatenate([pieces, exchange(pieces, step)], axis=0)
    return pieces


def scatter_pieces(pieces):
    for step in reversed(partner_steps(lax.axis_size("px"))):
        half = pieces.shape[0] // 2
        pieces = pieces[:half] + exchange(pieces[half:], step)
    return pieces


def total(value):
    for step in reversed(partner_steps(lax.axis_size("px"))):
        value = value + exchange(value, step)
    return value


def angle_tables(numerator, extent):
    angle = (2.0 * jnp.pi / extent) * (numerator % extent).astype(jnp.float32)
    return jnp.cos(angle), jnp.sin(angle)


def butterfly16(real, imag, sign):
    def four(a, b, c, d):
        (ar, ai), (br, bi), (cr, ci), (dr, di) = a, b, c, d
        sr, si, tr, ti = ar + cr, ai + ci, ar - cr, ai - ci
        ur, ui, vr, vi = br + dr, bi + di, br - dr, bi - di
        wr, wi = (-vi, vr) if sign > 0 else (vi, -vr)
        return (sr + ur, si + ui), (tr + wr, ti + wi), (sr - ur, si - ui), (tr - wr, ti - wi)

    def turned(value, power):
        power %= 16
        if power == 0:
            return value
        r, i = value
        cosine = float(np.cos(2 * np.pi * power / 16))
        sine = sign * float(np.sin(2 * np.pi * power / 16))
        if power == 4:
            return (-i, r) if sign > 0 else (i, -r)
        return (r * cosine - i * sine, r * sine + i * cosine)

    points = list(zip(real, imag))
    inner = [four(*(points[4 * j1 + j0] for j1 in range(4))) for j0 in range(4)]
    out = [None] * 16
    for b1 in range(4):
        column = [turned(inner[j0][b1], j0 * b1) for j0 in range(4)]
        for b0, value in enumerate(four(*column)):
            out[b1 + 4 * b0] = value
    return [v[0] for v in out], [v[1] for v in out]


def spectral_kernel(
    parts,
    extent,
    chunk,
    rows_ref,
    charge_ref,
    onehot_ref,
    cube_high,
    cube_low,
    back_high,
    back_low,
    turn_high,
    turn_low,
    plane_high,
    plane_low,
    unplane_high,
    unplane_low,
    line_high,
    line_low,
    unline_high,
    unline_low,
    twist_ref,
    filter_ref,
    out_ref,
    *scratch,
):
    grid = scratch[: 2 * parts]
    rows = scratch[2 * parts :]
    count = charge_ref.shape[0]
    width = parts * LANES
    kept = filter_ref.shape[1]
    slabs = extent // CUBE_COLS

    def clear(i, _):
        for ref in grid:
            ref[pl.ds(i * 64, 64), :] = jnp.zeros((64, LANES), jnp.float32)
        return 0

    lax.fori_loop(0, slabs * extent // 64, clear, 0)

    def turns(start):
        picked = onehot_ref[pl.ds(start, chunk), :]
        both = dot_in(picked, turn_high[...]) + dot_in(picked, turn_low[...])
        return both[:, :width], both[:, width:]

    def spread(step, _):
        start = pl.multiple_of(step * chunk, chunk)
        values = split(charge_ref[pl.ds(start, chunk), :])
        both = dot_three(values, (cube_high[...], cube_low[...]))
        real, imag = both[:, :width], both[:, width:]
        cosine, sine = turns(start)
        turned = (real * cosine + imag * sine, imag * cosine - real * sine)
        for part in range(2):
            for half in range(parts):
                rows[part * parts + half][...] = turned[part][:, half * LANES : (half + 1) * LANES]

        def add(i, _):
            row = rows_ref[start + i]
            for ref, source in zip(grid, rows):
                ref[pl.ds(row, 1), :] += source[pl.ds(i, 1), :]
            return 0

        lax.fori_loop(0, chunk, add, 0, unroll=8)
        return 0

    lax.fori_loop(0, count // chunk, spread, 0)

    def across(sign):
        def body(i, _):
            start = pl.multiple_of(i * 8, 8)
            for half in range(parts):
                places = [pl.ds(start + slab * extent, 8) for slab in range(slabs)]
                real = [grid[half][place, :] for place in places]
                imag = [grid[parts + half][place, :] for place in places]
                real, imag = butterfly16(real, imag, sign)
                for place, r, j in zip(places, real, imag):
                    grid[half][place, :] = r
                    grid[parts + half][place, :] = j
            return 0

        lax.fori_loop(0, extent // 8, body, 0)

    across(-1)

    def middle(b, _):
        place = pl.ds(pl.multiple_of(b * extent, extent), extent)
        stacked = jnp.concatenate(
            [
                jnp.concatenate([grid[part * parts + half][place, :] for half in range(parts)], axis=1)
                for part in range(2)
            ],
            axis=0,
        )
        planes = dot_three((plane_high[...], plane_low[...]), split(stacked))
        real, imag = planes[:kept], planes[kept:]
        twist_cos, twist_sin = twist_ref[b, 0:1, :], twist_ref[b, 1:2, :]
        twisted = (real * twist_cos + imag * twist_sin, imag * twist_cos - real * twist_sin)
        back = ([], [])
        for half in range(parts):
            cut = slice(half * LANES, (half + 1) * LANES)
            line = jnp.concatenate([twisted[0][:, cut], twisted[1][:, cut]], axis=1)
            full = dot_three(split(line), (line_high[...], line_low[...]))
            scale = filter_ref[b, :, cut]
            full = full * jnp.concatenate([scale, scale], axis=1)
            full = dot_three(split(full), (unline_high[...], unline_low[...]))
            back[0].append(full[:, :LANES])
            back[1].append(full[:, LANES:])
        real, imag = (jnp.concatenate(values, axis=1) for values in back)
        stacked = jnp.concatenate(
            [real * twist_cos - imag * twist_sin, imag * twist_cos + real * twist_sin], axis=0
        )
        planes = dot_three((unplane_high[...], unplane_low[...]), split(stacked))
        for part in range(2):
            for half in range(parts):
                grid[part * parts + half][place, :] = planes[
                    part * extent : (part + 1) * extent, half * LANES : (half + 1) * LANES
                ]
        return 0

    lax.fori_loop(0, slabs, middle, 0)
    across(1)

    def collect(step, _):
        start = pl.multiple_of(step * chunk, chunk)

        def take(i, _):
            row = rows_ref[start + i]
            for ref, source in zip(rows, grid):
                ref[pl.ds(i, 1), :] = source[pl.ds(row, 1), :]
            return 0

        lax.fori_loop(0, chunk, take, 0, unroll=8)
        cosine, sine = turns(start)
        real = jnp.concatenate([rows[half][...] for half in range(parts)], axis=1)
        imag = jnp.concatenate([rows[parts + half][...] for half in range(parts)], axis=1)
        both = jnp.concatenate([real * cosine - imag * sine, imag * cosine + real * sine], axis=1)
        out_ref[pl.ds(start, chunk), :] = dot_three(split(both), (back_high[...], back_low[...]))
        return 0

    lax.fori_loop(0, count // chunk, collect, 0)


def spectral_tables(kernel_local):
    members = lax.axis_size("px")
    extent = kernel_local.shape[0]
    slab = kernel_local.shape[1]
    padded_slab = max(LANES // CUBE_COLS, slab)
    width = padded_slab * CUBE_COLS
    first = lax.axis_index("px") * slab
    column = jnp.arange(width, dtype=jnp.int32)
    k1 = first + column // CUBE_COLS
    real_slab = (column // CUBE_COLS < slab).astype(jnp.float32)
    point = jnp.arange(CUBE_ROWS * CUBE_COLS, dtype=jnp.int32)
    cosine, sine = angle_tables((point // CUBE_COLS)[:, None] * k1[None, :], extent)
    same = (point[:, None] % CUBE_COLS == column[None, :] % CUBE_COLS) * real_slab[None, :]
    cube = jnp.concatenate([cosine * same, -sine * same], axis=1)
    turn_row = jnp.arange(extent // CUBE_ROWS, dtype=jnp.int32) * CUBE_ROWS
    cosine, sine = angle_tables(turn_row[:, None] * k1[None, :], extent)
    turn = jnp.concatenate([cosine, sine], axis=1)
    kept = -(-(extent // 2 + 1) // 8) * 8
    n0 = np.arange(extent)
    k0 = np.arange(kept)
    angle = 2.0 * np.pi / extent * (k0[:, None] * n0[None, :] % extent)
    cosine, sine = np.cos(angle), np.sin(angle)
    plane = np.block([[cosine, sine], [-sine, cosine]])
    unplane = np.block([[cosine.T, -sine.T], [sine.T, cosine.T]])
    inside = LANES // CUBE_COLS
    small = np.arange(CUBE_COLS)
    angle = 2.0 * np.pi / CUBE_COLS * (small[:, None] * small[None, :] % CUBE_COLS)
    cosine = np.kron(np.eye(inside), np.cos(angle))
    sine = np.kron(np.eye(inside), np.sin(angle))
    line = np.block([[cosine, -sine], [sine, cosine]])
    unline = np.block([[cosine, sine], [-sine, cosine]])
    lane = np.arange(width) % CUBE_COLS
    angle = 2.0 * np.pi / extent * (small[:, None] * lane[None, :])
    twist = np.stack([np.cos(angle), np.sin(angle)], axis=1)
    weight = np.where((k0 == 0) | (k0 == extent // 2), 1.0, 2.0) * (k0 <= extent // 2)
    weight = weight / float(extent) ** 3
    filters = kernel_local[:kept] * jnp.asarray(weight, jnp.float32)[:, None, None]
    filters = jnp.pad(filters, ((0, 0), (0, padded_slab - slab), (0, 0)))
    filters = filters.reshape(kept, padded_slab, extent // CUBE_COLS, CUBE_COLS)
    filters = filters.transpose(3, 0, 1, 2).reshape(CUBE_COLS, kept, width)
    tables = []
    for table in (cube, cube.T, turn, plane, unplane, line, unline):
        tables.extend(split_table(table))
    return tables + [jnp.asarray(twist, jnp.float32), filters]


def spectral(cubes, extent, charges, tables):
    count = charges.shape[0]
    width = tables[-1].shape[2]
    parts = width // LANES
    slabs = extent // CUBE_COLS
    per_plane = (extent // CUBE_ROWS) * slabs
    rows = (cubes % slabs) * extent + cubes // per_plane
    turn_index = cubes // slabs % (extent // CUBE_ROWS)
    onehot = (
        turn_index[:, None] == jnp.arange(extent // CUBE_ROWS, dtype=jnp.int32)[None, :]
    ).astype(jnp.bfloat16)
    chunk = 512
    whole = pl.BlockSpec(memory_space=pltpu.VMEM)
    return pl.pallas_call(
        functools.partial(spectral_kernel, parts, extent, chunk),
        out_shape=jax.ShapeDtypeStruct((count, LANES), jnp.float32),
        in_specs=[pl.BlockSpec(memory_space=pltpu.SMEM)] + [whole] * (2 + len(tables)),
        out_specs=whole,
        scratch_shapes=[pltpu.VMEM((slabs * extent, LANES), jnp.float32)] * (2 * parts)
        + [pltpu.VMEM((chunk, LANES), jnp.float32)] * (2 * parts),
        compiler_params=pltpu.CompilerParams(vmem_limit_bytes=48 * 1024 * 1024),
        name="spectral",
    )(rows, charges, onehot, *tables)


def halo(cells, width):
    count = lax.axis_size("px")
    ends = count - 1
    return jnp.concatenate(
        [
            lax.ppermute(cells[-width:], "px", [(i, i + 1) for i in range(ends)]),
            cells,
            lax.ppermute(cells[:width], "px", [(i + 1, i) for i in range(ends)]),
        ],
        axis=0,
    )


def on_device(
    right_side, self_term, proj_tiles, owner_dev, cube_slot, near_src, near_tiles, kernel_hat
):
    members = lax.axis_size("px")
    blocks = proj_tiles.shape[0]
    extent = kernel_hat.shape[0]
    cubes_dev = extent // members * (extent // CUBE_ROWS) * (extent // CUBE_COLS)
    self_local = self_term.reshape(blocks, 64)
    cubes = owner_dev[:, 0] * cubes_dev + cube_slot
    tables = spectral_tables(kernel_hat)
    all_cubes = gather_pieces(cubes.reshape(1, blocks)).reshape(members * blocks)

    def operator(values):
        charges = jnp.sum(proj_tiles * values[:, :, None], axis=1)
        gathered = gather_pieces(charges)
        picked = scatter_pieces(spectral(all_cubes, extent, gathered, tables))
        sources = halo(values, blocks // 4)[near_src].reshape(blocks, near_tiles.shape[2])
        return (
            self_local * values
            + jnp.sum(near_tiles * sources[:, None, :], axis=2)
            + jnp.sum(proj_tiles * picked[:, None, :], axis=2)
        )

    rhs = right_side.reshape(blocks, 64)
    first = operator(rhs)
    sums = total(
        jnp.stack([jnp.sum(rhs * rhs), jnp.sum(rhs * first), jnp.sum(first * first)]).reshape(1, 3)
    )
    second = operator(first)
    initial_norm = jnp.sqrt(sums[0, 0])
    diag_one = sums[0, 1] / sums[0, 0]
    gram_one = sums[0, 2] / sums[0, 0]
    scale = jnp.sqrt(gram_one)
    basis_one = rhs / initial_norm
    image_one = first / initial_norm
    basis_two = (image_one - diag_one * basis_one) / scale
    image_two = (second / initial_norm - diag_one * image_one) / scale
    sums = total(
        jnp.stack(
            [
                jnp.sum(basis_one * image_two),
                jnp.sum(image_one * image_two),
                jnp.sum(image_two * image_two),
            ]
        ).reshape(1, 3)
    )
    upper_two, gram_cross, gram_two = sums[0, 0], sums[0, 1], sums[0, 2]
    determinant = gram_one * gram_two - gram_cross * gram_cross
    weight_one = initial_norm * (diag_one * gram_two - upper_two * gram_cross) / determinant
    weight_two = initial_norm * (upper_two * gram_one - diag_one * gram_cross) / determinant
    answer = weight_one * basis_one + weight_two * basis_two
    residual = rhs - weight_one * image_one - weight_two * image_two
    return (answer.reshape(blocks * 64), residual.reshape(blocks * 64))


def solution(mesh):
    return jax.shard_map(
        on_device,
        mesh=mesh,
        in_specs=(
            P(("groups", "px")),
            P(("groups", "px")),
            P(("groups", "px"), None, None),
            P(("groups", "px"), None),
            P(("groups", "px")),
            P(("groups", "px"), None),
            P(("groups", "px"), None, None),
            P(None, "px", None),
        ),
        out_specs=(P(("groups", "px")), P(("groups", "px"))),
        check_vma=False,
    )
```

```python
import functools
import jax
import jax.numpy as jnp
import numpy as np
from jax import lax
from jax.experimental import pallas as pl
from jax.experimental.pallas import tpu as pltpu
from jax.sharding import PartitionSpec as P

LANES = 128
CUBE_ROWS = 8
CUBE_COLS = 16


def split(value):
    high = value.astype(jnp.bfloat16)
    low = (value - high.astype(jnp.float32)).astype(jnp.bfloat16)
    return high, low


def split_table(table):
    if isinstance(table, np.ndarray):
        table = table.astype(np.float32)
        high = table.astype(jnp.bfloat16)
        return jnp.asarray(high), jnp.asarray((table - high.astype(np.float32)).astype(jnp.bfloat16))
    high = lax.reduce_precision(table, 8, 7)
    return high.astype(jnp.bfloat16), (table - high).astype(jnp.bfloat16)


def dot_in(left, right):
    return jnp.dot(left, right, preferred_element_type=jnp.float32)


def dot_three(left, right):
    left_high, left_low = left
    right_high, right_low = right
    return dot_in(
        jnp.concatenate([left_high, left_low, left_high], axis=1),
        jnp.concatenate([right_high, right_high, right_low], axis=0),
    )


def partner_steps(members):
    return [1 << i for i in reversed(range(members.bit_length() - 1))]


def exchange(value, step):
    members = lax.axis_size("px")
    return lax.ppermute(value, "px", [(i, i ^ step) for i in range(members)])


def gather_pieces(piece, beside):
    steps = partner_steps(lax.axis_size("px"))
    pieces = piece[None]
    for step in steps[:-1]:
        pieces = jnp.concatenate([pieces, exchange(pieces, step)], axis=0)
    pieces, beside = lax.optimization_barrier((pieces, beside))
    return (pieces, exchange(pieces, steps[-1])), beside


def scatter_pieces(kept, sent):
    steps = list(reversed(partner_steps(lax.axis_size("px"))))
    pieces = kept + exchange(sent, steps[0])
    for step in steps[1:]:
        half = pieces.shape[0] // 2
        pieces = pieces[:half] + exchange(pieces[half:], step)
    return pieces


def total(value):
    for step in reversed(partner_steps(lax.axis_size("px"))):
        value = value + exchange(value, step)
    return value


def angle_tables(numerator, extent):
    angle = (2.0 * jnp.pi / extent) * (numerator % extent).astype(jnp.float32)
    return jnp.cos(angle), jnp.sin(angle)


def butterfly16(real, imag, sign):
    def four(a, b, c, d):
        (ar, ai), (br, bi), (cr, ci), (dr, di) = a, b, c, d
        sr, si, tr, ti = ar + cr, ai + ci, ar - cr, ai - ci
        ur, ui, vr, vi = br + dr, bi + di, br - dr, bi - di
        wr, wi = (-vi, vr) if sign > 0 else (vi, -vr)
        return (sr + ur, si + ui), (tr + wr, ti + wi), (sr - ur, si - ui), (tr - wr, ti - wi)

    def turned(value, power):
        power %= 16
        if power == 0:
            return value
        r, i = value
        cosine = float(np.cos(2 * np.pi * power / 16))
        sine = sign * float(np.sin(2 * np.pi * power / 16))
        if power == 4:
            return (-i, r) if sign > 0 else (i, -r)
        return (r * cosine - i * sine, r * sine + i * cosine)

    points = list(zip(real, imag))
    inner = [four(*(points[4 * j1 + j0] for j1 in range(4))) for j0 in range(4)]
    out = [None] * 16
    for b1 in range(4):
        column = [turned(inner[j0][b1], j0 * b1) for j0 in range(4)]
        for b0, value in enumerate(four(*column)):
            out[b1 + 4 * b0] = value
    return [v[0] for v in out], [v[1] for v in out]


def spectral_kernel(
    parts,
    extent,
    chunk,
    rows_ref,
    near_ref,
    distant_ref,
    onehot_ref,
    cube_high,
    cube_low,
    back_high,
    back_low,
    turn_high,
    turn_low,
    even_high,
    even_low,
    odd_high,
    odd_low,
    uneven_high,
    uneven_low,
    unodd_high,
    unodd_low,
    line_high,
    line_low,
    unline_high,
    unline_low,
    twist_ref,
    filter_ref,
    kept_ref,
    sent_ref,
    *scratch,
):
    grid = scratch[: 2 * parts]
    twin = scratch[2 * parts : 4 * parts]
    rows = scratch[4 * parts :]
    half_count = kept_ref.shape[0]
    pieces = near_ref.shape[0]
    blocks = half_count // pieces
    width = parts * LANES
    evens, odds = even_high.shape[0] // 2, odd_high.shape[0] // 2
    slabs = extent // CUBE_COLS

    def clear(i, _):
        for ref in grid + twin:
            ref[pl.ds(i * 64, 64), :] = jnp.zeros((64, LANES), jnp.float32)
        return 0

    lax.fori_loop(0, slabs * extent // 64, clear, 0)

    def turns(start):
        picked = onehot_ref[pl.ds(start, chunk), :]
        both = dot_in(picked, turn_high[...]) + dot_in(picked, turn_low[...])
        return both[:, :width], both[:, width:]

    def spread(source_ref, offset, step, _):
        start = pl.multiple_of(offset + step * chunk, chunk)
        taken = source_ref[pl.ds(step * (chunk // blocks), chunk // blocks), :blocks, :]
        values = split(taken.reshape(chunk, LANES))
        both = dot_three(values, (cube_high[...], cube_low[...]))
        real, imag = both[:, :width], both[:, width:]
        cosine, sine = turns(start)
        turned = (real * cosine + imag * sine, imag * cosine - real * sine)
        for part in range(2):
            for half in range(parts):
                rows[part * parts + half][...] = turned[part][:, half * LANES : (half + 1) * LANES]

        def add(i, _):
            for refs, place in ((grid, i), (twin, i + chunk // 2)):
                row = rows_ref[start + place]
                for ref, source in zip(refs, rows):
                    ref[pl.ds(row, 1), :] += source[pl.ds(place, 1), :]
            return 0

        lax.fori_loop(0, chunk // 2, add, 0, unroll=8)
        return 0

    for index, source_ref in enumerate((near_ref, distant_ref)):
        body = functools.partial(spread, source_ref, index * half_count)
        lax.fori_loop(0, half_count // chunk, body, 0)

    def across(sign):
        def body(i, _):
            start = pl.multiple_of(i * 8, 8)
            for half in range(parts):
                places = [pl.ds(start + slab * extent, 8) for slab in range(slabs)]
                real = [grid[half][place, :] for place in places]
                imag = [grid[parts + half][place, :] for place in places]
                if sign < 0:
                    real = [r + twin[half][place, :] for r, place in zip(real, places)]
                    imag = [r + twin[parts + half][place, :] for r, place in zip(imag, places)]
                real, imag = butterfly16(real, imag, sign)
                for place, r, j in zip(places, real, imag):
                    grid[half][place, :] = r
                    grid[parts + half][place, :] = j
            return 0

        lax.fori_loop(0, extent // 8, body, 0)

    across(-1)

    def middle(b, _):
        low = pl.ds(pl.multiple_of(b * extent, extent), extent // 2)
        high = pl.ds(pl.multiple_of(b * extent + extent // 2, extent // 2), extent // 2)

        def joined(place):
            return jnp.concatenate(
                [
                    jnp.concatenate(
                        [grid[part * parts + half][place, :] for half in range(parts)], axis=1
                    )
                    for part in range(2)
                ],
                axis=0,
            )

        first, last = joined(low), joined(high)
        even = dot_three((even_high[...], even_low[...]), split(first + last))
        odd = dot_three((odd_high[...], odd_low[...]), split(first - last))
        real = jnp.concatenate([even[:evens], odd[:odds]], axis=0)
        imag = jnp.concatenate([even[evens:], odd[odds:]], axis=0)
        twist_cos, twist_sin = twist_ref[b, 0:1, :], twist_ref[b, 1:2, :]
        twisted = (real * twist_cos + imag * twist_sin, imag * twist_cos - real * twist_sin)
        back = ([], [])
        for half in range(parts):
            cut = slice(half * LANES, (half + 1) * LANES)
            line = jnp.concatenate([twisted[0][:, cut], twisted[1][:, cut]], axis=1)
            full = dot_three(split(line), (line_high[...], line_low[...]))
            scale = filter_ref[b, :, cut]
            full = full * jnp.concatenate([scale, scale], axis=1)
            full = dot_three(split(full), (unline_high[...], unline_low[...]))
            back[0].append(full[:, :LANES])
            back[1].append(full[:, LANES:])
        real, imag = (jnp.concatenate(values, axis=1) for values in back)
        real, imag = real * twist_cos - imag * twist_sin, imag * twist_cos + real * twist_sin
        even = jnp.concatenate([real[:evens], imag[:evens]], axis=0)
        odd = jnp.concatenate([real[evens:], imag[evens:]], axis=0)
        even = dot_three((uneven_high[...], uneven_low[...]), split(even))
        odd = dot_three((unodd_high[...], unodd_low[...]), split(odd))
        for place, planes in ((low, even + odd), (high, even - odd)):
            for part in range(2):
                for half in range(parts):
                    grid[part * parts + half][place, :] = planes[
                        part * (extent // 2) : (part + 1) * (extent // 2),
                        half * LANES : (half + 1) * LANES,
                    ]
        return 0

    lax.fori_loop(0, slabs, middle, 0, unroll=4)
    across(1)

    def collect(out_ref, offset, step, _):
        start = pl.multiple_of(offset + step * chunk, chunk)

        def take(i, _):
            row = rows_ref[start + i]
            for ref, source in zip(rows, grid):
                ref[pl.ds(i, 1), :] = source[pl.ds(row, 1), :]
            return 0

        lax.fori_loop(0, chunk, take, 0, unroll=8)
        cosine, sine = turns(start)
        real = jnp.concatenate([rows[half][...] for half in range(parts)], axis=1)
        imag = jnp.concatenate([rows[parts + half][...] for half in range(parts)], axis=1)
        both = jnp.concatenate([real * cosine - imag * sine, imag * cosine + real * sine], axis=1)
        out_ref[pl.ds(pl.multiple_of(step * chunk, chunk), chunk), :] = dot_three(split(both), (back_high[...], back_low[...]))
        return 0

    for index, out_ref in enumerate((kept_ref, sent_ref)):
        body = functools.partial(collect, out_ref, index * half_count)
        lax.fori_loop(0, half_count // chunk, body, 0)


def spectral_tables(kernel_local):
    members = lax.axis_size("px")
    extent = kernel_local.shape[0]
    slab = kernel_local.shape[1]
    padded_slab = max(LANES // CUBE_COLS, slab)
    width = padded_slab * CUBE_COLS
    first = lax.axis_index("px") * slab
    column = jnp.arange(width, dtype=jnp.int32)
    k1 = first + column // CUBE_COLS
    real_slab = (column // CUBE_COLS < slab).astype(jnp.float32)
    point = jnp.arange(CUBE_ROWS * CUBE_COLS, dtype=jnp.int32)
    cosine, sine = angle_tables((point // CUBE_COLS)[:, None] * k1[None, :], extent)
    same = (point[:, None] % CUBE_COLS == column[None, :] % CUBE_COLS) * real_slab[None, :]
    cube = jnp.concatenate([cosine * same, -sine * same], axis=1)
    turn_row = jnp.arange(extent // CUBE_ROWS, dtype=jnp.int32) * CUBE_ROWS
    cosine, sine = angle_tables(turn_row[:, None] * k1[None, :], extent)
    turn = jnp.concatenate([cosine, sine], axis=1)
    half = extent // 2
    n0 = np.arange(half)
    k0_even = np.arange(0, -(-(half // 2 + 1) // 8) * 16, 2)
    k0_odd = np.arange(1, half, 2)
    k0 = np.concatenate([k0_even, k0_odd])
    planes = []
    for k0_part in (k0_even, k0_odd):
        angle = 2.0 * np.pi / extent * (k0_part[:, None] * n0[None, :] % extent)
        cosine, sine = np.cos(angle), np.sin(angle)
        planes.append(np.block([[cosine, sine], [-sine, cosine]]))
    inside = LANES // CUBE_COLS
    small = np.arange(CUBE_COLS)
    angle = 2.0 * np.pi / CUBE_COLS * (small[:, None] * small[None, :] % CUBE_COLS)
    cosine = np.kron(np.eye(inside), np.cos(angle))
    sine = np.kron(np.eye(inside), np.sin(angle))
    line = np.block([[cosine, -sine], [sine, cosine]])
    unline = np.block([[cosine, sine], [-sine, cosine]])
    lane = np.arange(width) % CUBE_COLS
    angle = 2.0 * np.pi / extent * (small[:, None] * lane[None, :])
    twist = np.stack([np.cos(angle), np.sin(angle)], axis=1)
    weight = np.where((k0 == 0) | (k0 == half), 1.0, 2.0) * (k0 <= half)
    weight = weight / float(extent) ** 3
    filters = jnp.concatenate(
        [kernel_local[: k0_even[-1] + 1 : 2], kernel_local[1:half:2]], axis=0
    )
    filters = filters * jnp.asarray(weight, jnp.float32)[:, None, None]
    filters = jnp.pad(filters, ((0, 0), (0, padded_slab - slab), (0, 0)))
    filters = filters.reshape(len(k0), padded_slab, extent // CUBE_COLS, CUBE_COLS)
    filters = filters.transpose(3, 0, 1, 2).reshape(CUBE_COLS, len(k0), width)
    tables = []
    for table in (cube, cube.T, turn, *planes, *(plane.T for plane in planes), line, unline):
        tables.extend(split_table(table))
    return tables + [jnp.asarray(twist, jnp.float32), filters]


def cube_places(cubes, extent):
    slabs = extent // CUBE_COLS
    turns = extent // CUBE_ROWS
    rows = (cubes % slabs) * extent + cubes // (turns * slabs)
    turn_index = cubes // slabs % turns
    onehot = turn_index[:, None] == jnp.arange(turns, dtype=jnp.int32)[None, :]
    return rows, onehot.astype(jnp.bfloat16)


def spectral(places, extent, blocks, gathered, tables):
    half_count = gathered[0].shape[0] * blocks
    parts = tables[-1].shape[2] // LANES
    slabs = extent // CUBE_COLS
    chunk = min(512, half_count)
    whole = pl.BlockSpec(memory_space=pltpu.VMEM)
    out = jax.ShapeDtypeStruct((half_count, LANES), jnp.float32)
    return pl.pallas_call(
        functools.partial(spectral_kernel, parts, extent, chunk),
        out_shape=(out, out),
        in_specs=[pl.BlockSpec(memory_space=pltpu.SMEM)] + [whole] * (3 + len(tables)),
        out_specs=(whole, whole),
        scratch_shapes=[pltpu.VMEM((slabs * extent, LANES), jnp.float32)] * (4 * parts)
        + [pltpu.VMEM((chunk, LANES), jnp.float32)] * (2 * parts),
        compiler_params=pltpu.CompilerParams(vmem_limit_bytes=56 * 1024 * 1024),
        name="spectral",
    )(places[0], *gathered, places[1], *tables)


NOTE_ROWS = 8
STEP_BLOCKS = 16
RIM_PART = 4


def sum_row(*values):
    lane = lax.broadcasted_iota(jnp.int32, (1, LANES), 1)
    row = jnp.zeros((1, LANES), jnp.float32)
    for index, value in enumerate(values):
        row = jnp.where(lane == index, value, row)
    return row


def put_edges(out_ref, values):
    step, steps = pl.program_id(0), pl.num_programs(0)
    panels = values.shape[1]
    below = out_ref.shape[0] - steps * STEP_BLOCKS // RIM_PART

    for first, lanes in ((0, slice(0, panels)), (steps - steps // RIM_PART, slice(panels, 2 * panels))):

        @pl.when((step >= first) & (step < first + steps // RIM_PART))
        def _():
            row = pl.multiple_of(below + (step - first) * STEP_BLOCKS, 8)
            out_ref[pl.ds(row, STEP_BLOCKS), lanes] = values


def project_kernel(proj_ref, values_ref, note_ref, out_ref):
    step = pl.program_id(0)
    charges = jnp.sum(proj_ref[...] * values_ref[...][:, :, None], axis=1)
    out_ref[pl.ds(pl.multiple_of(step * STEP_BLOCKS, STEP_BLOCKS), STEP_BLOCKS), :] = charges

    put_edges(out_ref, values_ref[...])

    @pl.when(step == pl.num_programs(0) - 1)
    def _():
        blocks = pl.num_programs(0) * STEP_BLOCKS
        out_ref[blocks : blocks + NOTE_ROWS, :] = jnp.broadcast_to(
            note_ref[...], (NOTE_ROWS, LANES)
        )


def complete_kernel(proj_ref, picked_ref, base_ref, rhs_ref, image_ref, out_ref):
    step = pl.program_id(0)
    tiles = proj_ref[...]
    image = base_ref[...] + jnp.sum(tiles * picked_ref[...][:, None, :], axis=2)
    image_ref[...] = image
    charges = jnp.sum(tiles * image[:, :, None], axis=1)
    out_ref[pl.ds(pl.multiple_of(step * STEP_BLOCKS, STEP_BLOCKS), STEP_BLOCKS), :] = charges
    put_edges(out_ref, image)
    blocks = pl.num_programs(0) * STEP_BLOCKS
    rhs = rhs_ref[...]
    row = sum_row(jnp.sum(rhs * rhs), jnp.sum(rhs * image), jnp.sum(image * image))

    @pl.when(step == 0)
    def _():
        out_ref[blocks : blocks + NOTE_ROWS, :] = jnp.zeros((NOTE_ROWS, LANES), jnp.float32)

    out_ref[blocks : blocks + 1, :] += row


def vector_scalars(sums):
    norm_sq, mixed, image_sq = sums[0:1, 0:1], sums[0:1, 1:2], sums[0:1, 2:3]
    gram_one = image_sq / norm_sq
    return jnp.sqrt(norm_sq), mixed / norm_sq, gram_one, jnp.sqrt(gram_one)


def close_kernel(proj_ref, picked_ref, base_ref, rhs_ref, first_ref, sums_ref, image_ref, out_ref):
    step = pl.program_id(0)
    second = base_ref[...] + jnp.sum(proj_ref[...] * picked_ref[...][:, None, :], axis=2)
    initial_norm, diag_one, _, scale = vector_scalars(sums_ref[...])
    basis_one = rhs_ref[...] / initial_norm
    image_one = first_ref[...] / initial_norm
    image_two = (second / initial_norm - diag_one * image_one) / scale
    image_ref[...] = image_two
    row = sum_row(
        jnp.sum(basis_one * image_two),
        jnp.sum(image_one * image_two),
        jnp.sum(image_two * image_two),
    )

    @pl.when(step == 0)
    def _():
        out_ref[...] = jnp.zeros((NOTE_ROWS, LANES), jnp.float32)

    out_ref[0:1, :] += row


def finish_kernel(rhs_ref, first_ref, image_ref, sums_ref, last_ref, answer_ref, residual_ref, rows_ref):
    initial_norm, diag_one, gram_one, scale = vector_scalars(sums_ref[...])
    last = last_ref[...]
    upper_two, gram_cross, gram_two = last[0:1, 0:1], last[0:1, 1:2], last[0:1, 2:3]
    rhs = rhs_ref[...]
    basis_one = rhs / initial_norm
    image_one = first_ref[...] / initial_norm
    basis_two = (image_one - diag_one * basis_one) / scale
    determinant = gram_one * gram_two - gram_cross * gram_cross
    weight_one = initial_norm * (diag_one * gram_two - upper_two * gram_cross) / determinant
    weight_two = initial_norm * (upper_two * gram_one - diag_one * gram_cross) / determinant
    half = rhs.shape[0] // 2
    for out_ref, value in (
        (answer_ref, weight_one * basis_one + weight_two * basis_two),
        (residual_ref, rhs - weight_one * image_one - weight_two * image_ref[...]),
    ):
        rows_ref[...] = value
        out_ref[...] = jnp.concatenate(
            [rows_ref[pl.ds(side, half, stride=2), :] for side in range(2)], axis=1
        )


def local_call(kernel, name, proj_tiles, rows, whole, outs):
    blocks, panels, points = proj_tiles.shape

    def cut(width):
        return pl.BlockSpec((STEP_BLOCKS, width), lambda i: (i, 0))

    def uncut(shape):
        return pl.BlockSpec(shape, lambda i: (0, 0))

    out_specs = [cut(out[1]) if out[0] == blocks else uncut(out) for out in outs]
    return pl.pallas_call(
        kernel,
        grid=(blocks // STEP_BLOCKS,),
        out_shape=[jax.ShapeDtypeStruct(out, jnp.float32) for out in outs],
        in_specs=[pl.BlockSpec((STEP_BLOCKS, panels, points), lambda i: (i, 0, 0))]
        + [cut(row.shape[1]) for row in rows]
        + [uncut(value.shape) for value in whole],
        out_specs=out_specs,
        cost_estimate=pl.CostEstimate(
            flops=4 * proj_tiles.size, bytes_accessed=4 * proj_tiles.size, transcendentals=0
        ),
        compiler_params=pltpu.CompilerParams(vmem_limit_bytes=16 * 1024 * 1024),
        name=name,
    )(proj_tiles, *rows, *whole)


def piece_place(device):
    steps = partner_steps(lax.axis_size("px"))[:-1]
    away = lax.axis_index("px") ^ device
    return sum((away // step % 2) << place for place, step in enumerate(steps))


def halo(cells, distant):
    me, members = lax.axis_index("px"), lax.axis_size("px")
    width = cells.shape[0] // RIM_PART
    panels = cells.shape[1]
    sides = []
    for device, lane, present in ((me - 1, panels, me > 0), (me + 1, 0, me < members - 1)):
        place = jnp.where(present, piece_place(device), 0)
        start = (place, distant.shape[1] - width, lane)
        edge = lax.dynamic_slice(distant, start, (1, width, panels))[0]
        sides.append(jnp.where(present, edge, 0.0))
    return jnp.concatenate([sides[0], cells, sides[1]], axis=0)


def on_device(
    right_side, self_term, proj_tiles, owner_dev, cube_slot, near_src, near_tiles, kernel_hat
):
    members = lax.axis_size("px")
    blocks = proj_tiles.shape[0]
    extent = kernel_hat.shape[0]
    cubes_dev = extent // members * (extent // CUBE_ROWS) * (extent // CUBE_COLS)
    self_local = self_term.reshape(blocks, 64)
    cubes = owner_dev[:, 0] * cubes_dev + cube_slot
    tables = spectral_tables(kernel_hat)

    rhs = right_side.reshape(blocks, 64)
    note_shape = (blocks + NOTE_ROWS + blocks // RIM_PART, LANES)

    def base_of(values, gathered):
        sources = halo(values, gathered[1])[near_src].reshape(blocks, near_tiles.shape[2])
        return self_local * values + jnp.sum(near_tiles * sources[:, None, :], axis=2)

    def far(places, gathered):
        return scatter_pieces(*spectral(places, extent, blocks, gathered, tables))

    note = jnp.pad(cubes.astype(jnp.float32)[None, :], ((0, 0), (0, LANES - blocks)))
    (payload,) = local_call(project_kernel, "project", proj_tiles, [rhs], [note], [note_shape])
    gathered, tables = gather_pieces(payload, tables)
    base = base_of(rhs, gathered)
    all_cubes = jnp.concatenate([half[:, blocks, :blocks] for half in gathered], axis=0)
    places = cube_places(all_cubes.astype(jnp.int32).reshape(members * blocks), extent)
    first, payload = local_call(
        complete_kernel,
        "complete",
        proj_tiles,
        [far(places, gathered), base, rhs],
        [],
        [(blocks, 64), note_shape],
    )
    gathered, _ = gather_pieces(payload, ())
    base = base_of(first, gathered)
    sums = sum(jnp.sum(half[:, blocks, :], axis=0, keepdims=True) for half in gathered)
    image, last = local_call(
        close_kernel,
        "close",
        proj_tiles,
        [far(places, gathered), base, rhs, first],
        [sums],
        [(blocks, 64), (NOTE_ROWS, LANES)],
    )
    last = total(last)
    out = jax.ShapeDtypeStruct((blocks // 2, 128), jnp.float32)
    answer, residual = pl.pallas_call(
        finish_kernel,
        out_shape=(out, out),
        scratch_shapes=[pltpu.VMEM((blocks, 64), jnp.float32)],
        name="finish",
    )(rhs, first, image, sums, last)
    return (answer.reshape(blocks * 64), residual.reshape(blocks * 64))


def solution(mesh):
    return jax.shard_map(
        on_device,
        mesh=mesh,
        in_specs=(
            P(("groups", "px")),
            P(("groups", "px")),
            P(("groups", "px"), None, None),
            P(("groups", "px"), None),
            P(("groups", "px")),
            P(("groups", "px"), None),
            P(("groups", "px"), None, None),
            P(None, "px", None),
        ),
        out_specs=(P(("groups", "px")), P(("groups", "px"))),
        check_vma=False,
    )
```

```python
import functools
import jax
import jax.numpy as jnp
import numpy as np
from jax import lax
from jax.experimental import pallas as pl
from jax.experimental.pallas import tpu as pltpu
from jax.sharding import PartitionSpec as P

LANES = 128
CUBE_ROWS = 8
CUBE_COLS = 16


def split(value):
    high = value.astype(jnp.bfloat16)
    low = (value - high.astype(jnp.float32)).astype(jnp.bfloat16)
    return high, low


def dot_in(left, right):
    return jnp.dot(left, right, preferred_element_type=jnp.float32)


def partner_steps(members):
    return [1 << i for i in reversed(range(members.bit_length() - 1))]


def exchange(value, step):
    members = lax.axis_size("px")
    return lax.ppermute(value, "px", [(i, i ^ step) for i in range(members)])


def gather_pieces(piece, beside):
    steps = partner_steps(lax.axis_size("px"))
    pieces = piece[None]
    for step in steps[:-1]:
        pieces = jnp.concatenate([pieces, exchange(pieces, step)], axis=0)
    pieces, beside = lax.optimization_barrier((pieces, beside))
    return (pieces, exchange(pieces, steps[-1])), beside


def scatter_pieces(kept, sent):
    steps = list(reversed(partner_steps(lax.axis_size("px"))))
    pieces = kept + exchange(sent, steps[0])
    for step in steps[1:]:
        half = pieces.shape[0] // 2
        pieces = pieces[:half] + exchange(pieces[half:], step)
    return pieces


def total(value):
    for step in reversed(partner_steps(lax.axis_size("px"))):
        value = value + exchange(value, step)
    return value


def butterfly16(real, imag, sign):
    def four(a, b, c, d):
        (ar, ai), (br, bi), (cr, ci), (dr, di) = a, b, c, d
        sr, si, tr, ti = ar + cr, ai + ci, ar - cr, ai - ci
        ur, ui, vr, vi = br + dr, bi + di, br - dr, bi - di
        wr, wi = (-vi, vr) if sign > 0 else (vi, -vr)
        return (sr + ur, si + ui), (tr + wr, ti + wi), (sr - ur, si - ui), (tr - wr, ti - wi)

    def turned(value, power):
        power %= 16
        if power == 0:
            return value
        r, i = value
        cosine = float(np.cos(2 * np.pi * power / 16))
        sine = sign * float(np.sin(2 * np.pi * power / 16))
        if power == 4:
            return (-i, r) if sign > 0 else (i, -r)
        return (r * cosine - i * sine, r * sine + i * cosine)

    points = list(zip(real, imag))
    inner = [four(*(points[4 * j1 + j0] for j1 in range(4))) for j0 in range(4)]
    out = [None] * 16
    for b1 in range(4):
        column = [turned(inner[j0][b1], j0 * b1) for j0 in range(4)]
        for b0, value in enumerate(four(*column)):
            out[b1 + 4 * b0] = value
    return [v[0] for v in out], [v[1] for v in out]


def left_terms(value):
    high, low = split(value)
    return jnp.concatenate([high, low, high], axis=1)


def right_terms(value):
    high, low = split(value)
    return jnp.concatenate([high, high, low], axis=0)


def where_equal(left, right):
    return jnp.where(left == right, 1.0, 0.0).astype(jnp.bfloat16)


COPIES = 2


def spectral_kernel(extent, chunk, constants, rows_ref, near_ref, distant_ref, codes_ref, *refs):
    cube_ref, back_ref, turn_ref = refs[:3]
    sources = refs[3 : 3 + constants]
    kept_ref, sent_ref = refs[3 + constants : 5 + constants]
    refs = refs[5 + constants :]
    tables, refs = refs[:constants], refs[constants:]
    grids, refs = refs[: 2 * COPIES], refs[2 * COPIES :]
    grids = [grids[2 * i : 2 * i + 2] for i in range(COPIES)]
    rows, dense, sem = refs[:2], refs[2], refs[3]
    even_ref, odd_ref, uneven_ref, unodd_ref = tables[:4]
    line_ref, unline_ref, twist_ref, filter_ref = tables[4:8]
    plane_ref, unplane_ref, full_ref, unfull_ref, edge_ref = tables[8:]
    half_count = kept_ref.shape[0]
    blocks = half_count // near_ref.shape[0]
    slabs = extent // CUBE_COLS
    half = extent // 2
    moves = [
        pltpu.make_async_copy(source, table, sem.at[i])
        for i, (source, table) in enumerate(zip(sources, tables))
    ]
    for move in moves:
        move.start()

    def clear(i, _):
        place = pl.ds(pl.multiple_of(i * 64, 64), 64)
        for grid in grids:
            for ref in grid:
                ref[place, :] = jnp.zeros((64, LANES), jnp.float32)
        return 0

    lax.fori_loop(0, slabs * extent // 64, clear, 0)
    dense[...] = jnp.zeros(dense.shape, jnp.float32)

    def marks(start):
        codes = codes_ref[pl.ds(start, chunk), :]
        turn_count = extent // CUBE_ROWS
        wide = lax.broadcasted_iota(jnp.int32, (chunk, extent), 1)
        turn_lane = lax.broadcasted_iota(jnp.int32, (chunk, 2 * turn_count), 1) % turn_count
        turned = dot_in(where_equal(turn_lane, codes[:, 1:2]), turn_ref[...])
        return codes, wide, turned[:, :LANES], turned[:, LANES:]

    def spread(source_ref, offset, step, _):
        start = pl.multiple_of(offset + step * chunk, chunk)
        taken = source_ref[pl.ds(step * (chunk // blocks), chunk // blocks), :blocks, :]
        both = dot_in(left_terms(taken.reshape(chunk, LANES)), cube_ref[...])
        codes, wide, cosine, sine = marks(start)
        real, imag = both[:, :LANES], both[:, LANES : 2 * LANES]
        rows[0][...] = real * cosine + imag * sine
        rows[1][...] = imag * cosine - real * sine
        high, low = split(jnp.where(wide // CUBE_COLS == codes[:, 2:3], both[:, 2 * LANES :], 0.0))
        plane = where_equal(wide, codes[:, 0:1])
        contract = (((0,), (0,)), ((), ()))
        dense[...] += lax.dot_general(
            plane, high, contract, preferred_element_type=jnp.float32
        ) + lax.dot_general(plane, low, contract, preferred_element_type=jnp.float32)

        def add(i, _):
            for copy in range(COPIES):
                place = i + copy * (chunk // COPIES)
                row = rows_ref[start + place]
                for ref, source in zip(grids[copy], rows):
                    ref[pl.ds(row, 1), :] += source[pl.ds(place, 1), :]
            return 0

        lax.fori_loop(0, chunk // COPIES, add, 0, unroll=8)
        return 0

    for index, source_ref in enumerate((near_ref, distant_ref)):
        body = functools.partial(spread, source_ref, index * half_count)
        lax.fori_loop(0, half_count // chunk, body, 0)

    grid_real, grid_imag = grids[0]

    def across(sign):
        def body(i, _):
            start = pl.multiple_of(i * 8, 8)
            places = [pl.ds(start + slab * extent, 8) for slab in range(slabs)]
            values = []
            for part in range(2):
                values.append([grids[0][part][place, :] for place in places])
                if sign < 0:
                    for grid in grids[1:]:
                        values[part] = [v + grid[part][p, :] for v, p in zip(values[part], places)]
            values = butterfly16(*values, sign)
            for place, r, j in zip(places, *values):
                grid_real[place, :] = r
                grid_imag[place, :] = j
            return 0

        lax.fori_loop(0, extent // 8, body, 0)

    across(-1)
    for move in moves:
        move.wait()

    def middle(pair, _):
        starts = [pl.multiple_of((2 * pair + i) * extent, extent) for i in range(2)]

        def joined(offset):
            return jnp.concatenate(
                [
                    jnp.concatenate([ref[pl.ds(start + offset, half), :] for start in starts], axis=1)
                    for ref in grids[0]
                ],
                axis=0,
            )

        first, last = joined(0), joined(half)
        even = dot_in(even_ref[...], right_terms(first + last))
        odd = dot_in(odd_ref[...], right_terms(first - last))
        real = jnp.concatenate([even[:half], odd[:half]], axis=0)
        imag = jnp.concatenate([even[half:], odd[half:]], axis=0)
        cosine, sine = twist_ref[pair, 0:1, :], twist_ref[pair, 1:2, :]
        real, imag = real * cosine + imag * sine, imag * cosine - real * sine
        lines = jnp.concatenate(
            [
                jnp.concatenate([real[:, cut], imag[:, cut]], axis=1)
                for cut in (slice(0, LANES), slice(LANES, 2 * LANES))
            ],
            axis=0,
        )
        lines = dot_in(left_terms(lines), line_ref[...])
        scale = jnp.concatenate([filter_ref[2 * pair], filter_ref[2 * pair + 1]], axis=0)
        lines = lines * jnp.concatenate([scale, scale], axis=1)
        lines = dot_in(left_terms(lines), unline_ref[...])
        real = jnp.concatenate([lines[:extent, :LANES], lines[extent:, :LANES]], axis=1)
        imag = jnp.concatenate([lines[:extent, LANES:], lines[extent:, LANES:]], axis=1)
        real, imag = real * cosine - imag * sine, imag * cosine + real * sine
        even = jnp.concatenate([real[:half], imag[:half]], axis=0)
        odd = jnp.concatenate([real[half:], imag[half:]], axis=0)
        even = dot_in(uneven_ref[...], right_terms(even))
        odd = dot_in(unodd_ref[...], right_terms(odd))
        for offset, planes in ((0, even + odd), (half, even - odd)):
            for part, ref in enumerate(grids[0]):
                for i, start in enumerate(starts):
                    ref[pl.ds(start + offset, half), :] = planes[
                        part * half : (part + 1) * half, i * LANES : (i + 1) * LANES
                    ]
        return 0

    lax.fori_loop(0, slabs // 2, middle, 0, unroll=2)
    planes = dot_in(plane_ref[...], right_terms(dense[...]))
    some = planes.shape[0] // 2
    planes = jnp.concatenate([planes[:some], planes[some:]], axis=1)
    planes = dot_in(left_terms(planes), full_ref[...])
    planes = planes * jnp.concatenate([edge_ref[...], edge_ref[...]], axis=1)
    planes = dot_in(left_terms(planes), unfull_ref[...])
    planes = jnp.concatenate([planes[:, :extent], planes[:, extent:]], axis=0)
    dense[...] = dot_in(unplane_ref[...], right_terms(planes))
    across(1)

    def collect(out_ref, offset, step, _):
        start = pl.multiple_of(offset + step * chunk, chunk)

        def take(i, _):
            row = rows_ref[start + i]
            for ref, source in zip(rows, grids[0]):
                ref[pl.ds(i, 1), :] = source[pl.ds(row, 1), :]
            return 0

        lax.fori_loop(0, chunk, take, 0, unroll=16)
        codes, wide, cosine, sine = marks(start)
        plane = where_equal(wide, codes[:, 0:1])
        high, low = split(dense[...])
        edge = dot_in(plane, high) + dot_in(plane, low)
        edge = jnp.where(wide // CUBE_COLS == codes[:, 2:3], edge, 0.0)
        real, imag = rows[0][...], rows[1][...]
        both = jnp.concatenate(
            [real * cosine - imag * sine, imag * cosine + real * sine, edge], axis=1
        )
        out_ref[pl.ds(pl.multiple_of(step * chunk, chunk), chunk), :] = dot_in(
            left_terms(both), back_ref[...]
        )
        return 0

    for index, out_ref in enumerate((kept_ref, sent_ref)):
        body = functools.partial(collect, out_ref, index * half_count)
        lax.fori_loop(0, half_count // chunk, body, 0)


def stacked_table(table, axis):
    table = np.asarray(table, np.float32)
    high = table.astype(jnp.bfloat16)
    low = (table - high.astype(np.float32)).astype(jnp.bfloat16)
    order = [high, high, low] if axis == 0 else [high, low, high]
    return jnp.asarray(np.concatenate(order, axis=axis))


def constant_tables(extent):
    half = extent // 2
    n0 = np.arange(half)
    planes = []
    for k0 in (np.arange(0, extent, 2), np.arange(1, extent, 2)):
        angle = 2.0 * np.pi / extent * (k0[:, None] * n0[None, :] % extent)
        cosine, sine = np.cos(angle), np.sin(angle)
        planes.append(np.block([[cosine, sine], [-sine, cosine]]))
    small = np.arange(CUBE_COLS)
    angle = 2.0 * np.pi / CUBE_COLS * (small[:, None] * small[None, :] % CUBE_COLS)
    cosine = np.kron(np.eye(LANES // CUBE_COLS), np.cos(angle))
    sine = np.kron(np.eye(LANES // CUBE_COLS), np.sin(angle))
    line = np.block([[cosine, -sine], [sine, cosine]])
    angle = 2.0 * np.pi / extent * (small[:, None] * (np.arange(LANES) % CUBE_COLS)[None, :])
    twist = np.stack([np.cos(angle), np.sin(angle)], axis=1)
    twist = np.concatenate([twist[0::2], twist[1::2]], axis=2)
    some = np.arange(-(-(half + 1) // 8) * 8)
    whole = np.arange(extent)
    angle = 2.0 * np.pi / extent * (some[:, None] * whole[None, :] % extent)
    plane = np.concatenate([np.cos(angle), -np.sin(angle)], axis=0)
    angle = 2.0 * np.pi / extent * (whole[:, None] * whole[None, :] % extent)
    cosine, sine = np.cos(angle), np.sin(angle)
    full = np.block([[cosine, -sine], [sine, cosine]])
    first = [stacked_table(table, 1) for table in (*planes, planes[0].T, planes[1].T)]
    first += [stacked_table(line, 0), stacked_table(line.T, 0), jnp.asarray(twist, jnp.float32)]
    last = [stacked_table(plane, 1), stacked_table(plane.T, 1)]
    last += [stacked_table(full, 0), stacked_table(full.T, 0)]
    return first, last


def tables_kernel(
    extent, slab, place_ref, kernel_ref, sort_ref, cube_ref, back_ref, turn_ref, filter_ref, *lines
):
    first, shift = place_ref[0], place_ref[1]
    held = slab // 2
    points = CUBE_ROWS * CUBE_COLS

    def angles(numerator):
        angle = (2.0 * np.pi / extent) * (numerator % extent).astype(jnp.float32)
        return jnp.cos(angle), jnp.sin(angle)

    for shape, axis in (((points, LANES), 0), ((LANES, points), 1)):
        point = lax.broadcasted_iota(jnp.int32, shape, axis)
        column = lax.broadcasted_iota(jnp.int32, shape, 1 - axis)
        k1 = first + column // CUBE_COLS
        cosine, sine = angles((point // CUBE_COLS) * k1)
        same = (point % CUBE_COLS == column % CUBE_COLS) & (column // CUBE_COLS < held)
        shape = (points, extent) if axis == 0 else (extent, points)
        point = lax.broadcasted_iota(jnp.int32, shape, axis)
        column = lax.broadcasted_iota(jnp.int32, shape, 1 - axis)
        flip = 1.0 - 2.0 * ((point // CUBE_COLS) % 2).astype(jnp.float32)
        edge = jnp.where(point % CUBE_COLS == column % CUBE_COLS, flip, 0.0)
        table = jnp.concatenate(
            [jnp.where(same, cosine, 0.0), jnp.where(same, -sine, 0.0), edge], axis=1 - axis
        )
        (cube_ref if axis == 0 else back_ref)[...] = right_terms(table)
    shape = (extent // CUBE_ROWS, LANES)
    column = lax.broadcasted_iota(jnp.int32, shape, 1)
    turn = lax.broadcasted_iota(jnp.int32, shape, 0) * CUBE_ROWS
    high, low = split(jnp.concatenate(angles(turn * (first + column // CUBE_COLS)), axis=1))
    turn_ref[...] = jnp.concatenate([high, low], axis=0)

    batch = 512

    def sort(i, _):
        place = pl.ds(pl.multiple_of(i * batch, batch), batch)
        values = kernel_ref[place, :]
        high = values.astype(jnp.bfloat16)
        rest = values - high.astype(jnp.float32)
        middle, low = split(rest)
        terms = jnp.concatenate([high, middle, low], axis=1)
        values = dot_in(terms, sort_ref[...])
        for side, ref in enumerate(lines):
            ref[place, :] = values[:, side * LANES : (side + 1) * LANES]
        return 0

    lax.fori_loop(0, extent * slab // batch, sort, 0)
    groups = LANES // CUBE_COLS
    lane = lax.broadcasted_iota(jnp.int32, (1, LANES), 1)
    k1 = first + lane // CUBE_COLS
    weight = jnp.where(k1 == 0, 1.0, 2.0) / float(extent) ** 3
    weight = jnp.where(lane // CUBE_COLS < held, weight, 0.0)
    count = 32
    for odd in range(2):

        def turn_over(i, _):
            for side, ref in enumerate(lines):
                values = [
                    ref[
                        pl.ds(shift + k + (2 * i * count + odd) * slab, count, stride=2 * slab), :
                    ]
                    if k < held
                    else jnp.zeros((count, LANES), jnp.float32)
                    for k in range(groups)
                ]
                group = lax.broadcasted_iota(jnp.int32, (count, LANES), 1) // CUBE_COLS
                step = 1
                while step < groups:
                    upper = group // step % 2 == 1
                    turned = list(values)
                    for k in range(groups):
                        if k // step % 2 == 0:
                            one, two = values[k], values[k + step]
                            turned[k] = jnp.where(upper, pltpu.roll(two, step * CUBE_COLS, 1), one)
                            turned[k + step] = jnp.where(
                                upper, two, pltpu.roll(one, LANES - step * CUBE_COLS, 1)
                            )
                    values = turned
                    step *= 2
                row = pl.multiple_of(odd * (extent // 2) + i * count, count)
                for k in range(groups):
                    filter_ref[side * groups + k, pl.ds(row, count), :] = values[k] * weight
            return 0

        lax.fori_loop(0, extent // 2 // count, turn_over, 0)


def spectral_tables(kernel_local):
    members = lax.axis_size("px")
    me = lax.axis_index("px")
    extent, slab = kernel_local.shape[:2]
    shift = (me >= members // 2).astype(jnp.int32)
    k2 = np.arange(extent)
    sort = np.zeros((extent, extent), np.float32)
    sort[k2, k2 % CUBE_COLS * CUBE_COLS + k2 // CUBE_COLS] = 1.0
    whole = pl.BlockSpec(memory_space=pltpu.VMEM)
    points = CUBE_ROWS * CUBE_COLS
    size = 2 * LANES + extent
    cube, back, turn, filters = pl.pallas_call(
        functools.partial(tables_kernel, extent, slab),
        out_shape=(
            jax.ShapeDtypeStruct((3 * points, size), jnp.bfloat16),
            jax.ShapeDtypeStruct((3 * size, points), jnp.bfloat16),
            jax.ShapeDtypeStruct((2 * extent // CUBE_ROWS, 2 * LANES), jnp.bfloat16),
            jax.ShapeDtypeStruct((CUBE_COLS, extent, LANES), jnp.float32),
        ),
        in_specs=[pl.BlockSpec(memory_space=pltpu.SMEM), whole, whole],
        out_specs=(whole,) * 4,
        scratch_shapes=[pltpu.VMEM((extent * slab, LANES), jnp.float32)] * 2,
        cost_estimate=pl.CostEstimate(
            flops=2 * extent * slab * 3 * extent * extent,
            bytes_accessed=8 * extent * slab * extent,
            transcendentals=0,
        ),
        compiler_params=pltpu.CompilerParams(vmem_limit_bytes=32 * 1024 * 1024),
        name="tables",
    )(
        jnp.stack([me * slab + shift, shift]),
        kernel_local.reshape(extent * slab, extent),
        jnp.asarray(np.concatenate([sort] * 3, axis=0), jnp.bfloat16),
    )
    first, last = constant_tables(extent)
    some = last[0].shape[0] // 2
    k0 = np.arange(some)
    weight = np.where((k0 == 0) | (k0 == extent // 2), 1.0, 2.0) * (k0 <= extent // 2)
    weight = jnp.asarray(weight / float(extent) ** 3, jnp.float32)[:, None]
    edge = jnp.where(me == members // 2, kernel_local[:some, 0, :] * weight, 0.0)
    return cube, back, turn, (*first, filters, *last, edge)


def cube_places(cubes, extent):
    slabs = extent // CUBE_COLS
    turns = extent // CUBE_ROWS
    plane, turn, slab = cubes // (turns * slabs), cubes // slabs % turns, cubes % slabs
    codes = jnp.stack([plane, turn, slab] + [jnp.zeros_like(slab)] * 5, axis=1)
    return slab * extent + plane, codes


def spectral(places, extent, blocks, gathered, tables):
    cube, back, turn, constants = tables
    half_count = gathered[0].shape[0] * blocks
    slabs = extent // CUBE_COLS
    chunk = min(512, half_count)
    whole = pl.BlockSpec(memory_space=pltpu.VMEM)
    out = jax.ShapeDtypeStruct((half_count, LANES), jnp.float32)
    return pl.pallas_call(
        functools.partial(spectral_kernel, extent, chunk, len(constants)),
        out_shape=(out, out),
        in_specs=[pl.BlockSpec(memory_space=pltpu.SMEM)]
        + [whole] * 6
        + [pl.BlockSpec(memory_space=pl.ANY)] * len(constants),
        out_specs=(whole, whole),
        scratch_shapes=[pltpu.VMEM(table.shape, table.dtype) for table in constants]
        + [pltpu.VMEM((slabs * extent, LANES), jnp.float32)] * (2 * COPIES)
        + [pltpu.VMEM((chunk, LANES), jnp.float32)] * 2
        + [pltpu.VMEM((extent, extent), jnp.float32)]
        + [pltpu.SemaphoreType.DMA((len(constants),))],
        compiler_params=pltpu.CompilerParams(vmem_limit_bytes=60 * 1024 * 1024),
        name="spectral",
    )(places[0], *gathered, places[1], cube, back, turn, *constants)


NOTE_ROWS = 8
STEP_BLOCKS = 16
RIM_PART = 4


def sum_row(*values):
    lane = lax.broadcasted_iota(jnp.int32, (1, LANES), 1)
    row = jnp.zeros((1, LANES), jnp.float32)
    for index, value in enumerate(values):
        row = jnp.where(lane == index, value, row)
    return row


def put_edges(out_ref, values):
    step, steps = pl.program_id(0), pl.num_programs(0)
    panels = values.shape[1]
    below = out_ref.shape[0] - steps * STEP_BLOCKS // RIM_PART

    for first, lanes in ((0, slice(0, panels)), (steps - steps // RIM_PART, slice(panels, 2 * panels))):

        @pl.when((step >= first) & (step < first + steps // RIM_PART))
        def _():
            row = pl.multiple_of(below + (step - first) * STEP_BLOCKS, 8)
            out_ref[pl.ds(row, STEP_BLOCKS), lanes] = values


def project_kernel(proj_ref, values_ref, note_ref, out_ref):
    step = pl.program_id(0)
    charges = jnp.sum(proj_ref[...] * values_ref[...][:, :, None], axis=1)
    out_ref[pl.ds(pl.multiple_of(step * STEP_BLOCKS, STEP_BLOCKS), STEP_BLOCKS), :] = charges

    put_edges(out_ref, values_ref[...])

    @pl.when(step == pl.num_programs(0) - 1)
    def _():
        blocks = pl.num_programs(0) * STEP_BLOCKS
        out_ref[blocks : blocks + NOTE_ROWS, :] = jnp.broadcast_to(
            note_ref[...], (NOTE_ROWS, LANES)
        )


def complete_kernel(proj_ref, picked_ref, base_ref, rhs_ref, image_ref, out_ref):
    step = pl.program_id(0)
    tiles = proj_ref[...]
    image = base_ref[...] + jnp.sum(tiles * picked_ref[...][:, None, :], axis=2)
    image_ref[...] = image
    charges = jnp.sum(tiles * image[:, :, None], axis=1)
    out_ref[pl.ds(pl.multiple_of(step * STEP_BLOCKS, STEP_BLOCKS), STEP_BLOCKS), :] = charges
    put_edges(out_ref, image)
    blocks = pl.num_programs(0) * STEP_BLOCKS
    rhs = rhs_ref[...]
    row = sum_row(jnp.sum(rhs * rhs), jnp.sum(rhs * image), jnp.sum(image * image))

    @pl.when(step == 0)
    def _():
        out_ref[blocks : blocks + NOTE_ROWS, :] = jnp.zeros((NOTE_ROWS, LANES), jnp.float32)

    out_ref[blocks : blocks + 1, :] += row


def vector_scalars(sums):
    norm_sq, mixed, image_sq = sums[0:1, 0:1], sums[0:1, 1:2], sums[0:1, 2:3]
    gram_one = image_sq / norm_sq
    return jnp.sqrt(norm_sq), mixed / norm_sq, gram_one, jnp.sqrt(gram_one)


def close_kernel(proj_ref, picked_ref, base_ref, rhs_ref, first_ref, sums_ref, image_ref, out_ref):
    step = pl.program_id(0)
    second = base_ref[...] + jnp.sum(proj_ref[...] * picked_ref[...][:, None, :], axis=2)
    initial_norm, diag_one, _, scale = vector_scalars(sums_ref[...])
    basis_one = rhs_ref[...] / initial_norm
    image_one = first_ref[...] / initial_norm
    image_two = (second / initial_norm - diag_one * image_one) / scale
    image_ref[...] = image_two
    row = sum_row(
        jnp.sum(basis_one * image_two),
        jnp.sum(image_one * image_two),
        jnp.sum(image_two * image_two),
    )

    @pl.when(step == 0)
    def _():
        out_ref[...] = jnp.zeros((NOTE_ROWS, LANES), jnp.float32)

    out_ref[0:1, :] += row


def finish_kernel(rhs_ref, first_ref, image_ref, sums_ref, last_ref, answer_ref, residual_ref, rows_ref):
    initial_norm, diag_one, gram_one, scale = vector_scalars(sums_ref[...])
    last = last_ref[...]
    upper_two, gram_cross, gram_two = last[0:1, 0:1], last[0:1, 1:2], last[0:1, 2:3]
    rhs = rhs_ref[...]
    basis_one = rhs / initial_norm
    image_one = first_ref[...] / initial_norm
    basis_two = (image_one - diag_one * basis_one) / scale
    determinant = gram_one * gram_two - gram_cross * gram_cross
    weight_one = initial_norm * (diag_one * gram_two - upper_two * gram_cross) / determinant
    weight_two = initial_norm * (upper_two * gram_one - diag_one * gram_cross) / determinant
    half = rhs.shape[0] // 2
    for out_ref, value in (
        (answer_ref, weight_one * basis_one + weight_two * basis_two),
        (residual_ref, rhs - weight_one * image_one - weight_two * image_ref[...]),
    ):
        rows_ref[...] = value
        out_ref[...] = jnp.concatenate(
            [rows_ref[pl.ds(side, half, stride=2), :] for side in range(2)], axis=1
        )


def local_call(kernel, name, proj_tiles, rows, whole, outs):
    blocks, panels, points = proj_tiles.shape

    def cut(width):
        return pl.BlockSpec((STEP_BLOCKS, width), lambda i: (i, 0))

    def uncut(shape):
        return pl.BlockSpec(shape, lambda i: (0, 0))

    out_specs = [cut(out[1]) if out[0] == blocks else uncut(out) for out in outs]
    return pl.pallas_call(
        kernel,
        grid=(blocks // STEP_BLOCKS,),
        out_shape=[jax.ShapeDtypeStruct(out, jnp.float32) for out in outs],
        in_specs=[pl.BlockSpec((STEP_BLOCKS, panels, points), lambda i: (i, 0, 0))]
        + [cut(row.shape[1]) for row in rows]
        + [uncut(value.shape) for value in whole],
        out_specs=out_specs,
        cost_estimate=pl.CostEstimate(
            flops=4 * proj_tiles.size, bytes_accessed=4 * proj_tiles.size, transcendentals=0
        ),
        compiler_params=pltpu.CompilerParams(vmem_limit_bytes=16 * 1024 * 1024),
        name=name,
    )(proj_tiles, *rows, *whole)


def piece_place(device):
    steps = partner_steps(lax.axis_size("px"))[:-1]
    away = lax.axis_index("px") ^ device
    return sum((away // step % 2) << place for place, step in enumerate(steps))


def halo(cells, distant):
    me, members = lax.axis_index("px"), lax.axis_size("px")
    width = cells.shape[0] // RIM_PART
    panels = cells.shape[1]
    sides = []
    for device, lane, present in ((me - 1, panels, me > 0), (me + 1, 0, me < members - 1)):
        place = jnp.where(present, piece_place(device), 0)
        start = (place, distant.shape[1] - width, lane)
        edge = lax.dynamic_slice(distant, start, (1, width, panels))[0]
        sides.append(jnp.where(present, edge, 0.0))
    return jnp.concatenate([sides[0], cells, sides[1]], axis=0)


def on_device(
    right_side, self_term, proj_tiles, owner_dev, cube_slot, near_src, near_tiles, kernel_hat
):
    members = lax.axis_size("px")
    blocks = proj_tiles.shape[0]
    extent = kernel_hat.shape[0]
    cubes_dev = extent // members * (extent // CUBE_ROWS) * (extent // CUBE_COLS)
    self_local = self_term.reshape(blocks, 64)
    cubes = owner_dev[:, 0] * cubes_dev + cube_slot
    tables = spectral_tables(kernel_hat)

    rhs = right_side.reshape(blocks, 64)
    note_shape = (blocks + NOTE_ROWS + blocks // RIM_PART, LANES)

    def base_of(values, gathered):
        sources = halo(values, gathered[1])[near_src].reshape(blocks, near_tiles.shape[2])
        return self_local * values + jnp.sum(near_tiles * sources[:, None, :], axis=2)

    def far(places, gathered):
        return scatter_pieces(*spectral(places, extent, blocks, gathered, tables))

    note = jnp.pad(cubes.astype(jnp.float32)[None, :], ((0, 0), (0, LANES - blocks)))
    (payload,) = local_call(project_kernel, "project", proj_tiles, [rhs], [note], [note_shape])
    gathered, tables = gather_pieces(payload, tables)
    base = base_of(rhs, gathered)
    all_cubes = jnp.concatenate([half[:, blocks, :blocks] for half in gathered], axis=0)
    places = cube_places(all_cubes.astype(jnp.int32).reshape(members * blocks), extent)
    first, payload = local_call(
        complete_kernel,
        "complete",
        proj_tiles,
        [far(places, gathered), base, rhs],
        [],
        [(blocks, 64), note_shape],
    )
    gathered, _ = gather_pieces(payload, ())
    base = base_of(first, gathered)
    sums = sum(jnp.sum(half[:, blocks, :], axis=0, keepdims=True) for half in gathered)
    image, last = local_call(
        close_kernel,
        "close",
        proj_tiles,
        [far(places, gathered), base, rhs, first],
        [sums],
        [(blocks, 64), (NOTE_ROWS, LANES)],
    )
    last = total(last)
    out = jax.ShapeDtypeStruct((blocks // 2, 128), jnp.float32)
    answer, residual = pl.pallas_call(
        finish_kernel,
        out_shape=(out, out),
        scratch_shapes=[pltpu.VMEM((blocks, 64), jnp.float32)],
        name="finish",
    )(rhs, first, image, sums, last)
    return (answer.reshape(blocks * 64), residual.reshape(blocks * 64))


def solution(mesh):
    return jax.shard_map(
        on_device,
        mesh=mesh,
        in_specs=(
            P(("groups", "px")),
            P(("groups", "px")),
            P(("groups", "px"), None, None),
            P(("groups", "px"), None),
            P(("groups", "px")),
            P(("groups", "px"), None),
            P(("groups", "px"), None, None),
            P(None, "px", None),
        ),
        out_specs=(P(("groups", "px")), P(("groups", "px"))),
        check_vma=False,
    )
```

```python
import functools
import jax
import jax.numpy as jnp
import numpy as np
from jax import lax
from jax.experimental import pallas as pl
from jax.experimental.pallas import tpu as pltpu
from jax.sharding import PartitionSpec as P

LANES = 128
CUBE_ROWS = 8
CUBE_COLS = 16
VMEM_BYTES = 60 * 1024 * 1024
SPECTRAL_BYTES = 60 * 1024 * 1024


def split(value):
    high = value.astype(jnp.bfloat16)
    low = (value - high.astype(jnp.float32)).astype(jnp.bfloat16)
    return high, low


def dot_in(left, right):
    return jnp.dot(left, right, preferred_element_type=jnp.float32)


def partner_steps(members):
    return [1 << i for i in reversed(range(members.bit_length() - 1))]


def exchange(value, step):
    members = lax.axis_size("px")
    return lax.ppermute(value, "px", [(i, i ^ step) for i in range(members)])


def gather_pieces(piece, beside):
    steps = partner_steps(lax.axis_size("px"))
    pieces = piece[None]
    done = []
    for index, step in enumerate(steps[:-1]):
        pieces = jnp.concatenate([pieces, exchange(pieces, step)], axis=0)
        if index < len(beside):
            pieces, value = lax.optimization_barrier((pieces, beside[index]))
            done.append(value)
    return (pieces, exchange(pieces, steps[-1])), done


def scatter_pieces(kept, sent):
    steps = list(reversed(partner_steps(lax.axis_size("px"))))
    pieces = kept + exchange(sent, steps[0])
    for step in steps[1:]:
        half = pieces.shape[0] // 2
        pieces = pieces[:half] + exchange(pieces[half:], step)
    return pieces


def total(value):
    members = lax.axis_size("px")
    copies = jnp.broadcast_to(value[None], (members, *value.shape))
    return jnp.sum(lax.all_to_all(copies, "px", 0, 0), axis=0)


def butterfly16(real, imag, sign):
    def four(a, b, c, d):
        (ar, ai), (br, bi), (cr, ci), (dr, di) = a, b, c, d
        sr, si, tr, ti = ar + cr, ai + ci, ar - cr, ai - ci
        ur, ui, vr, vi = br + dr, bi + di, br - dr, bi - di
        wr, wi = (-vi, vr) if sign > 0 else (vi, -vr)
        return (sr + ur, si + ui), (tr + wr, ti + wi), (sr - ur, si - ui), (tr - wr, ti - wi)

    def turned(value, power):
        power %= 16
        if power == 0:
            return value
        r, i = value
        cosine = float(np.cos(2 * np.pi * power / 16))
        sine = sign * float(np.sin(2 * np.pi * power / 16))
        if power == 4:
            return (-i, r) if sign > 0 else (i, -r)
        return (r * cosine - i * sine, r * sine + i * cosine)

    points = list(zip(real, imag))
    inner = [four(*(points[4 * j1 + j0] for j1 in range(4))) for j0 in range(4)]
    out = [None] * 16
    for b1 in range(4):
        column = [turned(inner[j0][b1], j0 * b1) for j0 in range(4)]
        for b0, value in enumerate(four(*column)):
            out[b1 + 4 * b0] = value
    return [v[0] for v in out], [v[1] for v in out]


def left_terms(value):
    high, low = split(value)
    return jnp.concatenate([high, low, high], axis=1)


def right_terms(value):
    high, low = split(value)
    return jnp.concatenate([high, high, low], axis=0)


def where_equal(left, right):
    return jnp.where(left == right, 1.0, 0.0).astype(jnp.bfloat16)


COPIES = 4
GROUP = 8


def spectral_kernel(extent, chunk, operands, rows_ref, codes_ref, *refs):
    sources, (kept_out, sent_out), refs = refs[:operands], refs[operands : operands + 2], refs[operands + 2 :]
    tables, (kept_ref, sent_ref), refs = refs[:operands], refs[operands : operands + 2], refs[operands + 2 :]
    grids, refs = refs[: 2 * COPIES], refs[2 * COPIES :]
    grids = [grids[2 * i : 2 * i + 2] for i in range(COPIES)]
    rows, dense, sem, out_sem = refs[:2], refs[2], refs[3], refs[4]
    near_ref, cube_ref, turn_ref, distant_ref, back_ref = tables[:5]
    even_ref, odd_ref, uneven_ref, unodd_ref = tables[5:9]
    line_ref, unline_ref, twist_ref, filter_ref = tables[9:13]
    plane_ref, unplane_ref, full_ref, unfull_ref, edge_ref = tables[13:]
    half_count = kept_ref.shape[0]
    blocks = half_count // near_ref.shape[0]
    slabs = extent // CUBE_COLS
    half = extent // 2
    moves = [
        pltpu.make_async_copy(source, table, sem.at[i])
        for i, (source, table) in enumerate(zip(sources, tables))
    ]
    for move in moves[:3]:
        move.start()

    def clear(i, _):
        place = pl.ds(pl.multiple_of(i * 64, 64), 64)
        for grid in grids:
            for ref in grid:
                ref[place, :] = jnp.zeros((64, LANES), jnp.float32)
        return 0

    lax.fori_loop(0, slabs * extent // 64, clear, 0)
    dense[...] = jnp.zeros(dense.shape, jnp.float32)

    def marks(start):
        codes = jnp.transpose(codes_ref[:, pl.ds(start, chunk)])
        turn_count = extent // CUBE_ROWS
        wide = lax.broadcasted_iota(jnp.int32, (chunk, extent), 1)
        turn_lane = lax.broadcasted_iota(jnp.int32, (chunk, 2 * turn_count), 1) % turn_count
        turned = dot_in(where_equal(turn_lane, codes[:, 1:2]), turn_ref[...])
        return codes, wide, turned[:, :LANES], turned[:, LANES:]

    def spread(source_ref, offset, step, _):
        start = pl.multiple_of(offset + step * chunk, chunk)
        taken = source_ref[pl.ds(step * (chunk // blocks), chunk // blocks), :blocks, :]
        both = dot_in(left_terms(taken.reshape(chunk, LANES)), cube_ref[...])
        codes, wide, cosine, sine = marks(start)
        real, imag = both[:, :LANES], both[:, LANES : 2 * LANES]
        rows[0][...] = real * cosine + imag * sine
        rows[1][...] = imag * cosine - real * sine
        high, low = split(jnp.where(wide // CUBE_COLS == codes[:, 2:3], both[:, 2 * LANES :], 0.0))
        plane = where_equal(wide, codes[:, 0:1])
        contract = (((0,), (0,)), ((), ()))
        dense[...] += lax.dot_general(
            plane, high, contract, preferred_element_type=jnp.float32
        ) + lax.dot_general(plane, low, contract, preferred_element_type=jnp.float32)

        def add(i, _):
            for copy in range(COPIES):
                place = i + copy * (chunk // COPIES)
                row = rows_ref[start + place]
                for ref, source in zip(grids[copy], rows):
                    ref[pl.ds(row, 1), :] += source[pl.ds(place, 1), :]
            return 0

        lax.fori_loop(0, chunk // COPIES, add, 0, unroll=8)
        return 0

    for move in moves[:3]:
        move.wait()
    for move in moves[3:]:
        move.start()
    for index, source_ref in enumerate((near_ref, distant_ref)):
        if index:
            moves[3].wait()
        body = functools.partial(spread, source_ref, index * half_count)
        lax.fori_loop(0, half_count // chunk, body, 0)

    grid_real, grid_imag = grids[0]

    def across(sign):
        def body(i, _):
            start = pl.multiple_of(i * 8, 8)
            places = [pl.ds(start + slab * extent, 8) for slab in range(slabs)]
            values = []
            for part in range(2):
                values.append([grids[0][part][place, :] for place in places])
                if sign < 0:
                    for grid in grids[1:]:
                        values[part] = [v + grid[part][p, :] for v, p in zip(values[part], places)]
            values = butterfly16(*values, sign)
            for place, r, j in zip(places, *values):
                grid_real[place, :] = r
                grid_imag[place, :] = j
            return 0

        lax.fori_loop(0, extent // 8, body, 0)

    across(-1)
    for move in moves[4:]:
        move.wait()

    def middle(group, _):
        starts = [pl.multiple_of((GROUP * group + i) * extent, extent) for i in range(GROUP)]
        cuts = [slice(i * LANES, (i + 1) * LANES) for i in range(GROUP)]

        def joined(offset):
            return jnp.concatenate(
                [
                    jnp.concatenate([ref[pl.ds(start + offset, half), :] for start in starts], axis=1)
                    for ref in grids[0]
                ],
                axis=0,
            )

        first, last = joined(0), joined(half)
        even = dot_in(even_ref[...], right_terms(first + last))
        odd = dot_in(odd_ref[...], right_terms(first - last))
        real = jnp.concatenate([even[:half], odd[:half]], axis=0)
        imag = jnp.concatenate([even[half:], odd[half:]], axis=0)
        cosine, sine = twist_ref[group, 0:1, :], twist_ref[group, 1:2, :]
        real, imag = real * cosine + imag * sine, imag * cosine - real * sine
        lines = jnp.concatenate(
            [
                jnp.concatenate([real[:, cut], imag[:, cut]], axis=1)
                for cut in cuts
            ],
            axis=0,
        )
        lines = dot_in(left_terms(lines), line_ref[...])
        scale = jnp.concatenate([filter_ref[GROUP * group + i] for i in range(GROUP)], axis=0)
        lines = lines * jnp.concatenate([scale, scale], axis=1)
        lines = dot_in(left_terms(lines), unline_ref[...])
        lines = [lines[i * extent : (i + 1) * extent] for i in range(GROUP)]
        real = jnp.concatenate([line[:, :LANES] for line in lines], axis=1)
        imag = jnp.concatenate([line[:, LANES:] for line in lines], axis=1)
        real, imag = real * cosine - imag * sine, imag * cosine + real * sine
        even = jnp.concatenate([real[:half], imag[:half]], axis=0)
        odd = jnp.concatenate([real[half:], imag[half:]], axis=0)
        even = dot_in(uneven_ref[...], right_terms(even))
        odd = dot_in(unodd_ref[...], right_terms(odd))
        for offset, planes in ((0, even + odd), (half, even - odd)):
            for part, ref in enumerate(grids[0]):
                for i, start in enumerate(starts):
                    ref[pl.ds(start + offset, half), :] = planes[
                        part * half : (part + 1) * half, i * LANES : (i + 1) * LANES
                    ]
        return 0

    lax.fori_loop(0, slabs // GROUP, middle, 0, unroll=1)
    planes = dot_in(plane_ref[...], right_terms(dense[...]))
    some = planes.shape[0] // 2
    planes = jnp.concatenate([planes[:some], planes[some:]], axis=1)
    planes = dot_in(left_terms(planes), full_ref[...])
    planes = planes * jnp.concatenate([edge_ref[...], edge_ref[...]], axis=1)
    planes = dot_in(left_terms(planes), unfull_ref[...])
    planes = jnp.concatenate([planes[:, :extent], planes[:, extent:]], axis=0)
    dense[...] = dot_in(unplane_ref[...], right_terms(planes))
    across(1)

    def leave(index, step):
        place = pl.ds(pl.multiple_of(step * chunk, chunk), chunk)
        out_ref = (kept_ref, sent_ref)[index]
        return pltpu.make_async_copy(
            out_ref.at[place, :], (kept_out, sent_out)[index].at[place, :], out_sem.at[index, step]
        )

    def collect(index, step, _):
        out_ref = (kept_ref, sent_ref)[index]
        offset = index * half_count
        start = pl.multiple_of(offset + step * chunk, chunk)

        def take(i, _):
            row = rows_ref[start + i]
            for ref, source in zip(rows, grids[0]):
                ref[pl.ds(i, 1), :] = source[pl.ds(row, 1), :]
            return 0

        lax.fori_loop(0, chunk, take, 0, unroll=16)
        codes, wide, cosine, sine = marks(start)
        plane = where_equal(wide, codes[:, 0:1])
        high, low = split(dense[...])
        edge = dot_in(plane, high) + dot_in(plane, low)
        edge = jnp.where(wide // CUBE_COLS == codes[:, 2:3], edge, 0.0)
        real, imag = rows[0][...], rows[1][...]
        both = jnp.concatenate(
            [real * cosine - imag * sine, imag * cosine + real * sine, edge], axis=1
        )
        out_ref[pl.ds(pl.multiple_of(step * chunk, chunk), chunk), :] = dot_in(
            left_terms(both), back_ref[...]
        )
        leave(index, step).start()
        return 0

    for index in range(2):
        lax.fori_loop(0, half_count // chunk, functools.partial(collect, index), 0)

    def finish(step, _):
        for index in range(2):
            leave(index, step).wait()
        return 0

    lax.fori_loop(0, half_count // chunk, finish, 0)


def stacked_table(table, axis):
    table = np.asarray(table, np.float32)
    high = table.astype(jnp.bfloat16)
    low = (table - high.astype(np.float32)).astype(jnp.bfloat16)
    order = [high, high, low] if axis == 0 else [high, low, high]
    return jnp.asarray(np.concatenate(order, axis=axis))


def constant_tables(extent):
    half = extent // 2
    n0 = np.arange(half)
    planes = []
    for k0 in (np.arange(0, extent, 2), np.arange(1, extent, 2)):
        angle = 2.0 * np.pi / extent * (k0[:, None] * n0[None, :] % extent)
        cosine, sine = np.cos(angle), np.sin(angle)
        planes.append(np.block([[cosine, sine], [-sine, cosine]]))
    small = np.arange(CUBE_COLS)
    angle = 2.0 * np.pi / CUBE_COLS * (small[:, None] * small[None, :] % CUBE_COLS)
    cosine = np.kron(np.eye(LANES // CUBE_COLS), np.cos(angle))
    sine = np.kron(np.eye(LANES // CUBE_COLS), np.sin(angle))
    line = np.block([[cosine, -sine], [sine, cosine]])
    angle = 2.0 * np.pi / extent * (small[:, None] * (np.arange(LANES) % CUBE_COLS)[None, :])
    twist = np.stack([np.cos(angle), np.sin(angle)], axis=1)
    twist = np.concatenate([twist[i::GROUP] for i in range(GROUP)], axis=2)
    some = np.arange(-(-(half + 1) // 8) * 8)
    whole = np.arange(extent)
    angle = 2.0 * np.pi / extent * (some[:, None] * whole[None, :] % extent)
    plane = np.concatenate([np.cos(angle), -np.sin(angle)], axis=0)
    angle = 2.0 * np.pi / extent * (whole[:, None] * whole[None, :] % extent)
    cosine, sine = np.cos(angle), np.sin(angle)
    full = np.block([[cosine, -sine], [sine, cosine]])
    first = [stacked_table(table, 1) for table in (*planes, planes[0].T, planes[1].T)]
    first += [stacked_table(line, 0), stacked_table(line.T, 0), jnp.asarray(twist, jnp.float32)]
    last = [stacked_table(plane, 1), stacked_table(plane.T, 1)]
    last += [stacked_table(full, 0), stacked_table(full.T, 0)]
    return first, last


def tables_kernel(extent, held, place_ref, cube_ref, back_ref, turn_ref):
    first = place_ref[0]
    points = CUBE_ROWS * CUBE_COLS

    def angles(numerator):
        angle = (2.0 * np.pi / extent) * (numerator % extent).astype(jnp.float32)
        return jnp.cos(angle), jnp.sin(angle)

    for shape, axis in (((points, LANES), 0), ((LANES, points), 1)):
        point = lax.broadcasted_iota(jnp.int32, shape, axis)
        column = lax.broadcasted_iota(jnp.int32, shape, 1 - axis)
        k1 = first + column // CUBE_COLS
        cosine, sine = angles((point // CUBE_COLS) * k1)
        same = (point % CUBE_COLS == column % CUBE_COLS) & (column // CUBE_COLS < held)
        shape = (points, extent) if axis == 0 else (extent, points)
        point = lax.broadcasted_iota(jnp.int32, shape, axis)
        column = lax.broadcasted_iota(jnp.int32, shape, 1 - axis)
        flip = 1.0 - 2.0 * ((point // CUBE_COLS) % 2).astype(jnp.float32)
        edge = jnp.where(point % CUBE_COLS == column % CUBE_COLS, flip, 0.0)
        table = jnp.concatenate(
            [jnp.where(same, cosine, 0.0), jnp.where(same, -sine, 0.0), edge], axis=1 - axis
        )
        (cube_ref if axis == 0 else back_ref)[...] = right_terms(table)
    shape = (extent // CUBE_ROWS, LANES)
    column = lax.broadcasted_iota(jnp.int32, shape, 1)
    turn = lax.broadcasted_iota(jnp.int32, shape, 0) * CUBE_ROWS
    high, low = split(jnp.concatenate(angles(turn * (first + column // CUBE_COLS)), axis=1))
    turn_ref[...] = jnp.concatenate([high, low], axis=0)


def filter_kernel(extent, slab, place_ref, kernel_ref, sort_ref, filter_ref, *lines):
    first, shift = place_ref[0], place_ref[1]
    held = slab // 2
    batch = kernel_ref.shape[0]
    count = batch // slab // 2
    step = pl.program_id(0)
    values = kernel_ref[...]
    high = values.astype(jnp.bfloat16)
    rest = values - high.astype(jnp.float32)
    values = dot_in(jnp.concatenate([high, *split(rest)], axis=1), sort_ref[...])
    for side, ref in enumerate(lines):
        ref[...] = values[:, side * LANES : (side + 1) * LANES]
    groups = LANES // CUBE_COLS
    lane = lax.broadcasted_iota(jnp.int32, (1, LANES), 1)
    weight = jnp.where(first + lane // CUBE_COLS == 0, 1.0, 2.0) / float(extent) ** 3
    weight = jnp.where(lane // CUBE_COLS < held, weight, 0.0)
    group = lax.broadcasted_iota(jnp.int32, (count, LANES), 1) // CUBE_COLS
    for odd in range(2):
        row = pl.multiple_of(odd * (extent // 2) + step * count, count)
        for side, ref in enumerate(lines):
            values = [
                ref[pl.ds(shift + k + odd * slab, count, stride=2 * slab), :]
                if k < held
                else jnp.zeros((count, LANES), jnp.float32)
                for k in range(groups)
            ]
            apart = 1
            while apart < groups:
                upper = group // apart % 2 == 1
                turned = list(values)
                for k in range(groups):
                    if k // apart % 2 == 0:
                        one, two = values[k], values[k + apart]
                        turned[k] = jnp.where(upper, pltpu.roll(two, apart * CUBE_COLS, 1), one)
                        turned[k + apart] = jnp.where(
                            upper, two, pltpu.roll(one, LANES - apart * CUBE_COLS, 1)
                        )
                values = turned
                apart *= 2
            for k in range(groups):
                filter_ref[side * groups + k, pl.ds(row, count), :] = values[k] * weight


def spectral_tables(kernel_local):
    members = lax.axis_size("px")
    me = lax.axis_index("px")
    extent, slab = kernel_local.shape[:2]
    shift = (me >= members // 2).astype(jnp.int32)
    k2 = np.arange(extent)
    sort = np.zeros((extent, extent), np.float32)
    sort[k2, k2 % CUBE_COLS * CUBE_COLS + k2 // CUBE_COLS] = 1.0
    whole = pl.BlockSpec(memory_space=pltpu.VMEM)
    points = CUBE_ROWS * CUBE_COLS
    size = 2 * LANES + extent
    place = jnp.stack([me * slab + shift, shift])
    scalars = pl.BlockSpec(memory_space=pltpu.SMEM)
    cube_tables = pl.pallas_call(
        functools.partial(tables_kernel, extent, slab // 2),
        out_shape=(
            jax.ShapeDtypeStruct((3 * points, size), jnp.bfloat16),
            jax.ShapeDtypeStruct((3 * size, points), jnp.bfloat16),
            jax.ShapeDtypeStruct((2 * extent // CUBE_ROWS, 2 * LANES), jnp.bfloat16),
        ),
        in_specs=[scalars],
        out_specs=(whole,) * 3,
        cost_estimate=pl.CostEstimate(
            flops=0, bytes_accessed=128 * extent * extent, transcendentals=0
        ),
        compiler_params=pltpu.CompilerParams(vmem_limit_bytes=VMEM_BYTES),
        name="tables",
    )(place)
    batch = 32 * slab
    filters = pl.pallas_call(
        functools.partial(filter_kernel, extent, slab),
        grid=(extent * slab // batch,),
        out_shape=jax.ShapeDtypeStruct((CUBE_COLS, extent, LANES), jnp.float32),
        in_specs=[
            scalars,
            pl.BlockSpec((batch, extent), lambda i: (i, 0)),
            pl.BlockSpec((3 * extent, extent), lambda i: (0, 0)),
        ],
        out_specs=pl.BlockSpec((CUBE_COLS, extent, LANES), lambda i: (0, 0, 0)),
        scratch_shapes=[pltpu.VMEM((batch, LANES), jnp.float32)] * 2,
        cost_estimate=pl.CostEstimate(
            flops=2 * extent * slab * 3 * extent * extent,
            bytes_accessed=8 * extent * slab * extent,
            transcendentals=0,
        ),
        compiler_params=pltpu.CompilerParams(vmem_limit_bytes=VMEM_BYTES // 4),
        name="filters",
    )(
        place,
        kernel_local.reshape(extent * slab, extent),
        jnp.asarray(np.concatenate([sort] * 3, axis=0), jnp.bfloat16),
    )
    first, last = constant_tables(extent)
    some = last[0].shape[0] // 2
    k0 = np.arange(some)
    weight = np.where((k0 == 0) | (k0 == extent // 2), 1.0, 2.0) * (k0 <= extent // 2)
    weight = jnp.asarray(weight / float(extent) ** 3, jnp.float32)[:, None]
    edge = jnp.where(me == members // 2, kernel_local[:some, 0, :] * weight, 0.0)
    return edge, cube_tables, filters, first, last


def cube_places(cubes, extent):
    slabs = extent // CUBE_COLS
    turns = extent // CUBE_ROWS
    plane, turn, slab = cubes // (turns * slabs), cubes // slabs % turns, cubes % slabs
    codes = jnp.stack([plane, turn, slab] + [jnp.zeros_like(slab)] * 5, axis=0)
    return slab * extent + plane, codes


def spectral(places, extent, blocks, gathered, tables):
    cube, back, turn, constants = tables
    half_count = gathered[0].shape[0] * blocks
    slabs = extent // CUBE_COLS
    chunk = min(512, half_count)
    operands = (gathered[0], cube, turn, gathered[1], back, *constants)
    whole = pl.BlockSpec(memory_space=pltpu.VMEM)
    anywhere = pl.BlockSpec(memory_space=pl.ANY)
    fixed = pl.BlockSpec(memory_space=pltpu.HBM)
    out = jax.ShapeDtypeStruct((half_count, LANES), jnp.float32)
    return pl.pallas_call(
        functools.partial(spectral_kernel, extent, chunk, len(operands)),
        out_shape=(out, out),
        in_specs=[pl.BlockSpec(memory_space=pltpu.SMEM), whole]
        + [anywhere, fixed, fixed, anywhere]
        + [fixed] * (len(operands) - 4),
        out_specs=(anywhere, anywhere),
        scratch_shapes=[pltpu.VMEM(operand.shape, operand.dtype) for operand in operands]
        + [pltpu.VMEM((half_count, LANES), jnp.float32)] * 2
        + [pltpu.VMEM((slabs * extent, LANES), jnp.float32)] * (2 * COPIES)
        + [pltpu.VMEM((chunk, LANES), jnp.float32)] * 2
        + [pltpu.VMEM((extent, extent), jnp.float32)]
        + [pltpu.SemaphoreType.DMA((len(operands),))]
        + [pltpu.SemaphoreType.DMA((2, half_count // chunk))],
        compiler_params=pltpu.CompilerParams(vmem_limit_bytes=SPECTRAL_BYTES),
        name="spectral",
    )(places[0], places[1], *operands)


NOTE_ROWS = 8
STEP_BLOCKS = 32
RIM_PART = 4


def sum_row(*values):
    lane = lax.broadcasted_iota(jnp.int32, (1, LANES), 1)
    row = jnp.zeros((1, LANES), jnp.float32)
    for index, value in enumerate(values):
        row = jnp.where(lane == index, value, row)
    return row


def put_edges(out_ref, values):
    step, steps = pl.program_id(0), pl.num_programs(0)
    panels = values.shape[1]
    below = out_ref.shape[0] - steps * STEP_BLOCKS // RIM_PART

    for first, lanes in ((0, slice(0, panels)), (steps - steps // RIM_PART, slice(panels, 2 * panels))):

        @pl.when((step >= first) & (step < first + steps // RIM_PART))
        def _():
            row = pl.multiple_of(below + (step - first) * STEP_BLOCKS, 8)
            out_ref[pl.ds(row, STEP_BLOCKS), lanes] = values


def project_kernel(proj_ref, values_ref, note_ref, out_ref):
    step = pl.program_id(0)
    charges = jnp.sum(proj_ref[...] * values_ref[...][:, :, None], axis=1)
    out_ref[pl.ds(pl.multiple_of(step * STEP_BLOCKS, STEP_BLOCKS), STEP_BLOCKS), :] = charges

    put_edges(out_ref, values_ref[...])

    @pl.when(step == pl.num_programs(0) - 1)
    def _():
        blocks = pl.num_programs(0) * STEP_BLOCKS
        out_ref[blocks : blocks + NOTE_ROWS, :] = jnp.broadcast_to(
            note_ref[...], (NOTE_ROWS, LANES)
        )


def complete_kernel(proj_ref, picked_ref, base_ref, rhs_ref, image_ref, out_ref):
    step = pl.program_id(0)
    tiles = proj_ref[...]
    image = base_ref[...] + jnp.sum(tiles * picked_ref[...][:, None, :], axis=2)
    image_ref[...] = image
    charges = jnp.sum(tiles * image[:, :, None], axis=1)
    out_ref[pl.ds(pl.multiple_of(step * STEP_BLOCKS, STEP_BLOCKS), STEP_BLOCKS), :] = charges
    put_edges(out_ref, image)
    blocks = pl.num_programs(0) * STEP_BLOCKS
    rhs = rhs_ref[...]
    row = sum_row(jnp.sum(rhs * rhs), jnp.sum(rhs * image), jnp.sum(image * image))

    @pl.when(step == 0)
    def _():
        out_ref[blocks : blocks + NOTE_ROWS, :] = jnp.zeros((NOTE_ROWS, LANES), jnp.float32)

    out_ref[blocks : blocks + 1, :] += row


def vector_scalars(sums):
    norm_sq, mixed, image_sq = sums[0:1, 0:1], sums[0:1, 1:2], sums[0:1, 2:3]
    gram_one = image_sq / norm_sq
    return jnp.sqrt(norm_sq), mixed / norm_sq, gram_one, jnp.sqrt(gram_one)


def close_kernel(proj_ref, picked_ref, base_ref, rhs_ref, first_ref, sums_ref, image_ref, out_ref):
    step = pl.program_id(0)
    second = base_ref[...] + jnp.sum(proj_ref[...] * picked_ref[...][:, None, :], axis=2)
    initial_norm, diag_one, _, scale = vector_scalars(sums_ref[...])
    basis_one = rhs_ref[...] / initial_norm
    image_one = first_ref[...] / initial_norm
    image_two = (second / initial_norm - diag_one * image_one) / scale
    image_ref[...] = image_two
    row = sum_row(
        jnp.sum(basis_one * image_two),
        jnp.sum(image_one * image_two),
        jnp.sum(image_two * image_two),
    )

    @pl.when(step == 0)
    def _():
        out_ref[...] = jnp.zeros((NOTE_ROWS, LANES), jnp.float32)

    out_ref[0:1, :] += row


def finish_kernel(rhs_ref, first_ref, image_ref, sums_ref, last_ref, answer_ref, residual_ref, rows_ref):
    initial_norm, diag_one, gram_one, scale = vector_scalars(sums_ref[...])
    last = last_ref[...]
    upper_two, gram_cross, gram_two = last[0:1, 0:1], last[0:1, 1:2], last[0:1, 2:3]
    rhs = rhs_ref[...]
    basis_one = rhs / initial_norm
    image_one = first_ref[...] / initial_norm
    basis_two = (image_one - diag_one * basis_one) / scale
    determinant = gram_one * gram_two - gram_cross * gram_cross
    weight_one = initial_norm * (diag_one * gram_two - upper_two * gram_cross) / determinant
    weight_two = initial_norm * (upper_two * gram_one - diag_one * gram_cross) / determinant
    half = rhs.shape[0] // 2
    for out_ref, value in (
        (answer_ref, weight_one * basis_one + weight_two * basis_two),
        (residual_ref, rhs - weight_one * image_one - weight_two * image_ref[...]),
    ):
        rows_ref[...] = value
        out_ref[...] = jnp.concatenate(
            [rows_ref[pl.ds(side, half, stride=2), :] for side in range(2)], axis=1
        )


def local_call(kernel, name, proj_tiles, rows, whole, outs):
    blocks, panels, points = proj_tiles.shape

    def cut(width):
        return pl.BlockSpec((STEP_BLOCKS, width), lambda i: (i, 0))

    def uncut(shape):
        return pl.BlockSpec(shape, lambda i: (0, 0))

    out_specs = [cut(out[1]) if out[0] == blocks else uncut(out) for out in outs]
    return pl.pallas_call(
        kernel,
        grid=(blocks // STEP_BLOCKS,),
        out_shape=[jax.ShapeDtypeStruct(out, jnp.float32) for out in outs],
        in_specs=[pl.BlockSpec((STEP_BLOCKS, panels, points), lambda i: (i, 0, 0))]
        + [cut(row.shape[1]) for row in rows]
        + [uncut(value.shape) for value in whole],
        out_specs=out_specs,
        cost_estimate=pl.CostEstimate(
            flops=4 * proj_tiles.size, bytes_accessed=4 * proj_tiles.size, transcendentals=0
        ),
        compiler_params=pltpu.CompilerParams(vmem_limit_bytes=VMEM_BYTES // 4),
        name=name,
    )(proj_tiles, *rows, *whole)


def piece_place(device):
    steps = partner_steps(lax.axis_size("px"))[:-1]
    away = lax.axis_index("px") ^ device
    return sum((away // step % 2) << place for place, step in enumerate(steps))


def halo(cells, distant):
    me, members = lax.axis_index("px"), lax.axis_size("px")
    width = cells.shape[0] // RIM_PART
    panels = cells.shape[1]
    sides = []
    for device, lane, present in ((me - 1, panels, me > 0), (me + 1, 0, me < members - 1)):
        place = jnp.where(present, piece_place(device), 0)
        start = (place, distant.shape[1] - width, lane)
        edge = lax.dynamic_slice(distant, start, (1, width, panels))[0]
        sides.append(jnp.where(present, edge, 0.0))
    return jnp.concatenate([sides[0], cells, sides[1]], axis=0)


def on_device(
    right_side, self_term, proj_tiles, owner_dev, cube_slot, near_src, near_tiles, kernel_hat
):
    members = lax.axis_size("px")
    blocks = proj_tiles.shape[0]
    extent = kernel_hat.shape[0]
    cubes_dev = extent // members * (extent // CUBE_ROWS) * (extent // CUBE_COLS)
    self_local = self_term.reshape(blocks, 64)
    cubes = owner_dev[:, 0] * cubes_dev + cube_slot
    *late, first, last = spectral_tables(kernel_hat)

    rhs = right_side.reshape(blocks, 64)
    note_shape = (blocks + NOTE_ROWS + blocks // RIM_PART, LANES)

    def base_of(values, gathered):
        sources = halo(values, gathered[1])[near_src].reshape(blocks, near_tiles.shape[2])
        return self_local * values + jnp.sum(near_tiles * sources[:, None, :], axis=2)

    def far(places, gathered):
        return scatter_pieces(*spectral(places, extent, blocks, gathered, tables))

    note = jnp.pad(cubes.astype(jnp.float32)[None, :], ((0, 0), (0, LANES - blocks)))
    (payload,) = local_call(project_kernel, "project", proj_tiles, [rhs], [note], [note_shape])
    gathered, (edge, cube_tables, filters) = gather_pieces(payload, late)
    tables = (*cube_tables, (*first, filters, *last, edge))
    base = base_of(rhs, gathered)
    all_cubes = jnp.concatenate([half[:, blocks, :blocks] for half in gathered], axis=0)
    places = cube_places(all_cubes.astype(jnp.int32).reshape(members * blocks), extent)
    image_one, payload = local_call(
        complete_kernel,
        "complete",
        proj_tiles,
        [far(places, gathered), base, rhs],
        [],
        [(blocks, 64), note_shape],
    )
    gathered, _ = gather_pieces(payload, ())
    base = base_of(image_one, gathered)
    sums = sum(jnp.sum(half[:, blocks, :], axis=0, keepdims=True) for half in gathered)
    image, weights = local_call(
        close_kernel,
        "close",
        proj_tiles,
        [far(places, gathered), base, rhs, image_one],
        [sums],
        [(blocks, 64), (NOTE_ROWS, LANES)],
    )
    weights = total(weights)
    out = jax.ShapeDtypeStruct((blocks // 2, 128), jnp.float32)
    answer, residual = pl.pallas_call(
        finish_kernel,
        out_shape=(out, out),
        scratch_shapes=[pltpu.VMEM((blocks, 64), jnp.float32)],
        name="finish",
    )(rhs, image_one, image, sums, weights)
    return (answer.reshape(blocks * 64), residual.reshape(blocks * 64))


def solution(mesh):
    return jax.shard_map(
        on_device,
        mesh=mesh,
        in_specs=(
            P(("groups", "px")),
            P(("groups", "px")),
            P(("groups", "px"), None, None),
            P(("groups", "px"), None),
            P(("groups", "px")),
            P(("groups", "px"), None),
            P(("groups", "px"), None, None),
            P(None, "px", None),
        ),
        out_specs=(P(("groups", "px")), P(("groups", "px"))),
        check_vma=False,
    )
```

```python
import functools
import jax
import jax.numpy as jnp
import numpy as np
from jax import lax
from jax.experimental import pallas as pl
from jax.experimental.pallas import tpu as pltpu
from jax.sharding import PartitionSpec as P

LANES = 128
CUBE_ROWS = 8
CUBE_COLS = 16
VMEM_BYTES = 60 * 1024 * 1024
SPECTRAL_BYTES = 60 * 1024 * 1024


def split(value):
    high = value.astype(jnp.bfloat16)
    low = (value - high.astype(jnp.float32)).astype(jnp.bfloat16)
    return high, low


def dot_in(left, right):
    return jnp.dot(left, right, preferred_element_type=jnp.float32)


def partner_steps(members):
    return [1 << i for i in reversed(range(members.bit_length() - 1))]


def exchange(value, step):
    members = lax.axis_size("px")
    return lax.ppermute(value, "px", [(i, i ^ step) for i in range(members)])


def step_orders(members):
    steps = partner_steps(members)
    return steps[:-3], (steps[-3:-1], steps[-3:-1][::-1]), steps[-1]


def gather_pieces(piece, beside):
    steps = partner_steps(lax.axis_size("px"))
    pieces = piece[None]
    done = []
    for index, step in enumerate(steps[:-1]):
        pieces = jnp.concatenate([pieces, exchange(pieces, step)], axis=0)
        if index < len(beside):
            pieces, value = lax.optimization_barrier((pieces, beside[index]))
            done.append(value)
    return (pieces, exchange(pieces, steps[-1])), done


def scatter_pieces(kept, sent, beside):
    lead, orders, last = step_orders(lax.axis_size("px"))
    arrived = exchange(sent, last)
    parts = [kept[i] + arrived[i] for i in range(2)]
    parts, beside = lax.optimization_barrier((parts, beside))
    for steps in zip(*(order[::-1] for order in orders)):
        half = parts[0].shape[0] // 2
        parts = [part[:half] + exchange(part[half:], step) for part, step in zip(parts, steps)]
    pieces = jnp.concatenate(parts, axis=1)
    for step in lead[::-1]:
        half = pieces.shape[0] // 2
        pieces = pieces[:half] + exchange(pieces[half:], step)
    return pieces[0], beside


def total(value):
    members = lax.axis_size("px")
    copies = jnp.broadcast_to(value[None], (members, *value.shape))
    return jnp.sum(lax.all_to_all(copies, "px", 0, 0), axis=0)


def butterfly16(real, imag, sign):
    def four(a, b, c, d):
        (ar, ai), (br, bi), (cr, ci), (dr, di) = a, b, c, d
        sr, si, tr, ti = ar + cr, ai + ci, ar - cr, ai - ci
        ur, ui, vr, vi = br + dr, bi + di, br - dr, bi - di
        wr, wi = (-vi, vr) if sign > 0 else (vi, -vr)
        return (sr + ur, si + ui), (tr + wr, ti + wi), (sr - ur, si - ui), (tr - wr, ti - wi)

    def turned(value, power):
        power %= 16
        if power == 0:
            return value
        r, i = value
        cosine = float(np.cos(2 * np.pi * power / 16))
        sine = sign * float(np.sin(2 * np.pi * power / 16))
        if power == 4:
            return (-i, r) if sign > 0 else (i, -r)
        return (r * cosine - i * sine, r * sine + i * cosine)

    points = list(zip(real, imag))
    inner = [four(*(points[4 * j1 + j0] for j1 in range(4))) for j0 in range(4)]
    out = [None] * 16
    for b1 in range(4):
        column = [turned(inner[j0][b1], j0 * b1) for j0 in range(4)]
        for b0, value in enumerate(four(*column)):
            out[b1 + 4 * b0] = value
    return [v[0] for v in out], [v[1] for v in out]


def left_terms(value):
    high, low = split(value)
    return jnp.concatenate([high, low, high], axis=1)


def right_terms(value):
    high, low = split(value)
    return jnp.concatenate([high, high, low], axis=0)


def where_equal(left, right):
    return jnp.where(left == right, 1.0, 0.0).astype(jnp.bfloat16)


COPIES = 4
GROUP = 8


def spectral_kernel(extent, chunk, operands, rows_ref, codes_ref, *refs):
    sources, (kept_out, sent_out), refs = refs[:operands], refs[operands : operands + 2], refs[operands + 2 :]
    tables, (kept_ref, sent_ref), refs = refs[:operands], refs[operands : operands + 2], refs[operands + 2 :]
    grids, refs = refs[: 2 * COPIES], refs[2 * COPIES :]
    grids = [grids[2 * i : 2 * i + 2] for i in range(COPIES)]
    rows, dense, sem, out_sem = refs[:2], refs[2], refs[3], refs[4]
    near_ref, distant_ref, cube_ref, turn_ref, back_ref = tables[:5]
    even_ref, odd_ref, uneven_ref, unodd_ref = tables[5:9]
    line_ref, unline_ref, twist_ref, filter_ref = tables[9:13]
    plane_ref, unplane_ref, full_ref, unfull_ref, edge_ref = tables[13:]
    pieces, blocks = kept_ref.shape[:2]
    half_count = pieces * blocks
    slabs = extent // CUBE_COLS
    half = extent // 2
    lead = pieces // 4
    taken = chunk // blocks
    bunch = min(lead, taken)

    def other_place(place):
        first, second = place // lead % 2, place // (2 * lead)
        return place % lead + lead * (second + 2 * first)

    moves = [
        pltpu.make_async_copy(source, table, sem.at[i])
        for i, (source, table) in enumerate(zip(sources, tables))
    ]
    early, late = [moves[0], *moves[2:4]], moves[1:2]
    for move in early:
        move.start()

    def clear(i, _):
        place = pl.ds(pl.multiple_of(i * 64, 64), 64)
        for grid in grids:
            for ref in grid:
                ref[place, :] = jnp.zeros((64, LANES), jnp.float32)
        return 0

    lax.fori_loop(0, slabs * extent // 64, clear, 0)
    dense[...] = jnp.zeros(dense.shape, jnp.float32)

    def marks(start):
        codes = jnp.transpose(codes_ref[:, pl.ds(start, chunk)])
        turn_count = extent // CUBE_ROWS
        wide = lax.broadcasted_iota(jnp.int32, (chunk, extent), 1)
        turn_lane = lax.broadcasted_iota(jnp.int32, (chunk, 2 * turn_count), 1) % turn_count
        turned = dot_in(where_equal(turn_lane, codes[:, 1:2]), turn_ref[...])
        return codes, wide, turned[:, :LANES], turned[:, LANES:]

    def spread(source_ref, offset, step, _):
        start = pl.multiple_of(offset + step * chunk, chunk)
        values = source_ref[pl.ds(step * taken, taken), :blocks, :]
        both = dot_in(left_terms(values.reshape(chunk, LANES)), cube_ref[...])
        codes, wide, cosine, sine = marks(start)
        real, imag = both[:, :LANES], both[:, LANES : 2 * LANES]
        rows[0][...] = real * cosine + imag * sine
        rows[1][...] = imag * cosine - real * sine
        high, low = split(jnp.where(wide // CUBE_COLS == codes[:, 2:3], both[:, 2 * LANES :], 0.0))
        plane = where_equal(wide, codes[:, 0:1])
        contract = (((0,), (0,)), ((), ()))
        dense[...] += lax.dot_general(
            plane, high, contract, preferred_element_type=jnp.float32
        ) + lax.dot_general(plane, low, contract, preferred_element_type=jnp.float32)

        def add(i, _):
            for copy in range(COPIES):
                place = i + copy * (chunk // COPIES)
                row = rows_ref[start + place]
                for ref, source in zip(grids[copy], rows):
                    ref[pl.ds(row, 1), :] += source[pl.ds(place, 1), :]
            return 0

        lax.fori_loop(0, chunk // COPIES, add, 0, unroll=8)
        return 0

    for move in early:
        move.wait()
    for move in late + moves[4:]:
        move.start()
    for index, source_ref in enumerate((near_ref, distant_ref)):
        if index:
            for move in late:
                move.wait()
        body = functools.partial(spread, source_ref, index * half_count)
        lax.fori_loop(0, half_count // chunk, body, 0)

    grid_real, grid_imag = grids[0]

    def across(sign):
        def body(i, _):
            start = pl.multiple_of(i * 8, 8)
            places = [pl.ds(start + slab * extent, 8) for slab in range(slabs)]
            values = []
            for part in range(2):
                values.append([grids[0][part][place, :] for place in places])
                if sign < 0:
                    for grid in grids[1:]:
                        values[part] = [v + grid[part][p, :] for v, p in zip(values[part], places)]
            values = butterfly16(*values, sign)
            for place, r, j in zip(places, *values):
                grid_real[place, :] = r
                grid_imag[place, :] = j
            return 0

        lax.fori_loop(0, extent // 8, body, 0)

    across(-1)
    for move in moves[4:]:
        move.wait()

    def middle(group, _):
        starts = [pl.multiple_of((GROUP * group + i) * extent, extent) for i in range(GROUP)]
        cuts = [slice(i * LANES, (i + 1) * LANES) for i in range(GROUP)]

        def joined(offset):
            return jnp.concatenate(
                [
                    jnp.concatenate([ref[pl.ds(start + offset, half), :] for start in starts], axis=1)
                    for ref in grids[0]
                ],
                axis=0,
            )

        first, last = joined(0), joined(half)
        even = dot_in(even_ref[...], right_terms(first + last))
        odd = dot_in(odd_ref[...], right_terms(first - last))
        real = jnp.concatenate([even[:half], odd[:half]], axis=0)
        imag = jnp.concatenate([even[half:], odd[half:]], axis=0)
        cosine, sine = twist_ref[group, 0:1, :], twist_ref[group, 1:2, :]
        real, imag = real * cosine + imag * sine, imag * cosine - real * sine
        lines = jnp.concatenate(
            [
                jnp.concatenate([real[:, cut], imag[:, cut]], axis=1)
                for cut in cuts
            ],
            axis=0,
        )
        lines = dot_in(left_terms(lines), line_ref[...])
        scale = jnp.concatenate([filter_ref[GROUP * group + i] for i in range(GROUP)], axis=0)
        lines = lines * jnp.concatenate([scale, scale], axis=1)
        lines = dot_in(left_terms(lines), unline_ref[...])
        lines = [lines[i * extent : (i + 1) * extent] for i in range(GROUP)]
        real = jnp.concatenate([line[:, :LANES] for line in lines], axis=1)
        imag = jnp.concatenate([line[:, LANES:] for line in lines], axis=1)
        real, imag = real * cosine - imag * sine, imag * cosine + real * sine
        even = jnp.concatenate([real[:half], imag[:half]], axis=0)
        odd = jnp.concatenate([real[half:], imag[half:]], axis=0)
        even = dot_in(uneven_ref[...], right_terms(even))
        odd = dot_in(unodd_ref[...], right_terms(odd))
        for offset, planes in ((0, even + odd), (half, even - odd)):
            for part, ref in enumerate(grids[0]):
                for i, start in enumerate(starts):
                    ref[pl.ds(start + offset, half), :] = planes[
                        part * half : (part + 1) * half, i * LANES : (i + 1) * LANES
                    ]
        return 0

    lax.fori_loop(0, slabs // GROUP, middle, 0, unroll=1)
    planes = dot_in(plane_ref[...], right_terms(dense[...]))
    some = planes.shape[0] // 2
    planes = jnp.concatenate([planes[:some], planes[some:]], axis=1)
    planes = dot_in(left_terms(planes), full_ref[...])
    planes = planes * jnp.concatenate([edge_ref[...], edge_ref[...]], axis=1)
    planes = dot_in(left_terms(planes), unfull_ref[...])
    planes = jnp.concatenate([planes[:, :extent], planes[:, extent:]], axis=0)
    dense[...] = dot_in(unplane_ref[...], right_terms(planes))
    across(1)

    def leaving(index, step):
        out, ref = (kept_out, sent_out)[index], (kept_ref, sent_ref)[index]
        cut = blocks // 2
        place = pl.ds(step * taken, taken)
        moves = [(ref.at[place, :cut, :], out.at[0, place])]
        for i in range(taken // bunch):
            start = step * taken + i * bunch
            goal = out.at[1, pl.ds(other_place(start), bunch)]
            moves.append((ref.at[pl.ds(start, bunch), cut:, :], goal))
        return [
            pltpu.make_async_copy(*move, out_sem.at[index, step, i])
            for i, move in enumerate(moves)
        ]

    def collect(index, step, _):
        out_ref = (kept_ref, sent_ref)[index]
        offset = index * half_count
        start = pl.multiple_of(offset + step * chunk, chunk)

        def take(i, _):
            row = rows_ref[start + i]
            for ref, source in zip(rows, grids[0]):
                ref[pl.ds(i, 1), :] = source[pl.ds(row, 1), :]
            return 0

        lax.fori_loop(0, chunk, take, 0, unroll=16)
        codes, wide, cosine, sine = marks(start)
        plane = where_equal(wide, codes[:, 0:1])
        high, low = split(dense[...])
        edge = dot_in(plane, high) + dot_in(plane, low)
        edge = jnp.where(wide // CUBE_COLS == codes[:, 2:3], edge, 0.0)
        real, imag = rows[0][...], rows[1][...]
        both = jnp.concatenate(
            [real * cosine - imag * sine, imag * cosine + real * sine, edge], axis=1
        )
        both = dot_in(left_terms(both), back_ref[...])
        out_ref[pl.ds(step * taken, taken), :, :] = both.reshape(taken, blocks, LANES)
        for move in leaving(index, step):
            move.start()
        return 0

    for index in range(2):
        lax.fori_loop(0, half_count // chunk, functools.partial(collect, index), 0)

    def finish(step, _):
        for index in range(2):
            for move in leaving(index, step):
                move.wait()
        return 0

    lax.fori_loop(0, half_count // chunk, finish, 0)


def stacked_table(table, axis):
    table = np.asarray(table, np.float32)
    high = table.astype(jnp.bfloat16)
    low = (table - high.astype(np.float32)).astype(jnp.bfloat16)
    order = [high, high, low] if axis == 0 else [high, low, high]
    return jnp.asarray(np.concatenate(order, axis=axis))


def constant_tables(extent):
    half = extent // 2
    n0 = np.arange(half)
    planes = []
    for k0 in (np.arange(0, extent, 2), np.arange(1, extent, 2)):
        angle = 2.0 * np.pi / extent * (k0[:, None] * n0[None, :] % extent)
        cosine, sine = np.cos(angle), np.sin(angle)
        planes.append(np.block([[cosine, sine], [-sine, cosine]]))
    small = np.arange(CUBE_COLS)
    angle = 2.0 * np.pi / CUBE_COLS * (small[:, None] * small[None, :] % CUBE_COLS)
    cosine = np.kron(np.eye(LANES // CUBE_COLS), np.cos(angle))
    sine = np.kron(np.eye(LANES // CUBE_COLS), np.sin(angle))
    line = np.block([[cosine, -sine], [sine, cosine]])
    angle = 2.0 * np.pi / extent * (small[:, None] * (np.arange(LANES) % CUBE_COLS)[None, :])
    twist = np.stack([np.cos(angle), np.sin(angle)], axis=1)
    twist = np.concatenate([twist[i::GROUP] for i in range(GROUP)], axis=2)
    some = np.arange(-(-(half + 1) // 8) * 8)
    whole = np.arange(extent)
    angle = 2.0 * np.pi / extent * (some[:, None] * whole[None, :] % extent)
    plane = np.concatenate([np.cos(angle), -np.sin(angle)], axis=0)
    angle = 2.0 * np.pi / extent * (whole[:, None] * whole[None, :] % extent)
    cosine, sine = np.cos(angle), np.sin(angle)
    full = np.block([[cosine, -sine], [sine, cosine]])
    first = [stacked_table(table, 1) for table in (*planes, planes[0].T, planes[1].T)]
    first += [stacked_table(line, 0), stacked_table(line.T, 0), jnp.asarray(twist, jnp.float32)]
    last = [stacked_table(plane, 1), stacked_table(plane.T, 1)]
    last += [stacked_table(full, 0), stacked_table(full.T, 0)]
    return first, last


def tables_kernel(extent, held, place_ref, cube_ref, back_ref, turn_ref):
    first = place_ref[0]
    points = CUBE_ROWS * CUBE_COLS

    def angles(numerator):
        angle = (2.0 * np.pi / extent) * (numerator % extent).astype(jnp.float32)
        return jnp.cos(angle), jnp.sin(angle)

    for shape, axis in (((points, LANES), 0), ((LANES, points), 1)):
        point = lax.broadcasted_iota(jnp.int32, shape, axis)
        column = lax.broadcasted_iota(jnp.int32, shape, 1 - axis)
        k1 = first + column // CUBE_COLS
        cosine, sine = angles((point // CUBE_COLS) * k1)
        same = (point % CUBE_COLS == column % CUBE_COLS) & (column // CUBE_COLS < held)
        shape = (points, extent) if axis == 0 else (extent, points)
        point = lax.broadcasted_iota(jnp.int32, shape, axis)
        column = lax.broadcasted_iota(jnp.int32, shape, 1 - axis)
        flip = 1.0 - 2.0 * ((point // CUBE_COLS) % 2).astype(jnp.float32)
        edge = jnp.where(point % CUBE_COLS == column % CUBE_COLS, flip, 0.0)
        table = jnp.concatenate(
            [jnp.where(same, cosine, 0.0), jnp.where(same, -sine, 0.0), edge], axis=1 - axis
        )
        (cube_ref if axis == 0 else back_ref)[...] = right_terms(table)
    shape = (extent // CUBE_ROWS, LANES)
    column = lax.broadcasted_iota(jnp.int32, shape, 1)
    turn = lax.broadcasted_iota(jnp.int32, shape, 0) * CUBE_ROWS
    high, low = split(jnp.concatenate(angles(turn * (first + column // CUBE_COLS)), axis=1))
    turn_ref[...] = jnp.concatenate([high, low], axis=0)


def filter_kernel(extent, slab, place_ref, kernel_ref, sort_ref, filter_ref, *lines):
    first, shift = place_ref[0], place_ref[1]
    held = slab // 2
    batch = kernel_ref.shape[0]
    count = batch // slab // 2
    step = pl.program_id(0)
    values = kernel_ref[...]
    high = values.astype(jnp.bfloat16)
    rest = values - high.astype(jnp.float32)
    values = dot_in(jnp.concatenate([high, *split(rest)], axis=1), sort_ref[...])
    for side, ref in enumerate(lines):
        ref[...] = values[:, side * LANES : (side + 1) * LANES]
    groups = LANES // CUBE_COLS
    lane = lax.broadcasted_iota(jnp.int32, (1, LANES), 1)
    weight = jnp.where(first + lane // CUBE_COLS == 0, 1.0, 2.0) / float(extent) ** 3
    weight = jnp.where(lane // CUBE_COLS < held, weight, 0.0)
    group = lax.broadcasted_iota(jnp.int32, (count, LANES), 1) // CUBE_COLS
    for odd in range(2):
        row = pl.multiple_of(odd * (extent // 2) + step * count, count)
        for side, ref in enumerate(lines):
            values = [
                ref[pl.ds(shift + k + odd * slab, count, stride=2 * slab), :]
                if k < held
                else jnp.zeros((count, LANES), jnp.float32)
                for k in range(groups)
            ]
            apart = 1
            while apart < groups:
                upper = group // apart % 2 == 1
                turned = list(values)
                for k in range(groups):
                    if k // apart % 2 == 0:
                        one, two = values[k], values[k + apart]
                        turned[k] = jnp.where(upper, pltpu.roll(two, apart * CUBE_COLS, 1), one)
                        turned[k + apart] = jnp.where(
                            upper, two, pltpu.roll(one, LANES - apart * CUBE_COLS, 1)
                        )
                values = turned
                apart *= 2
            for k in range(groups):
                filter_ref[side * groups + k, pl.ds(row, count), :] = values[k] * weight


def spectral_tables(kernel_local):
    members = lax.axis_size("px")
    me = lax.axis_index("px")
    extent, slab = kernel_local.shape[:2]
    shift = (me >= members // 2).astype(jnp.int32)
    k2 = np.arange(extent)
    sort = np.zeros((extent, extent), np.float32)
    sort[k2, k2 % CUBE_COLS * CUBE_COLS + k2 // CUBE_COLS] = 1.0
    whole = pl.BlockSpec(memory_space=pltpu.VMEM)
    points = CUBE_ROWS * CUBE_COLS
    size = 2 * LANES + extent
    place = jnp.stack([me * slab + shift, shift])
    scalars = pl.BlockSpec(memory_space=pltpu.SMEM)
    cube_tables = pl.pallas_call(
        functools.partial(tables_kernel, extent, slab // 2),
        out_shape=(
            jax.ShapeDtypeStruct((3 * points, size), jnp.bfloat16),
            jax.ShapeDtypeStruct((3 * size, points), jnp.bfloat16),
            jax.ShapeDtypeStruct((2 * extent // CUBE_ROWS, 2 * LANES), jnp.bfloat16),
        ),
        in_specs=[scalars],
        out_specs=(whole,) * 3,
        cost_estimate=pl.CostEstimate(
            flops=0, bytes_accessed=128 * extent * extent, transcendentals=0
        ),
        compiler_params=pltpu.CompilerParams(vmem_limit_bytes=VMEM_BYTES),
        name="tables",
    )(place)
    batch = 32 * slab
    filters = pl.pallas_call(
        functools.partial(filter_kernel, extent, slab),
        grid=(extent * slab // batch,),
        out_shape=jax.ShapeDtypeStruct((CUBE_COLS, extent, LANES), jnp.float32),
        in_specs=[
            scalars,
            pl.BlockSpec((batch, extent), lambda i: (i, 0)),
            pl.BlockSpec((3 * extent, extent), lambda i: (0, 0)),
        ],
        out_specs=pl.BlockSpec((CUBE_COLS, extent, LANES), lambda i: (0, 0, 0)),
        scratch_shapes=[pltpu.VMEM((batch, LANES), jnp.float32)] * 2,
        cost_estimate=pl.CostEstimate(
            flops=2 * extent * slab * 3 * extent * extent,
            bytes_accessed=8 * extent * slab * extent,
            transcendentals=0,
        ),
        compiler_params=pltpu.CompilerParams(vmem_limit_bytes=VMEM_BYTES // 4),
        name="filters",
    )(
        place,
        kernel_local.reshape(extent * slab, extent),
        jnp.asarray(np.concatenate([sort] * 3, axis=0), jnp.bfloat16),
    )
    first, last = constant_tables(extent)
    some = last[0].shape[0] // 2
    k0 = np.arange(some)
    weight = np.where((k0 == 0) | (k0 == extent // 2), 1.0, 2.0) * (k0 <= extent // 2)
    weight = jnp.asarray(weight / float(extent) ** 3, jnp.float32)[:, None]
    edge = jnp.where(me == members // 2, kernel_local[:some, 0, :] * weight, 0.0)
    return edge, cube_tables, filters, first, last


def cube_places(cubes, extent):
    slabs = extent // CUBE_COLS
    turns = extent // CUBE_ROWS
    plane, turn, slab = cubes // (turns * slabs), cubes // slabs % turns, cubes % slabs
    codes = jnp.stack([plane, turn, slab] + [jnp.zeros_like(slab)] * 5, axis=0)
    return slab * extent + plane, codes


def spectral(places, extent, blocks, gathered, tables):
    cube, back, turn, constants = tables
    pieces = gathered[0].shape[0]
    slabs = extent // CUBE_COLS
    taken = min(4, pieces)
    chunk = taken * blocks
    operands = (*gathered, cube, turn, back, *constants)
    anywhere = pl.BlockSpec(memory_space=pl.ANY)
    fixed = pl.BlockSpec(memory_space=pltpu.HBM)
    out = jax.ShapeDtypeStruct((2, pieces, blocks // 2, LANES), jnp.float32)
    return pl.pallas_call(
        functools.partial(spectral_kernel, extent, chunk, len(operands)),
        out_shape=(out, out),
        in_specs=[
            pl.BlockSpec(memory_space=pltpu.SMEM),
            pl.BlockSpec(memory_space=pltpu.VMEM),
            *[anywhere] * 2,
            *[fixed] * (len(operands) - 2),
        ],
        out_specs=(anywhere, anywhere),
        scratch_shapes=[pltpu.VMEM(operand.shape, operand.dtype) for operand in operands]
        + [pltpu.VMEM((pieces, blocks, LANES), jnp.float32)] * 2
        + [pltpu.VMEM((slabs * extent, LANES), jnp.float32)] * (2 * COPIES)
        + [pltpu.VMEM((chunk, LANES), jnp.float32)] * 2
        + [pltpu.VMEM((extent, extent), jnp.float32)]
        + [pltpu.SemaphoreType.DMA((len(operands),))]
        + [pltpu.SemaphoreType.DMA((2, pieces // taken, 5))],
        compiler_params=pltpu.CompilerParams(vmem_limit_bytes=SPECTRAL_BYTES),
        name="spectral",
    )(places[0], places[1], *operands)


NOTE_ROWS = 8
STEP_BLOCKS = 32
RIM_PART = 4


def sum_row(*values):
    lane = lax.broadcasted_iota(jnp.int32, (1, LANES), 1)
    row = jnp.zeros((1, LANES), jnp.float32)
    for index, value in enumerate(values):
        row = jnp.where(lane == index, value, row)
    return row


def put_edges(out_ref, values):
    step, steps = pl.program_id(0), pl.num_programs(0)
    panels = values.shape[1]
    below = out_ref.shape[0] - steps * STEP_BLOCKS // RIM_PART

    for first, lanes in ((0, slice(0, panels)), (steps - steps // RIM_PART, slice(panels, 2 * panels))):

        @pl.when((step >= first) & (step < first + steps // RIM_PART))
        def _():
            row = pl.multiple_of(below + (step - first) * STEP_BLOCKS, 8)
            out_ref[pl.ds(row, STEP_BLOCKS), lanes] = values


def project_kernel(proj_ref, values_ref, note_ref, out_ref):
    step = pl.program_id(0)
    charges = jnp.sum(proj_ref[...] * values_ref[...][:, :, None], axis=1)
    out_ref[pl.ds(pl.multiple_of(step * STEP_BLOCKS, STEP_BLOCKS), STEP_BLOCKS), :] = charges

    put_edges(out_ref, values_ref[...])

    @pl.when(step == pl.num_programs(0) - 1)
    def _():
        blocks = pl.num_programs(0) * STEP_BLOCKS
        out_ref[blocks : blocks + NOTE_ROWS, :] = jnp.broadcast_to(
            note_ref[...], (NOTE_ROWS, LANES)
        )


def complete_kernel(proj_ref, picked_ref, base_ref, rhs_ref, image_ref, out_ref):
    step = pl.program_id(0)
    tiles = proj_ref[...]
    image = base_ref[...] + jnp.sum(tiles * picked_ref[...][:, None, :], axis=2)
    image_ref[...] = image
    charges = jnp.sum(tiles * image[:, :, None], axis=1)
    out_ref[pl.ds(pl.multiple_of(step * STEP_BLOCKS, STEP_BLOCKS), STEP_BLOCKS), :] = charges
    put_edges(out_ref, image)
    blocks = pl.num_programs(0) * STEP_BLOCKS
    rhs = rhs_ref[...]
    row = sum_row(jnp.sum(rhs * rhs), jnp.sum(rhs * image), jnp.sum(image * image))

    @pl.when(step == 0)
    def _():
        out_ref[blocks : blocks + NOTE_ROWS, :] = jnp.zeros((NOTE_ROWS, LANES), jnp.float32)

    out_ref[blocks : blocks + 1, :] += row


def vector_scalars(sums):
    norm_sq, mixed, image_sq = sums[0:1, 0:1], sums[0:1, 1:2], sums[0:1, 2:3]
    gram_one = image_sq / norm_sq
    return jnp.sqrt(norm_sq), mixed / norm_sq, gram_one, jnp.sqrt(gram_one)


def close_kernel(proj_ref, picked_ref, base_ref, rhs_ref, first_ref, sums_ref, image_ref, out_ref):
    step = pl.program_id(0)
    second = base_ref[...] + jnp.sum(proj_ref[...] * picked_ref[...][:, None, :], axis=2)
    initial_norm, diag_one, _, scale = vector_scalars(sums_ref[...])
    basis_one = rhs_ref[...] / initial_norm
    image_one = first_ref[...] / initial_norm
    image_two = (second / initial_norm - diag_one * image_one) / scale
    image_ref[...] = image_two
    row = sum_row(
        jnp.sum(basis_one * image_two),
        jnp.sum(image_one * image_two),
        jnp.sum(image_two * image_two),
    )

    @pl.when(step == 0)
    def _():
        out_ref[...] = jnp.zeros((NOTE_ROWS, LANES), jnp.float32)

    out_ref[0:1, :] += row


def finish_kernel(rhs_ref, first_ref, image_ref, sums_ref, last_ref, answer_ref, residual_ref, rows_ref):
    initial_norm, diag_one, gram_one, scale = vector_scalars(sums_ref[...])
    last = last_ref[...]
    upper_two, gram_cross, gram_two = last[0:1, 0:1], last[0:1, 1:2], last[0:1, 2:3]
    rhs = rhs_ref[...]
    basis_one = rhs / initial_norm
    image_one = first_ref[...] / initial_norm
    basis_two = (image_one - diag_one * basis_one) / scale
    determinant = gram_one * gram_two - gram_cross * gram_cross
    weight_one = initial_norm * (diag_one * gram_two - upper_two * gram_cross) / determinant
    weight_two = initial_norm * (upper_two * gram_one - diag_one * gram_cross) / determinant
    half = rhs.shape[0] // 2
    for out_ref, value in (
        (answer_ref, weight_one * basis_one + weight_two * basis_two),
        (residual_ref, rhs - weight_one * image_one - weight_two * image_ref[...]),
    ):
        rows_ref[...] = value
        out_ref[...] = jnp.concatenate(
            [rows_ref[pl.ds(side, half, stride=2), :] for side in range(2)], axis=1
        )


def local_call(kernel, name, proj_tiles, rows, whole, outs):
    blocks, panels, points = proj_tiles.shape

    def cut(width):
        return pl.BlockSpec((STEP_BLOCKS, width), lambda i: (i, 0))

    def uncut(shape):
        return pl.BlockSpec(shape, lambda i: (0, 0))

    out_specs = [cut(out[1]) if out[0] == blocks else uncut(out) for out in outs]
    return pl.pallas_call(
        kernel,
        grid=(blocks // STEP_BLOCKS,),
        out_shape=[jax.ShapeDtypeStruct(out, jnp.float32) for out in outs],
        in_specs=[pl.BlockSpec((STEP_BLOCKS, panels, points), lambda i: (i, 0, 0))]
        + [cut(row.shape[1]) for row in rows]
        + [uncut(value.shape) for value in whole],
        out_specs=out_specs,
        cost_estimate=pl.CostEstimate(
            flops=4 * proj_tiles.size, bytes_accessed=4 * proj_tiles.size, transcendentals=0
        ),
        compiler_params=pltpu.CompilerParams(vmem_limit_bytes=VMEM_BYTES // 4),
        name=name,
    )(proj_tiles, *rows, *whole)


def piece_place(device):
    steps = partner_steps(lax.axis_size("px"))[:-1]
    away = lax.axis_index("px") ^ device
    return sum((away // step % 2) << place for place, step in enumerate(steps))


def halo(cells, distant):
    me, members = lax.axis_index("px"), lax.axis_size("px")
    width = cells.shape[0] // RIM_PART
    panels = cells.shape[1]
    sides = []
    for device, lane, present in ((me - 1, panels, me > 0), (me + 1, 0, me < members - 1)):
        place = jnp.where(present, piece_place(device), 0)
        start = (place, distant.shape[1] - width, lane)
        edge = lax.dynamic_slice(distant, start, (1, width, panels))[0]
        sides.append(jnp.where(present, edge, 0.0))
    return jnp.concatenate([sides[0], cells, sides[1]], axis=0)


def on_device(
    right_side, self_term, proj_tiles, owner_dev, cube_slot, near_src, near_tiles, kernel_hat
):
    members = lax.axis_size("px")
    blocks = proj_tiles.shape[0]
    extent = kernel_hat.shape[0]
    cubes_dev = extent // members * (extent // CUBE_ROWS) * (extent // CUBE_COLS)
    self_local = self_term.reshape(blocks, 64)
    cubes = owner_dev[:, 0] * cubes_dev + cube_slot
    *late, first, last = spectral_tables(kernel_hat)

    rhs = right_side.reshape(blocks, 64)
    note_shape = (blocks + NOTE_ROWS + blocks // RIM_PART, LANES)

    def base_of(values, extended):
        sources = extended[near_src].reshape(blocks, near_tiles.shape[2])
        return self_local * values + jnp.sum(near_tiles * sources[:, None, :], axis=2)

    def far(places, gathered, values):
        extended = halo(values, gathered[1])
        shares = spectral(places, extent, blocks, gathered, tables)
        picked, extended = scatter_pieces(*shares, extended)
        return picked, base_of(values, extended)

    note = jnp.pad(cubes.astype(jnp.float32)[None, :], ((0, 0), (0, LANES - blocks)))
    (payload,) = local_call(project_kernel, "project", proj_tiles, [rhs], [note], [note_shape])
    gathered, (edge, cube_tables, filters) = gather_pieces(payload, late)
    tables = (*cube_tables, (*first, filters, *last, edge))
    all_cubes = jnp.concatenate([half[:, blocks, :blocks] for half in gathered], axis=0)
    places = cube_places(all_cubes.astype(jnp.int32).reshape(members * blocks), extent)
    image_one, payload = local_call(
        complete_kernel,
        "complete",
        proj_tiles,
        [*far(places, gathered, rhs), rhs],
        [],
        [(blocks, 64), note_shape],
    )
    gathered, _ = gather_pieces(payload, ())
    sums = sum(jnp.sum(half[:, blocks, :], axis=0, keepdims=True) for half in gathered)
    image, weights = local_call(
        close_kernel,
        "close",
        proj_tiles,
        [*far(places, gathered, image_one), rhs, image_one],
        [sums],
        [(blocks, 64), (NOTE_ROWS, LANES)],
    )
    weights = total(weights)
    out = jax.ShapeDtypeStruct((blocks // 2, 128), jnp.float32)
    answer, residual = pl.pallas_call(
        finish_kernel,
        out_shape=(out, out),
        scratch_shapes=[pltpu.VMEM((blocks, 64), jnp.float32)],
        name="finish",
    )(rhs, image_one, image, sums, weights)
    return (answer.reshape(blocks * 64), residual.reshape(blocks * 64))


def solution(mesh):
    return jax.shard_map(
        on_device,
        mesh=mesh,
        in_specs=(
            P(("groups", "px")),
            P(("groups", "px")),
            P(("groups", "px"), None, None),
            P(("groups", "px"), None),
            P(("groups", "px")),
            P(("groups", "px"), None),
            P(("groups", "px"), None, None),
            P(None, "px", None),
        ),
        out_specs=(P(("groups", "px")), P(("groups", "px"))),
        check_vma=False,
    )
```

```python
import functools
import jax
import jax.numpy as jnp
import numpy as np
from jax import lax
from jax.experimental import pallas as pl
from jax.experimental.pallas import tpu as pltpu
from jax.sharding import PartitionSpec as P

LANES = 128
CUBE_ROWS = 8
CUBE_COLS = 16
VMEM_BYTES = 60 * 1024 * 1024
SPECTRAL_BYTES = 60 * 1024 * 1024


def split(value):
    high = value.astype(jnp.bfloat16)
    low = (value - high.astype(jnp.float32)).astype(jnp.bfloat16)
    return high, low


def dot_in(left, right):
    return jnp.dot(left, right, preferred_element_type=jnp.float32)


def partner_steps(members):
    return [1 << i for i in reversed(range(members.bit_length() - 1))]


def exchange(value, step):
    members = lax.axis_size("px")
    return lax.ppermute(value, "px", [(i, i ^ step) for i in range(members)])


def step_orders(members):
    steps = partner_steps(members)
    return steps[:-3], (steps[-3:-1], steps[-3:-1][::-1]), steps[-1]


def gather_pieces(piece, beside):
    steps = partner_steps(lax.axis_size("px"))
    pieces = piece[None]
    done = []
    for index, step in enumerate(steps[:-1]):
        pieces = jnp.concatenate([pieces, exchange(pieces, step)], axis=0)
        if index < len(beside):
            pieces, value = lax.optimization_barrier((pieces, beside[index]))
            done.append(value)
    return (pieces, exchange(pieces, steps[-1])), done


def scatter_pieces(kept, sent, beside):
    lead, orders, last = step_orders(lax.axis_size("px"))
    arrived = exchange(sent, last)
    parts = [kept[i] + arrived[i] for i in range(2)]
    parts, beside = lax.optimization_barrier((parts, beside))
    for steps in zip(*(order[::-1] for order in orders)):
        half = parts[0].shape[0] // 2
        parts = [part[:half] + exchange(part[half:], step) for part, step in zip(parts, steps)]
    pieces = jnp.concatenate(parts, axis=1)
    for step in lead[::-1]:
        half = pieces.shape[0] // 2
        pieces = pieces[:half] + exchange(pieces[half:], step)
    return pieces[0], beside


def total(value):
    members = lax.axis_size("px")
    copies = jnp.broadcast_to(value[None], (members, *value.shape))
    return jnp.sum(lax.all_to_all(copies, "px", 0, 0), axis=0)


def butterfly16(real, imag, sign):
    def four(a, b, c, d):
        (ar, ai), (br, bi), (cr, ci), (dr, di) = a, b, c, d
        sr, si, tr, ti = ar + cr, ai + ci, ar - cr, ai - ci
        ur, ui, vr, vi = br + dr, bi + di, br - dr, bi - di
        wr, wi = (-vi, vr) if sign > 0 else (vi, -vr)
        return (sr + ur, si + ui), (tr + wr, ti + wi), (sr - ur, si - ui), (tr - wr, ti - wi)

    def turned(value, power):
        power %= 16
        if power == 0:
            return value
        r, i = value
        cosine = float(np.cos(2 * np.pi * power / 16))
        sine = sign * float(np.sin(2 * np.pi * power / 16))
        if power == 4:
            return (-i, r) if sign > 0 else (i, -r)
        return (r * cosine - i * sine, r * sine + i * cosine)

    points = list(zip(real, imag))
    inner = [four(*(points[4 * j1 + j0] for j1 in range(4))) for j0 in range(4)]
    out = [None] * 16
    for b1 in range(4):
        column = [turned(inner[j0][b1], j0 * b1) for j0 in range(4)]
        for b0, value in enumerate(four(*column)):
            out[b1 + 4 * b0] = value
    return [v[0] for v in out], [v[1] for v in out]


def left_terms(value):
    high, low = split(value)
    return jnp.concatenate([high, low, high], axis=1)


def right_terms(value):
    high, low = split(value)
    return jnp.concatenate([high, high, low], axis=0)


def where_equal(left, right):
    return jnp.where(left == right, 1.0, 0.0).astype(jnp.bfloat16)


COPIES = 4
GROUP = 8


def spectral_kernel(extent, chunk, operands, rows_ref, codes_ref, *refs):
    sources, (kept_out, sent_out), refs = refs[:operands], refs[operands : operands + 2], refs[operands + 2 :]
    tables, (kept_ref, sent_ref), refs = refs[:operands], refs[operands : operands + 2], refs[operands + 2 :]
    grids, refs = refs[: 2 * COPIES], refs[2 * COPIES :]
    grids = [grids[2 * i : 2 * i + 2] for i in range(COPIES)]
    rows, dense, sem, out_sem = refs[:2], refs[2], refs[3], refs[4]
    near_ref, distant_ref, cube_ref, turn_ref, back_ref = tables[:5]
    even_ref, odd_ref, uneven_ref, unodd_ref = tables[5:9]
    line_ref, unline_ref, twist_ref, filter_ref = tables[9:13]
    plane_ref, unplane_ref, full_ref, unfull_ref, edge_ref = tables[13:]
    pieces, blocks = kept_ref.shape[:2]
    half_count = pieces * blocks
    slabs = extent // CUBE_COLS
    half = extent // 2
    lead = pieces // 4
    taken = chunk // blocks
    bunch = min(lead, taken)

    def other_place(place):
        first, second = place // lead % 2, place // (2 * lead)
        return place % lead + lead * (second + 2 * first)

    moves = [
        pltpu.make_async_copy(source, table, sem.at[i])
        for i, (source, table) in enumerate(zip(sources, tables))
    ]
    early, late = [moves[0], *moves[2:4]], moves[1:2]
    for move in early:
        move.start()

    def clear(i, _):
        place = pl.ds(pl.multiple_of(i * 64, 64), 64)
        for grid in grids:
            for ref in grid:
                ref[place, :] = jnp.zeros((64, LANES), jnp.float32)
        return 0

    lax.fori_loop(0, slabs * extent // 64, clear, 0)
    dense[...] = jnp.zeros(dense.shape, jnp.float32)

    def marks(start):
        codes = jnp.transpose(codes_ref[:, pl.ds(start, chunk)])
        turn_count = extent // CUBE_ROWS
        wide = lax.broadcasted_iota(jnp.int32, (chunk, extent), 1)
        turn_lane = lax.broadcasted_iota(jnp.int32, (chunk, 2 * turn_count), 1) % turn_count
        turned = dot_in(where_equal(turn_lane, codes[:, 1:2]), turn_ref[...])
        return codes, wide, turned[:, :LANES], turned[:, LANES:]

    def spread(source_ref, offset, step, _):
        start = pl.multiple_of(offset + step * chunk, chunk)
        values = source_ref[pl.ds(step * taken, taken), :blocks, :]
        both = dot_in(left_terms(values.reshape(chunk, LANES)), cube_ref[...])
        codes, wide, cosine, sine = marks(start)
        real, imag = both[:, :LANES], both[:, LANES : 2 * LANES]
        rows[0][...] = real * cosine + imag * sine
        rows[1][...] = imag * cosine - real * sine
        high, low = split(jnp.where(wide // CUBE_COLS == codes[:, 2:3], both[:, 2 * LANES :], 0.0))
        plane = where_equal(wide, codes[:, 0:1])
        contract = (((0,), (0,)), ((), ()))
        dense[...] += lax.dot_general(
            plane, high, contract, preferred_element_type=jnp.float32
        ) + lax.dot_general(plane, low, contract, preferred_element_type=jnp.float32)

        def add(i, _):
            for copy in range(COPIES):
                place = i + copy * (chunk // COPIES)
                row = rows_ref[start + place]
                for ref, source in zip(grids[copy], rows):
                    ref[pl.ds(row, 1), :] += source[pl.ds(place, 1), :]
            return 0

        lax.fori_loop(0, chunk // COPIES, add, 0, unroll=16)
        return 0

    for move in early:
        move.wait()
    for move in late + moves[4:]:
        move.start()
    for index, source_ref in enumerate((near_ref, distant_ref)):
        if index:
            for move in late:
                move.wait()
        body = functools.partial(spread, source_ref, index * half_count)
        lax.fori_loop(0, half_count // chunk, body, 0)

    grid_real, grid_imag = grids[0]

    def across(sign):
        def body(i, _):
            start = pl.multiple_of(i * 8, 8)
            places = [pl.ds(start + slab * extent, 8) for slab in range(slabs)]
            values = []
            for part in range(2):
                values.append([grids[0][part][place, :] for place in places])
                if sign < 0:
                    for grid in grids[1:]:
                        values[part] = [v + grid[part][p, :] for v, p in zip(values[part], places)]
            values = butterfly16(*values, sign)
            for place, r, j in zip(places, *values):
                grid_real[place, :] = r
                grid_imag[place, :] = j
            return 0

        lax.fori_loop(0, extent // 8, body, 0, unroll=2)

    across(-1)
    for move in moves[4:]:
        move.wait()

    def middle(group, _):
        starts = [pl.multiple_of((GROUP * group + i) * extent, extent) for i in range(GROUP)]
        cuts = [slice(i * LANES, (i + 1) * LANES) for i in range(GROUP)]

        def joined(offset):
            return jnp.concatenate(
                [
                    jnp.concatenate([ref[pl.ds(start + offset, half), :] for start in starts], axis=1)
                    for ref in grids[0]
                ],
                axis=0,
            )

        first, last = joined(0), joined(half)
        even = dot_in(even_ref[...], right_terms(first + last))
        odd = dot_in(odd_ref[...], right_terms(first - last))
        real = jnp.concatenate([even[:half], odd[:half]], axis=0)
        imag = jnp.concatenate([even[half:], odd[half:]], axis=0)
        cosine, sine = twist_ref[group, 0:1, :], twist_ref[group, 1:2, :]
        real, imag = real * cosine + imag * sine, imag * cosine - real * sine
        lines = jnp.concatenate(
            [
                jnp.concatenate([real[:, cut], imag[:, cut]], axis=1)
                for cut in cuts
            ],
            axis=0,
        )
        lines = dot_in(left_terms(lines), line_ref[...])
        scale = jnp.concatenate([filter_ref[GROUP * group + i] for i in range(GROUP)], axis=0)
        lines = lines * jnp.concatenate([scale, scale], axis=1)
        lines = dot_in(left_terms(lines), unline_ref[...])
        lines = [lines[i * extent : (i + 1) * extent] for i in range(GROUP)]
        real = jnp.concatenate([line[:, :LANES] for line in lines], axis=1)
        imag = jnp.concatenate([line[:, LANES:] for line in lines], axis=1)
        real, imag = real * cosine - imag * sine, imag * cosine + real * sine
        even = jnp.concatenate([real[:half], imag[:half]], axis=0)
        odd = jnp.concatenate([real[half:], imag[half:]], axis=0)
        even = dot_in(uneven_ref[...], right_terms(even))
        odd = dot_in(unodd_ref[...], right_terms(odd))
        for offset, planes in ((0, even + odd), (half, even - odd)):
            for part, ref in enumerate(grids[0]):
                for i, start in enumerate(starts):
                    ref[pl.ds(start + offset, half), :] = planes[
                        part * half : (part + 1) * half, i * LANES : (i + 1) * LANES
                    ]
        return 0

    lax.fori_loop(0, slabs // GROUP, middle, 0, unroll=1)
    planes = dot_in(plane_ref[...], right_terms(dense[...]))
    some = planes.shape[0] // 2
    planes = jnp.concatenate([planes[:some], planes[some:]], axis=1)
    planes = dot_in(left_terms(planes), full_ref[...])
    planes = planes * jnp.concatenate([edge_ref[...], edge_ref[...]], axis=1)
    planes = dot_in(left_terms(planes), unfull_ref[...])
    planes = jnp.concatenate([planes[:, :extent], planes[:, extent:]], axis=0)
    dense[...] = dot_in(unplane_ref[...], right_terms(planes))
    across(1)

    def leaving(index, step):
        out, ref = (kept_out, sent_out)[index], (kept_ref, sent_ref)[index]
        cut = blocks // 2
        place = pl.ds(step * taken, taken)
        moves = [(ref.at[place, :cut, :], out.at[0, place])]
        for i in range(taken // bunch):
            start = step * taken + i * bunch
            goal = out.at[1, pl.ds(other_place(start), bunch)]
            moves.append((ref.at[pl.ds(start, bunch), cut:, :], goal))
        return [
            pltpu.make_async_copy(*move, out_sem.at[index, step, i])
            for i, move in enumerate(moves)
        ]

    def collect(index, step, _):
        out_ref = (kept_ref, sent_ref)[index]
        offset = index * half_count
        start = pl.multiple_of(offset + step * chunk, chunk)

        def take(i, _):
            row = rows_ref[start + i]
            for ref, source in zip(rows, grids[0]):
                ref[pl.ds(i, 1), :] = source[pl.ds(row, 1), :]
            return 0

        lax.fori_loop(0, chunk, take, 0, unroll=32)
        codes, wide, cosine, sine = marks(start)
        plane = where_equal(wide, codes[:, 0:1])
        high, low = split(dense[...])
        edge = dot_in(plane, high) + dot_in(plane, low)
        edge = jnp.where(wide // CUBE_COLS == codes[:, 2:3], edge, 0.0)
        real, imag = rows[0][...], rows[1][...]
        both = jnp.concatenate(
            [real * cosine - imag * sine, imag * cosine + real * sine, edge], axis=1
        )
        both = dot_in(left_terms(both), back_ref[...])
        out_ref[pl.ds(step * taken, taken), :, :] = both.reshape(taken, blocks, LANES)
        for move in leaving(index, step):
            move.start()
        return 0

    for index in range(2):
        lax.fori_loop(0, half_count // chunk, functools.partial(collect, index), 0)

    def finish(step, _):
        for index in range(2):
            for move in leaving(index, step):
                move.wait()
        return 0

    lax.fori_loop(0, half_count // chunk, finish, 0)


def stacked_table(table, axis):
    table = np.asarray(table, np.float32)
    high = table.astype(jnp.bfloat16)
    low = (table - high.astype(np.float32)).astype(jnp.bfloat16)
    order = [high, high, low] if axis == 0 else [high, low, high]
    return jnp.asarray(np.concatenate(order, axis=axis))


def constant_tables(extent):
    half = extent // 2
    n0 = np.arange(half)
    planes = []
    for k0 in (np.arange(0, extent, 2), np.arange(1, extent, 2)):
        angle = 2.0 * np.pi / extent * (k0[:, None] * n0[None, :] % extent)
        cosine, sine = np.cos(angle), np.sin(angle)
        planes.append(np.block([[cosine, sine], [-sine, cosine]]))
    small = np.arange(CUBE_COLS)
    angle = 2.0 * np.pi / CUBE_COLS * (small[:, None] * small[None, :] % CUBE_COLS)
    cosine = np.kron(np.eye(LANES // CUBE_COLS), np.cos(angle))
    sine = np.kron(np.eye(LANES // CUBE_COLS), np.sin(angle))
    line = np.block([[cosine, -sine], [sine, cosine]])
    angle = 2.0 * np.pi / extent * (small[:, None] * (np.arange(LANES) % CUBE_COLS)[None, :])
    twist = np.stack([np.cos(angle), np.sin(angle)], axis=1)
    twist = np.concatenate([twist[i::GROUP] for i in range(GROUP)], axis=2)
    some = np.arange(-(-(half + 1) // 8) * 8)
    whole = np.arange(extent)
    angle = 2.0 * np.pi / extent * (some[:, None] * whole[None, :] % extent)
    plane = np.concatenate([np.cos(angle), -np.sin(angle)], axis=0)
    angle = 2.0 * np.pi / extent * (whole[:, None] * whole[None, :] % extent)
    cosine, sine = np.cos(angle), np.sin(angle)
    full = np.block([[cosine, -sine], [sine, cosine]])
    first = [stacked_table(table, 1) for table in (*planes, planes[0].T, planes[1].T)]
    first += [stacked_table(line, 0), stacked_table(line.T, 0), jnp.asarray(twist, jnp.float32)]
    last = [stacked_table(plane, 1), stacked_table(plane.T, 1)]
    last += [stacked_table(full, 0), stacked_table(full.T, 0)]
    return first, last


def tables_kernel(extent, held, place_ref, cube_ref, back_ref, turn_ref):
    first = place_ref[0]
    points = CUBE_ROWS * CUBE_COLS

    def angles(numerator):
        angle = (2.0 * np.pi / extent) * (numerator % extent).astype(jnp.float32)
        return jnp.cos(angle), jnp.sin(angle)

    for shape, axis in (((points, LANES), 0), ((LANES, points), 1)):
        point = lax.broadcasted_iota(jnp.int32, shape, axis)
        column = lax.broadcasted_iota(jnp.int32, shape, 1 - axis)
        k1 = first + column // CUBE_COLS
        cosine, sine = angles((point // CUBE_COLS) * k1)
        same = (point % CUBE_COLS == column % CUBE_COLS) & (column // CUBE_COLS < held)
        shape = (points, extent) if axis == 0 else (extent, points)
        point = lax.broadcasted_iota(jnp.int32, shape, axis)
        column = lax.broadcasted_iota(jnp.int32, shape, 1 - axis)
        flip = 1.0 - 2.0 * ((point // CUBE_COLS) % 2).astype(jnp.float32)
        edge = jnp.where(point % CUBE_COLS == column % CUBE_COLS, flip, 0.0)
        table = jnp.concatenate(
            [jnp.where(same, cosine, 0.0), jnp.where(same, -sine, 0.0), edge], axis=1 - axis
        )
        (cube_ref if axis == 0 else back_ref)[...] = right_terms(table)
    shape = (extent // CUBE_ROWS, LANES)
    column = lax.broadcasted_iota(jnp.int32, shape, 1)
    turn = lax.broadcasted_iota(jnp.int32, shape, 0) * CUBE_ROWS
    high, low = split(jnp.concatenate(angles(turn * (first + column // CUBE_COLS)), axis=1))
    turn_ref[...] = jnp.concatenate([high, low], axis=0)


def filter_kernel(extent, slab, place_ref, kernel_ref, sort_ref, filter_ref, *lines):
    first, shift = place_ref[0], place_ref[1]
    held = slab // 2
    batch = kernel_ref.shape[0]
    count = batch // slab // 2
    step = pl.program_id(0)
    values = kernel_ref[...]
    high = values.astype(jnp.bfloat16)
    rest = values - high.astype(jnp.float32)
    values = dot_in(jnp.concatenate([high, *split(rest)], axis=1), sort_ref[...])
    for side, ref in enumerate(lines):
        ref[...] = values[:, side * LANES : (side + 1) * LANES]
    groups = LANES // CUBE_COLS
    lane = lax.broadcasted_iota(jnp.int32, (1, LANES), 1)
    weight = jnp.where(first + lane // CUBE_COLS == 0, 1.0, 2.0) / float(extent) ** 3
    weight = jnp.where(lane // CUBE_COLS < held, weight, 0.0)
    group = lax.broadcasted_iota(jnp.int32, (count, LANES), 1) // CUBE_COLS
    for odd in range(2):
        row = pl.multiple_of(odd * (extent // 2) + step * count, count)
        for side, ref in enumerate(lines):
            values = [
                ref[pl.ds(shift + k + odd * slab, count, stride=2 * slab), :]
                if k < held
                else jnp.zeros((count, LANES), jnp.float32)
                for k in range(groups)
            ]
            apart = 1
            while apart < groups:
                upper = group // apart % 2 == 1
                turned = list(values)
                for k in range(groups):
                    if k // apart % 2 == 0:
                        one, two = values[k], values[k + apart]
                        turned[k] = jnp.where(upper, pltpu.roll(two, apart * CUBE_COLS, 1), one)
                        turned[k + apart] = jnp.where(
                            upper, two, pltpu.roll(one, LANES - apart * CUBE_COLS, 1)
                        )
                values = turned
                apart *= 2
            for k in range(groups):
                filter_ref[side * groups + k, pl.ds(row, count), :] = values[k] * weight


def spectral_tables(kernel_local):
    members = lax.axis_size("px")
    me = lax.axis_index("px")
    extent, slab = kernel_local.shape[:2]
    shift = (me >= members // 2).astype(jnp.int32)
    k2 = np.arange(extent)
    sort = np.zeros((extent, extent), np.float32)
    sort[k2, k2 % CUBE_COLS * CUBE_COLS + k2 // CUBE_COLS] = 1.0
    whole = pl.BlockSpec(memory_space=pltpu.VMEM)
    points = CUBE_ROWS * CUBE_COLS
    size = 2 * LANES + extent
    place = jnp.stack([me * slab + shift, shift])
    scalars = pl.BlockSpec(memory_space=pltpu.SMEM)
    cube_tables = pl.pallas_call(
        functools.partial(tables_kernel, extent, slab // 2),
        out_shape=(
            jax.ShapeDtypeStruct((3 * points, size), jnp.bfloat16),
            jax.ShapeDtypeStruct((3 * size, points), jnp.bfloat16),
            jax.ShapeDtypeStruct((2 * extent // CUBE_ROWS, 2 * LANES), jnp.bfloat16),
        ),
        in_specs=[scalars],
        out_specs=(whole,) * 3,
        cost_estimate=pl.CostEstimate(
            flops=0, bytes_accessed=128 * extent * extent, transcendentals=0
        ),
        compiler_params=pltpu.CompilerParams(vmem_limit_bytes=VMEM_BYTES),
        name="tables",
    )(place)
    batch = 32 * slab
    filters = pl.pallas_call(
        functools.partial(filter_kernel, extent, slab),
        grid=(extent * slab // batch,),
        out_shape=jax.ShapeDtypeStruct((CUBE_COLS, extent, LANES), jnp.float32),
        in_specs=[
            scalars,
            pl.BlockSpec((batch, extent), lambda i: (i, 0)),
            pl.BlockSpec((3 * extent, extent), lambda i: (0, 0)),
        ],
        out_specs=pl.BlockSpec((CUBE_COLS, extent, LANES), lambda i: (0, 0, 0)),
        scratch_shapes=[pltpu.VMEM((batch, LANES), jnp.float32)] * 2,
        cost_estimate=pl.CostEstimate(
            flops=2 * extent * slab * 3 * extent * extent,
            bytes_accessed=8 * extent * slab * extent,
            transcendentals=0,
        ),
        compiler_params=pltpu.CompilerParams(vmem_limit_bytes=VMEM_BYTES // 4),
        name="filters",
    )(
        place,
        kernel_local.reshape(extent * slab, extent),
        jnp.asarray(np.concatenate([sort] * 3, axis=0), jnp.bfloat16),
    )
    first, last = constant_tables(extent)
    some = last[0].shape[0] // 2
    k0 = np.arange(some)
    weight = np.where((k0 == 0) | (k0 == extent // 2), 1.0, 2.0) * (k0 <= extent // 2)
    weight = jnp.asarray(weight / float(extent) ** 3, jnp.float32)[:, None]
    edge = jnp.where(me == members // 2, kernel_local[:some, 0, :] * weight, 0.0)
    return edge, cube_tables, filters, first, last


def cube_places(cubes, extent):
    slabs = extent // CUBE_COLS
    turns = extent // CUBE_ROWS
    plane, turn, slab = cubes // (turns * slabs), cubes // slabs % turns, cubes % slabs
    codes = jnp.stack([plane, turn, slab] + [jnp.zeros_like(slab)] * 5, axis=0)
    return slab * extent + plane, codes


def spectral(places, extent, blocks, gathered, tables):
    cube, back, turn, constants = tables
    pieces = gathered[0].shape[0]
    slabs = extent // CUBE_COLS
    taken = min(4, pieces)
    chunk = taken * blocks
    operands = (*gathered, cube, turn, back, *constants)
    anywhere = pl.BlockSpec(memory_space=pl.ANY)
    fixed = pl.BlockSpec(memory_space=pltpu.HBM)
    out = jax.ShapeDtypeStruct((2, pieces, blocks // 2, LANES), jnp.float32)
    return pl.pallas_call(
        functools.partial(spectral_kernel, extent, chunk, len(operands)),
        out_shape=(out, out),
        in_specs=[
            pl.BlockSpec(memory_space=pltpu.SMEM),
            pl.BlockSpec(memory_space=pltpu.VMEM),
            *[anywhere] * 2,
            *[fixed] * (len(operands) - 2),
        ],
        out_specs=(anywhere, anywhere),
        scratch_shapes=[pltpu.VMEM(operand.shape, operand.dtype) for operand in operands]
        + [pltpu.VMEM((pieces, blocks, LANES), jnp.float32)] * 2
        + [pltpu.VMEM((slabs * extent, LANES), jnp.float32)] * (2 * COPIES)
        + [pltpu.VMEM((chunk, LANES), jnp.float32)] * 2
        + [pltpu.VMEM((extent, extent), jnp.float32)]
        + [pltpu.SemaphoreType.DMA((len(operands),))]
        + [pltpu.SemaphoreType.DMA((2, pieces // taken, 5))],
        compiler_params=pltpu.CompilerParams(vmem_limit_bytes=SPECTRAL_BYTES),
        name="spectral",
    )(places[0], places[1], *operands)


NOTE_ROWS = 8
STEP_BLOCKS = 32
RIM_PART = 4


def sum_row(*values):
    lane = lax.broadcasted_iota(jnp.int32, (1, LANES), 1)
    row = jnp.zeros((1, LANES), jnp.float32)
    for index, value in enumerate(values):
        row = jnp.where(lane == index, value, row)
    return row


def put_edges(out_ref, values):
    step, steps = pl.program_id(0), pl.num_programs(0)
    panels = values.shape[1]
    below = out_ref.shape[0] - steps * STEP_BLOCKS // RIM_PART

    for first, lanes in ((0, slice(0, panels)), (steps - steps // RIM_PART, slice(panels, 2 * panels))):

        @pl.when((step >= first) & (step < first + steps // RIM_PART))
        def _():
            row = pl.multiple_of(below + (step - first) * STEP_BLOCKS, 8)
            out_ref[pl.ds(row, STEP_BLOCKS), lanes] = values


def project_kernel(proj_ref, values_ref, note_ref, out_ref):
    step = pl.program_id(0)
    charges = jnp.sum(proj_ref[...] * values_ref[...][:, :, None], axis=1)
    out_ref[pl.ds(pl.multiple_of(step * STEP_BLOCKS, STEP_BLOCKS), STEP_BLOCKS), :] = charges

    put_edges(out_ref, values_ref[...])

    @pl.when(step == pl.num_programs(0) - 1)
    def _():
        blocks = pl.num_programs(0) * STEP_BLOCKS
        out_ref[blocks : blocks + NOTE_ROWS, :] = jnp.broadcast_to(
            note_ref[...], (NOTE_ROWS, LANES)
        )


def complete_kernel(proj_ref, picked_ref, base_ref, rhs_ref, image_ref, out_ref):
    step = pl.program_id(0)
    tiles = proj_ref[...]
    image = base_ref[...] + jnp.sum(tiles * picked_ref[...][:, None, :], axis=2)
    image_ref[...] = image
    charges = jnp.sum(tiles * image[:, :, None], axis=1)
    out_ref[pl.ds(pl.multiple_of(step * STEP_BLOCKS, STEP_BLOCKS), STEP_BLOCKS), :] = charges
    put_edges(out_ref, image)
    blocks = pl.num_programs(0) * STEP_BLOCKS
    rhs = rhs_ref[...]
    row = sum_row(jnp.sum(rhs * rhs), jnp.sum(rhs * image), jnp.sum(image * image))

    @pl.when(step == 0)
    def _():
        out_ref[blocks : blocks + NOTE_ROWS, :] = jnp.zeros((NOTE_ROWS, LANES), jnp.float32)

    out_ref[blocks : blocks + 1, :] += row


def vector_scalars(sums):
    norm_sq, mixed, image_sq = sums[0:1, 0:1], sums[0:1, 1:2], sums[0:1, 2:3]
    gram_one = image_sq / norm_sq
    return jnp.sqrt(norm_sq), mixed / norm_sq, gram_one, jnp.sqrt(gram_one)


def close_kernel(proj_ref, picked_ref, base_ref, rhs_ref, first_ref, sums_ref, image_ref, out_ref):
    step = pl.program_id(0)
    second = base_ref[...] + jnp.sum(proj_ref[...] * picked_ref[...][:, None, :], axis=2)
    initial_norm, diag_one, _, scale = vector_scalars(sums_ref[...])
    basis_one = rhs_ref[...] / initial_norm
    image_one = first_ref[...] / initial_norm
    image_two = (second / initial_norm - diag_one * image_one) / scale
    image_ref[...] = image_two
    row = sum_row(
        jnp.sum(basis_one * image_two),
        jnp.sum(image_one * image_two),
        jnp.sum(image_two * image_two),
    )

    @pl.when(step == 0)
    def _():
        out_ref[...] = jnp.zeros((NOTE_ROWS, LANES), jnp.float32)

    out_ref[0:1, :] += row


def finish_kernel(rhs_ref, first_ref, image_ref, sums_ref, last_ref, answer_ref, residual_ref, rows_ref):
    initial_norm, diag_one, gram_one, scale = vector_scalars(sums_ref[...])
    last = last_ref[...]
    upper_two, gram_cross, gram_two = last[0:1, 0:1], last[0:1, 1:2], last[0:1, 2:3]
    rhs = rhs_ref[...]
    basis_one = rhs / initial_norm
    image_one = first_ref[...] / initial_norm
    basis_two = (image_one - diag_one * basis_one) / scale
    determinant = gram_one * gram_two - gram_cross * gram_cross
    weight_one = initial_norm * (diag_one * gram_two - upper_two * gram_cross) / determinant
    weight_two = initial_norm * (upper_two * gram_one - diag_one * gram_cross) / determinant
    half = rhs.shape[0] // 2
    for out_ref, value in (
        (answer_ref, weight_one * basis_one + weight_two * basis_two),
        (residual_ref, rhs - weight_one * image_one - weight_two * image_ref[...]),
    ):
        rows_ref[...] = value
        out_ref[...] = jnp.concatenate(
            [rows_ref[pl.ds(side, half, stride=2), :] for side in range(2)], axis=1
        )


def local_call(kernel, name, proj_tiles, rows, whole, outs):
    blocks, panels, points = proj_tiles.shape

    def cut(width):
        return pl.BlockSpec((STEP_BLOCKS, width), lambda i: (i, 0))

    def uncut(shape):
        return pl.BlockSpec(shape, lambda i: (0, 0))

    out_specs = [cut(out[1]) if out[0] == blocks else uncut(out) for out in outs]
    return pl.pallas_call(
        kernel,
        grid=(blocks // STEP_BLOCKS,),
        out_shape=[jax.ShapeDtypeStruct(out, jnp.float32) for out in outs],
        in_specs=[pl.BlockSpec((STEP_BLOCKS, panels, points), lambda i: (i, 0, 0))]
        + [cut(row.shape[1]) for row in rows]
        + [uncut(value.shape) for value in whole],
        out_specs=out_specs,
        cost_estimate=pl.CostEstimate(
            flops=4 * proj_tiles.size, bytes_accessed=4 * proj_tiles.size, transcendentals=0
        ),
        compiler_params=pltpu.CompilerParams(vmem_limit_bytes=VMEM_BYTES // 4),
        name=name,
    )(proj_tiles, *rows, *whole)


def piece_place(device):
    steps = partner_steps(lax.axis_size("px"))[:-1]
    away = lax.axis_index("px") ^ device
    return sum((away // step % 2) << place for place, step in enumerate(steps))


def halo(cells, distant):
    me, members = lax.axis_index("px"), lax.axis_size("px")
    width = cells.shape[0] // RIM_PART
    panels = cells.shape[1]
    sides = []
    for device, lane, present in ((me - 1, panels, me > 0), (me + 1, 0, me < members - 1)):
        place = jnp.where(present, piece_place(device), 0)
        start = (place, distant.shape[1] - width, lane)
        edge = lax.dynamic_slice(distant, start, (1, width, panels))[0]
        sides.append(jnp.where(present, edge, 0.0))
    return jnp.concatenate([sides[0], cells, sides[1]], axis=0)


def on_device(
    right_side, self_term, proj_tiles, owner_dev, cube_slot, near_src, near_tiles, kernel_hat
):
    members = lax.axis_size("px")
    blocks = proj_tiles.shape[0]
    extent = kernel_hat.shape[0]
    cubes_dev = extent // members * (extent // CUBE_ROWS) * (extent // CUBE_COLS)
    self_local = self_term.reshape(blocks, 64)
    cubes = owner_dev[:, 0] * cubes_dev + cube_slot
    *late, first, last = spectral_tables(kernel_hat)

    rhs = right_side.reshape(blocks, 64)
    note_shape = (blocks + NOTE_ROWS + blocks // RIM_PART, LANES)

    def base_of(values, extended):
        sources = extended[near_src].reshape(blocks, near_tiles.shape[2])
        return self_local * values + jnp.sum(near_tiles * sources[:, None, :], axis=2)

    def far(places, gathered, values):
        extended = halo(values, gathered[1])
        shares = spectral(places, extent, blocks, gathered, tables)
        picked, extended = scatter_pieces(*shares, extended)
        return picked, base_of(values, extended)

    note = jnp.pad(cubes.astype(jnp.float32)[None, :], ((0, 0), (0, LANES - blocks)))
    (payload,) = local_call(project_kernel, "project", proj_tiles, [rhs], [note], [note_shape])
    gathered, (edge, cube_tables, filters) = gather_pieces(payload, late)
    tables = (*cube_tables, (*first, filters, *last, edge))
    all_cubes = jnp.concatenate([half[:, blocks, :blocks] for half in gathered], axis=0)
    places = cube_places(all_cubes.astype(jnp.int32).reshape(members * blocks), extent)
    image_one, payload = local_call(
        complete_kernel,
        "complete",
        proj_tiles,
        [*far(places, gathered, rhs), rhs],
        [],
        [(blocks, 64), note_shape],
    )
    gathered, _ = gather_pieces(payload, ())
    sums = sum(jnp.sum(half[:, blocks, :], axis=0, keepdims=True) for half in gathered)
    image, weights = local_call(
        close_kernel,
        "close",
        proj_tiles,
        [*far(places, gathered, image_one), rhs, image_one],
        [sums],
        [(blocks, 64), (NOTE_ROWS, LANES)],
    )
    weights = total(weights)
    out = jax.ShapeDtypeStruct((blocks // 2, 128), jnp.float32)
    answer, residual = pl.pallas_call(
        finish_kernel,
        out_shape=(out, out),
        scratch_shapes=[pltpu.VMEM((blocks, 64), jnp.float32)],
        name="finish",
    )(rhs, image_one, image, sums, weights)
    return (answer.reshape(blocks * 64), residual.reshape(blocks * 64))


def solution(mesh):
    return jax.shard_map(
        on_device,
        mesh=mesh,
        in_specs=(
            P(("groups", "px")),
            P(("groups", "px")),
            P(("groups", "px"), None, None),
            P(("groups", "px"), None),
            P(("groups", "px")),
            P(("groups", "px"), None),
            P(("groups", "px"), None, None),
            P(None, "px", None),
        ),
        out_specs=(P(("groups", "px")), P(("groups", "px"))),
        check_vma=False,
    )
```

```python
import functools
import jax
import jax.numpy as jnp
import numpy as np
from jax import lax
from jax.experimental import pallas as pl
from jax.experimental.pallas import tpu as pltpu
from jax.sharding import PartitionSpec as P

LANES = 128
CUBE_ROWS = 8
CUBE_COLS = 16
VMEM_BYTES = 60 * 1024 * 1024
SPECTRAL_BYTES = 60 * 1024 * 1024


def split(value):
    high = value.astype(jnp.bfloat16)
    low = (value - high.astype(jnp.float32)).astype(jnp.bfloat16)
    return high, low


def dot_in(left, right):
    return jnp.dot(left, right, preferred_element_type=jnp.float32)


def partner_steps(members):
    return [1 << i for i in reversed(range(members.bit_length() - 1))]


def exchange(value, step):
    members = lax.axis_size("px")
    return lax.ppermute(value, "px", [(i, i ^ step) for i in range(members)])


def step_orders(members):
    steps = partner_steps(members)
    return steps[:-3], (steps[-3:-1], steps[-3:-1][::-1]), steps[-1]


def gather_pieces(piece, beside):
    steps = partner_steps(lax.axis_size("px"))
    pieces = piece[None]
    done = []
    for index, step in enumerate(steps[:-1]):
        pieces = jnp.concatenate([pieces, exchange(pieces, step)], axis=0)
        if index < len(beside):
            pieces, value = lax.optimization_barrier((pieces, beside[index]))
            done.append(value)
    return (pieces, exchange(pieces, steps[-1])), done


def scatter_pieces(kept, sent, beside):
    lead, orders, last = step_orders(lax.axis_size("px"))
    arrived = exchange(sent, last)
    parts = [kept[i] + arrived[i] for i in range(2)]
    parts, beside = lax.optimization_barrier((parts, beside))
    for steps in zip(*(order[::-1] for order in orders)):
        half = parts[0].shape[0] // 2
        parts = [part[:half] + exchange(part[half:], step) for part, step in zip(parts, steps)]
    pieces = jnp.concatenate(parts, axis=1)
    for step in lead[::-1]:
        half = pieces.shape[0] // 2
        pieces = pieces[:half] + exchange(pieces[half:], step)
    return pieces[0], beside


def total(value):
    members = lax.axis_size("px")
    copies = jnp.broadcast_to(value[None], (members, *value.shape))
    return jnp.sum(lax.all_to_all(copies, "px", 0, 0), axis=0)


def butterfly16(real, imag, sign):
    def four(a, b, c, d):
        (ar, ai), (br, bi), (cr, ci), (dr, di) = a, b, c, d
        sr, si, tr, ti = ar + cr, ai + ci, ar - cr, ai - ci
        ur, ui, vr, vi = br + dr, bi + di, br - dr, bi - di
        wr, wi = (-vi, vr) if sign > 0 else (vi, -vr)
        return (sr + ur, si + ui), (tr + wr, ti + wi), (sr - ur, si - ui), (tr - wr, ti - wi)

    def turned(value, power):
        power %= 16
        if power == 0:
            return value
        r, i = value
        cosine = float(np.cos(2 * np.pi * power / 16))
        sine = sign * float(np.sin(2 * np.pi * power / 16))
        if power == 4:
            return (-i, r) if sign > 0 else (i, -r)
        return (r * cosine - i * sine, r * sine + i * cosine)

    points = list(zip(real, imag))
    inner = [four(*(points[4 * j1 + j0] for j1 in range(4))) for j0 in range(4)]
    out = [None] * 16
    for b1 in range(4):
        column = [turned(inner[j0][b1], j0 * b1) for j0 in range(4)]
        for b0, value in enumerate(four(*column)):
            out[b1 + 4 * b0] = value
    return [v[0] for v in out], [v[1] for v in out]


def left_terms(value):
    high, low = split(value)
    return jnp.concatenate([high, low, high], axis=1)


def right_terms(value):
    high, low = split(value)
    return jnp.concatenate([high, high, low], axis=0)


def where_equal(left, right):
    return jnp.where(left == right, 1.0, 0.0).astype(jnp.bfloat16)


COPIES = 4
GROUP = 8


def spectral_kernel(extent, chunk, operands, rows_ref, codes_ref, *refs):
    sources, (kept_out, sent_out), refs = refs[:operands], refs[operands : operands + 2], refs[operands + 2 :]
    tables, (kept_ref, sent_ref), refs = refs[:operands], refs[operands : operands + 2], refs[operands + 2 :]
    grids, refs = refs[: 2 * COPIES], refs[2 * COPIES :]
    grids = [grids[2 * i : 2 * i + 2] for i in range(COPIES)]
    rows, dense, sem, out_sem = refs[:2], refs[2], refs[3], refs[4]
    near_ref, distant_ref, cube_ref, turn_ref, back_ref = tables[:5]
    even_ref, odd_ref, uneven_ref, unodd_ref = tables[5:9]
    line_ref, unline_ref, twist_ref, filter_ref = tables[9:13]
    plane_ref, unplane_ref, full_ref, unfull_ref, edge_ref = tables[13:]
    pieces, blocks = kept_ref.shape[:2]
    half_count = pieces * blocks
    slabs = extent // CUBE_COLS
    half = extent // 2
    lead = pieces // 4
    taken = chunk // blocks
    bunch = min(lead, taken)

    def other_place(place):
        first, second = place // lead % 2, place // (2 * lead)
        return place % lead + lead * (second + 2 * first)

    moves = [
        pltpu.make_async_copy(source, table, sem.at[i])
        for i, (source, table) in enumerate(zip(sources, tables))
    ]
    early, late = [moves[0], *moves[2:4]], moves[1:2]
    for move in early:
        move.start()

    def clear(i, _):
        place = pl.ds(pl.multiple_of(i * 64, 64), 64)
        for grid in grids:
            for ref in grid:
                ref[place, :] = jnp.zeros((64, LANES), jnp.float32)
        return 0

    lax.fori_loop(0, slabs * extent // 64, clear, 0)
    dense[...] = jnp.zeros(dense.shape, jnp.float32)

    def marks(start):
        codes = jnp.transpose(codes_ref[:, pl.ds(start, chunk)])
        turn_count = extent // CUBE_ROWS
        wide = lax.broadcasted_iota(jnp.int32, (chunk, extent), 1)
        turn_lane = lax.broadcasted_iota(jnp.int32, (chunk, 2 * turn_count), 1) % turn_count
        turned = dot_in(where_equal(turn_lane, codes[:, 1:2]), turn_ref[...])
        return codes, wide, turned[:, :LANES], turned[:, LANES:]

    def spread(source_ref, offset, step, _):
        start = pl.multiple_of(offset + step * chunk, chunk)
        values = source_ref[pl.ds(step * taken, taken), :blocks, :]
        both = dot_in(left_terms(values.reshape(chunk, LANES)), cube_ref[...])
        codes, wide, cosine, sine = marks(start)
        real, imag = both[:, :LANES], both[:, LANES : 2 * LANES]
        rows[0][...] = real * cosine + imag * sine
        rows[1][...] = imag * cosine - real * sine
        high, low = split(jnp.where(wide // CUBE_COLS == codes[:, 2:3], both[:, 2 * LANES :], 0.0))
        plane = where_equal(wide, codes[:, 0:1])
        contract = (((0,), (0,)), ((), ()))
        dense[...] += lax.dot_general(
            plane, high, contract, preferred_element_type=jnp.float32
        ) + lax.dot_general(plane, low, contract, preferred_element_type=jnp.float32)

        def add(i, _):
            for copy in range(COPIES):
                place = i + copy * (chunk // COPIES)
                row = rows_ref[start + place]
                for ref, source in zip(grids[copy], rows):
                    ref[pl.ds(row, 1), :] += source[pl.ds(place, 1), :]
            return 0

        lax.fori_loop(0, chunk // COPIES, add, 0, unroll=32)
        return 0

    for move in early:
        move.wait()
    for move in late + moves[4:]:
        move.start()
    for index, source_ref in enumerate((near_ref, distant_ref)):
        if index:
            for move in late:
                move.wait()
        body = functools.partial(spread, source_ref, index * half_count)
        lax.fori_loop(0, half_count // chunk, body, 0)

    grid_real, grid_imag = grids[0]

    def across(sign):
        def body(i, _):
            start = pl.multiple_of(i * 8, 8)
            places = [pl.ds(start + slab * extent, 8) for slab in range(slabs)]
            values = []
            for part in range(2):
                values.append([grids[0][part][place, :] for place in places])
                if sign < 0:
                    for grid in grids[1:]:
                        values[part] = [v + grid[part][p, :] for v, p in zip(values[part], places)]
            values = butterfly16(*values, sign)
            for place, r, j in zip(places, *values):
                grid_real[place, :] = r
                grid_imag[place, :] = j
            return 0

        lax.fori_loop(0, extent // 8, body, 0, unroll=4)

    across(-1)
    for move in moves[4:]:
        move.wait()

    def middle(group, _):
        starts = [pl.multiple_of((GROUP * group + i) * extent, extent) for i in range(GROUP)]
        cuts = [slice(i * LANES, (i + 1) * LANES) for i in range(GROUP)]

        def joined(offset):
            return jnp.concatenate(
                [
                    jnp.concatenate([ref[pl.ds(start + offset, half), :] for start in starts], axis=1)
                    for ref in grids[0]
                ],
                axis=0,
            )

        first, last = joined(0), joined(half)
        even = dot_in(even_ref[...], right_terms(first + last))
        odd = dot_in(odd_ref[...], right_terms(first - last))
        real = jnp.concatenate([even[:half], odd[:half]], axis=0)
        imag = jnp.concatenate([even[half:], odd[half:]], axis=0)
        cosine, sine = twist_ref[group, 0:1, :], twist_ref[group, 1:2, :]
        real, imag = real * cosine + imag * sine, imag * cosine - real * sine
        lines = jnp.concatenate(
            [
                jnp.concatenate([real[:, cut], imag[:, cut]], axis=1)
                for cut in cuts
            ],
            axis=0,
        )
        lines = dot_in(left_terms(lines), line_ref[...])
        scale = jnp.concatenate([filter_ref[GROUP * group + i] for i in range(GROUP)], axis=0)
        lines = lines * jnp.concatenate([scale, scale], axis=1)
        lines = dot_in(left_terms(lines), unline_ref[...])
        lines = [lines[i * extent : (i + 1) * extent] for i in range(GROUP)]
        real = jnp.concatenate([line[:, :LANES] for line in lines], axis=1)
        imag = jnp.concatenate([line[:, LANES:] for line in lines], axis=1)
        real, imag = real * cosine - imag * sine, imag * cosine + real * sine
        even = jnp.concatenate([real[:half], imag[:half]], axis=0)
        odd = jnp.concatenate([real[half:], imag[half:]], axis=0)
        even = dot_in(uneven_ref[...], right_terms(even))
        odd = dot_in(unodd_ref[...], right_terms(odd))
        for offset, planes in ((0, even + odd), (half, even - odd)):
            for part, ref in enumerate(grids[0]):
                for i, start in enumerate(starts):
                    ref[pl.ds(start + offset, half), :] = planes[
                        part * half : (part + 1) * half, i * LANES : (i + 1) * LANES
                    ]
        return 0

    lax.fori_loop(0, slabs // GROUP, middle, 0, unroll=1)
    planes = dot_in(plane_ref[...], right_terms(dense[...]))
    some = planes.shape[0] // 2
    planes = jnp.concatenate([planes[:some], planes[some:]], axis=1)
    planes = dot_in(left_terms(planes), full_ref[...])
    planes = planes * jnp.concatenate([edge_ref[...], edge_ref[...]], axis=1)
    planes = dot_in(left_terms(planes), unfull_ref[...])
    planes = jnp.concatenate([planes[:, :extent], planes[:, extent:]], axis=0)
    dense[...] = dot_in(unplane_ref[...], right_terms(planes))
    across(1)

    def leaving(index, step):
        out, ref = (kept_out, sent_out)[index], (kept_ref, sent_ref)[index]
        cut = blocks // 2
        place = pl.ds(step * taken, taken)
        moves = [(ref.at[place, :cut, :], out.at[0, place])]
        for i in range(taken // bunch):
            start = step * taken + i * bunch
            goal = out.at[1, pl.ds(other_place(start), bunch)]
            moves.append((ref.at[pl.ds(start, bunch), cut:, :], goal))
        return [
            pltpu.make_async_copy(*move, out_sem.at[index, step, i])
            for i, move in enumerate(moves)
        ]

    def collect(index, step, _):
        out_ref = (kept_ref, sent_ref)[index]
        offset = index * half_count
        start = pl.multiple_of(offset + step * chunk, chunk)

        def take(i, _):
            row = rows_ref[start + i]
            for ref, source in zip(rows, grids[0]):
                ref[pl.ds(i, 1), :] = source[pl.ds(row, 1), :]
            return 0

        lax.fori_loop(0, chunk, take, 0, unroll=64)
        codes, wide, cosine, sine = marks(start)
        plane = where_equal(wide, codes[:, 0:1])
        high, low = split(dense[...])
        edge = dot_in(plane, high) + dot_in(plane, low)
        edge = jnp.where(wide // CUBE_COLS == codes[:, 2:3], edge, 0.0)
        real, imag = rows[0][...], rows[1][...]
        both = jnp.concatenate(
            [real * cosine - imag * sine, imag * cosine + real * sine, edge], axis=1
        )
        both = dot_in(left_terms(both), back_ref[...])
        out_ref[pl.ds(step * taken, taken), :, :] = both.reshape(taken, blocks, LANES)
        for move in leaving(index, step):
            move.start()
        return 0

    for index in range(2):
        lax.fori_loop(0, half_count // chunk, functools.partial(collect, index), 0)

    def finish(step, _):
        for index in range(2):
            for move in leaving(index, step):
                move.wait()
        return 0

    lax.fori_loop(0, half_count // chunk, finish, 0)


def stacked_table(table, axis):
    table = np.asarray(table, np.float32)
    high = table.astype(jnp.bfloat16)
    low = (table - high.astype(np.float32)).astype(jnp.bfloat16)
    order = [high, high, low] if axis == 0 else [high, low, high]
    return jnp.asarray(np.concatenate(order, axis=axis))


def constant_tables(extent):
    half = extent // 2
    n0 = np.arange(half)
    planes = []
    for k0 in (np.arange(0, extent, 2), np.arange(1, extent, 2)):
        angle = 2.0 * np.pi / extent * (k0[:, None] * n0[None, :] % extent)
        cosine, sine = np.cos(angle), np.sin(angle)
        planes.append(np.block([[cosine, sine], [-sine, cosine]]))
    small = np.arange(CUBE_COLS)
    angle = 2.0 * np.pi / CUBE_COLS * (small[:, None] * small[None, :] % CUBE_COLS)
    cosine = np.kron(np.eye(LANES // CUBE_COLS), np.cos(angle))
    sine = np.kron(np.eye(LANES // CUBE_COLS), np.sin(angle))
    line = np.block([[cosine, -sine], [sine, cosine]])
    angle = 2.0 * np.pi / extent * (small[:, None] * (np.arange(LANES) % CUBE_COLS)[None, :])
    twist = np.stack([np.cos(angle), np.sin(angle)], axis=1)
    twist = np.concatenate([twist[i::GROUP] for i in range(GROUP)], axis=2)
    some = np.arange(-(-(half + 1) // 8) * 8)
    whole = np.arange(extent)
    angle = 2.0 * np.pi / extent * (some[:, None] * whole[None, :] % extent)
    plane = np.concatenate([np.cos(angle), -np.sin(angle)], axis=0)
    angle = 2.0 * np.pi / extent * (whole[:, None] * whole[None, :] % extent)
    cosine, sine = np.cos(angle), np.sin(angle)
    full = np.block([[cosine, -sine], [sine, cosine]])
    first = [stacked_table(table, 1) for table in (*planes, planes[0].T, planes[1].T)]
    first += [stacked_table(line, 0), stacked_table(line.T, 0), jnp.asarray(twist, jnp.float32)]
    last = [stacked_table(plane, 1), stacked_table(plane.T, 1)]
    last += [stacked_table(full, 0), stacked_table(full.T, 0)]
    return first, last


def tables_kernel(extent, held, place_ref, cube_ref, back_ref, turn_ref):
    first = place_ref[0]
    points = CUBE_ROWS * CUBE_COLS

    def angles(numerator):
        angle = (2.0 * np.pi / extent) * (numerator % extent).astype(jnp.float32)
        return jnp.cos(angle), jnp.sin(angle)

    for shape, axis in (((points, LANES), 0), ((LANES, points), 1)):
        point = lax.broadcasted_iota(jnp.int32, shape, axis)
        column = lax.broadcasted_iota(jnp.int32, shape, 1 - axis)
        k1 = first + column // CUBE_COLS
        cosine, sine = angles((point // CUBE_COLS) * k1)
        same = (point % CUBE_COLS == column % CUBE_COLS) & (column // CUBE_COLS < held)
        shape = (points, extent) if axis == 0 else (extent, points)
        point = lax.broadcasted_iota(jnp.int32, shape, axis)
        column = lax.broadcasted_iota(jnp.int32, shape, 1 - axis)
        flip = 1.0 - 2.0 * ((point // CUBE_COLS) % 2).astype(jnp.float32)
        edge = jnp.where(point % CUBE_COLS == column % CUBE_COLS, flip, 0.0)
        table = jnp.concatenate(
            [jnp.where(same, cosine, 0.0), jnp.where(same, -sine, 0.0), edge], axis=1 - axis
        )
        (cube_ref if axis == 0 else back_ref)[...] = right_terms(table)
    shape = (extent // CUBE_ROWS, LANES)
    column = lax.broadcasted_iota(jnp.int32, shape, 1)
    turn = lax.broadcasted_iota(jnp.int32, shape, 0) * CUBE_ROWS
    high, low = split(jnp.concatenate(angles(turn * (first + column // CUBE_COLS)), axis=1))
    turn_ref[...] = jnp.concatenate([high, low], axis=0)


def filter_kernel(extent, slab, place_ref, kernel_ref, sort_ref, filter_ref, *lines):
    first, shift = place_ref[0], place_ref[1]
    held = slab // 2
    batch = kernel_ref.shape[0]
    count = batch // slab // 2
    step = pl.program_id(0)
    values = kernel_ref[...]
    high = values.astype(jnp.bfloat16)
    rest = values - high.astype(jnp.float32)
    values = dot_in(jnp.concatenate([high, *split(rest)], axis=1), sort_ref[...])
    for side, ref in enumerate(lines):
        ref[...] = values[:, side * LANES : (side + 1) * LANES]
    groups = LANES // CUBE_COLS
    lane = lax.broadcasted_iota(jnp.int32, (1, LANES), 1)
    weight = jnp.where(first + lane // CUBE_COLS == 0, 1.0, 2.0) / float(extent) ** 3
    weight = jnp.where(lane // CUBE_COLS < held, weight, 0.0)
    group = lax.broadcasted_iota(jnp.int32, (count, LANES), 1) // CUBE_COLS
    for odd in range(2):
        row = pl.multiple_of(odd * (extent // 2) + step * count, count)
        for side, ref in enumerate(lines):
            values = [
                ref[pl.ds(shift + k + odd * slab, count, stride=2 * slab), :]
                if k < held
                else jnp.zeros((count, LANES), jnp.float32)
                for k in range(groups)
            ]
            apart = 1
            while apart < groups:
                upper = group // apart % 2 == 1
                turned = list(values)
                for k in range(groups):
                    if k // apart % 2 == 0:
                        one, two = values[k], values[k + apart]
                        turned[k] = jnp.where(upper, pltpu.roll(two, apart * CUBE_COLS, 1), one)
                        turned[k + apart] = jnp.where(
                            upper, two, pltpu.roll(one, LANES - apart * CUBE_COLS, 1)
                        )
                values = turned
                apart *= 2
            for k in range(groups):
                filter_ref[side * groups + k, pl.ds(row, count), :] = values[k] * weight


def spectral_tables(kernel_local):
    members = lax.axis_size("px")
    me = lax.axis_index("px")
    extent, slab = kernel_local.shape[:2]
    shift = (me >= members // 2).astype(jnp.int32)
    k2 = np.arange(extent)
    sort = np.zeros((extent, extent), np.float32)
    sort[k2, k2 % CUBE_COLS * CUBE_COLS + k2 // CUBE_COLS] = 1.0
    whole = pl.BlockSpec(memory_space=pltpu.VMEM)
    points = CUBE_ROWS * CUBE_COLS
    size = 2 * LANES + extent
    place = jnp.stack([me * slab + shift, shift])
    scalars = pl.BlockSpec(memory_space=pltpu.SMEM)
    cube_tables = pl.pallas_call(
        functools.partial(tables_kernel, extent, slab // 2),
        out_shape=(
            jax.ShapeDtypeStruct((3 * points, size), jnp.bfloat16),
            jax.ShapeDtypeStruct((3 * size, points), jnp.bfloat16),
            jax.ShapeDtypeStruct((2 * extent // CUBE_ROWS, 2 * LANES), jnp.bfloat16),
        ),
        in_specs=[scalars],
        out_specs=(whole,) * 3,
        cost_estimate=pl.CostEstimate(
            flops=0, bytes_accessed=128 * extent * extent, transcendentals=0
        ),
        compiler_params=pltpu.CompilerParams(vmem_limit_bytes=VMEM_BYTES),
        name="tables",
    )(place)
    batch = 32 * slab
    filters = pl.pallas_call(
        functools.partial(filter_kernel, extent, slab),
        grid=(extent * slab // batch,),
        out_shape=jax.ShapeDtypeStruct((CUBE_COLS, extent, LANES), jnp.float32),
        in_specs=[
            scalars,
            pl.BlockSpec((batch, extent), lambda i: (i, 0)),
            pl.BlockSpec((3 * extent, extent), lambda i: (0, 0)),
        ],
        out_specs=pl.BlockSpec((CUBE_COLS, extent, LANES), lambda i: (0, 0, 0)),
        scratch_shapes=[pltpu.VMEM((batch, LANES), jnp.float32)] * 2,
        cost_estimate=pl.CostEstimate(
            flops=2 * extent * slab * 3 * extent * extent,
            bytes_accessed=8 * extent * slab * extent,
            transcendentals=0,
        ),
        compiler_params=pltpu.CompilerParams(vmem_limit_bytes=VMEM_BYTES // 4),
        name="filters",
    )(
        place,
        kernel_local.reshape(extent * slab, extent),
        jnp.asarray(np.concatenate([sort] * 3, axis=0), jnp.bfloat16),
    )
    first, last = constant_tables(extent)
    some = last[0].shape[0] // 2
    k0 = np.arange(some)
    weight = np.where((k0 == 0) | (k0 == extent // 2), 1.0, 2.0) * (k0 <= extent // 2)
    weight = jnp.asarray(weight / float(extent) ** 3, jnp.float32)[:, None]
    edge = jnp.where(me == members // 2, kernel_local[:some, 0, :] * weight, 0.0)
    return edge, cube_tables, filters, first, last


def cube_places(cubes, extent):
    slabs = extent // CUBE_COLS
    turns = extent // CUBE_ROWS
    plane, turn, slab = cubes // (turns * slabs), cubes // slabs % turns, cubes % slabs
    codes = jnp.stack([plane, turn, slab] + [jnp.zeros_like(slab)] * 5, axis=0)
    return slab * extent + plane, codes


def spectral(places, extent, blocks, gathered, tables):
    cube, back, turn, constants = tables
    pieces = gathered[0].shape[0]
    slabs = extent // CUBE_COLS
    taken = min(4, pieces)
    chunk = taken * blocks
    operands = (*gathered, cube, turn, back, *constants)
    anywhere = pl.BlockSpec(memory_space=pl.ANY)
    fixed = pl.BlockSpec(memory_space=pltpu.HBM)
    out = jax.ShapeDtypeStruct((2, pieces, blocks // 2, LANES), jnp.float32)
    return pl.pallas_call(
        functools.partial(spectral_kernel, extent, chunk, len(operands)),
        out_shape=(out, out),
        in_specs=[
            pl.BlockSpec(memory_space=pltpu.SMEM),
            pl.BlockSpec(memory_space=pltpu.VMEM),
            *[anywhere] * 2,
            *[fixed] * (len(operands) - 2),
        ],
        out_specs=(anywhere, anywhere),
        scratch_shapes=[pltpu.VMEM(operand.shape, operand.dtype) for operand in operands]
        + [pltpu.VMEM((pieces, blocks, LANES), jnp.float32)] * 2
        + [pltpu.VMEM((slabs * extent, LANES), jnp.float32)] * (2 * COPIES)
        + [pltpu.VMEM((chunk, LANES), jnp.float32)] * 2
        + [pltpu.VMEM((extent, extent), jnp.float32)]
        + [pltpu.SemaphoreType.DMA((len(operands),))]
        + [pltpu.SemaphoreType.DMA((2, pieces // taken, 5))],
        compiler_params=pltpu.CompilerParams(vmem_limit_bytes=SPECTRAL_BYTES),
        name="spectral",
    )(places[0], places[1], *operands)


NOTE_ROWS = 8
STEP_BLOCKS = 32
RIM_PART = 4


def sum_row(*values):
    lane = lax.broadcasted_iota(jnp.int32, (1, LANES), 1)
    row = jnp.zeros((1, LANES), jnp.float32)
    for index, value in enumerate(values):
        row = jnp.where(lane == index, value, row)
    return row


def put_edges(out_ref, values):
    step, steps = pl.program_id(0), pl.num_programs(0)
    panels = values.shape[1]
    below = out_ref.shape[0] - steps * STEP_BLOCKS // RIM_PART

    for first, lanes in ((0, slice(0, panels)), (steps - steps // RIM_PART, slice(panels, 2 * panels))):

        @pl.when((step >= first) & (step < first + steps // RIM_PART))
        def _():
            row = pl.multiple_of(below + (step - first) * STEP_BLOCKS, 8)
            out_ref[pl.ds(row, STEP_BLOCKS), lanes] = values


def project_kernel(proj_ref, values_ref, note_ref, out_ref):
    step = pl.program_id(0)
    charges = jnp.sum(proj_ref[...] * values_ref[...][:, :, None], axis=1)
    out_ref[pl.ds(pl.multiple_of(step * STEP_BLOCKS, STEP_BLOCKS), STEP_BLOCKS), :] = charges

    put_edges(out_ref, values_ref[...])

    @pl.when(step == pl.num_programs(0) - 1)
    def _():
        blocks = pl.num_programs(0) * STEP_BLOCKS
        out_ref[blocks : blocks + NOTE_ROWS, :] = jnp.broadcast_to(
            note_ref[...], (NOTE_ROWS, LANES)
        )


def complete_kernel(proj_ref, picked_ref, base_ref, rhs_ref, image_ref, out_ref):
    step = pl.program_id(0)
    tiles = proj_ref[...]
    image = base_ref[...] + jnp.sum(tiles * picked_ref[...][:, None, :], axis=2)
    image_ref[...] = image
    charges = jnp.sum(tiles * image[:, :, None], axis=1)
    out_ref[pl.ds(pl.multiple_of(step * STEP_BLOCKS, STEP_BLOCKS), STEP_BLOCKS), :] = charges
    put_edges(out_ref, image)
    blocks = pl.num_programs(0) * STEP_BLOCKS
    rhs = rhs_ref[...]
    row = sum_row(jnp.sum(rhs * rhs), jnp.sum(rhs * image), jnp.sum(image * image))

    @pl.when(step == 0)
    def _():
        out_ref[blocks : blocks + NOTE_ROWS, :] = jnp.zeros((NOTE_ROWS, LANES), jnp.float32)

    out_ref[blocks : blocks + 1, :] += row


def vector_scalars(sums):
    norm_sq, mixed, image_sq = sums[0:1, 0:1], sums[0:1, 1:2], sums[0:1, 2:3]
    gram_one = image_sq / norm_sq
    return jnp.sqrt(norm_sq), mixed / norm_sq, gram_one, jnp.sqrt(gram_one)


def close_kernel(proj_ref, picked_ref, base_ref, rhs_ref, first_ref, sums_ref, image_ref, out_ref):
    step = pl.program_id(0)
    second = base_ref[...] + jnp.sum(proj_ref[...] * picked_ref[...][:, None, :], axis=2)
    initial_norm, diag_one, _, scale = vector_scalars(sums_ref[...])
    basis_one = rhs_ref[...] / initial_norm
    image_one = first_ref[...] / initial_norm
    image_two = (second / initial_norm - diag_one * image_one) / scale
    image_ref[...] = image_two
    row = sum_row(
        jnp.sum(basis_one * image_two),
        jnp.sum(image_one * image_two),
        jnp.sum(image_two * image_two),
    )

    @pl.when(step == 0)
    def _():
        out_ref[...] = jnp.zeros((NOTE_ROWS, LANES), jnp.float32)

    out_ref[0:1, :] += row


def finish_kernel(rhs_ref, first_ref, image_ref, sums_ref, last_ref, answer_ref, residual_ref, rows_ref):
    initial_norm, diag_one, gram_one, scale = vector_scalars(sums_ref[...])
    last = last_ref[...]
    upper_two, gram_cross, gram_two = last[0:1, 0:1], last[0:1, 1:2], last[0:1, 2:3]
    rhs = rhs_ref[...]
    basis_one = rhs / initial_norm
    image_one = first_ref[...] / initial_norm
    basis_two = (image_one - diag_one * basis_one) / scale
    determinant = gram_one * gram_two - gram_cross * gram_cross
    weight_one = initial_norm * (diag_one * gram_two - upper_two * gram_cross) / determinant
    weight_two = initial_norm * (upper_two * gram_one - diag_one * gram_cross) / determinant
    half = rhs.shape[0] // 2
    for out_ref, value in (
        (answer_ref, weight_one * basis_one + weight_two * basis_two),
        (residual_ref, rhs - weight_one * image_one - weight_two * image_ref[...]),
    ):
        rows_ref[...] = value
        out_ref[...] = jnp.concatenate(
            [rows_ref[pl.ds(side, half, stride=2), :] for side in range(2)], axis=1
        )


def local_call(kernel, name, proj_tiles, rows, whole, outs):
    blocks, panels, points = proj_tiles.shape

    def cut(width):
        return pl.BlockSpec((STEP_BLOCKS, width), lambda i: (i, 0))

    def uncut(shape):
        return pl.BlockSpec(shape, lambda i: (0, 0))

    out_specs = [cut(out[1]) if out[0] == blocks else uncut(out) for out in outs]
    return pl.pallas_call(
        kernel,
        grid=(blocks // STEP_BLOCKS,),
        out_shape=[jax.ShapeDtypeStruct(out, jnp.float32) for out in outs],
        in_specs=[pl.BlockSpec((STEP_BLOCKS, panels, points), lambda i: (i, 0, 0))]
        + [cut(row.shape[1]) for row in rows]
        + [uncut(value.shape) for value in whole],
        out_specs=out_specs,
        cost_estimate=pl.CostEstimate(
            flops=4 * proj_tiles.size, bytes_accessed=4 * proj_tiles.size, transcendentals=0
        ),
        compiler_params=pltpu.CompilerParams(vmem_limit_bytes=VMEM_BYTES // 4),
        name=name,
    )(proj_tiles, *rows, *whole)


def piece_place(device):
    steps = partner_steps(lax.axis_size("px"))[:-1]
    away = lax.axis_index("px") ^ device
    return sum((away // step % 2) << place for place, step in enumerate(steps))


def halo(cells, distant):
    me, members = lax.axis_index("px"), lax.axis_size("px")
    width = cells.shape[0] // RIM_PART
    panels = cells.shape[1]
    sides = []
    for device, lane, present in ((me - 1, panels, me > 0), (me + 1, 0, me < members - 1)):
        place = jnp.where(present, piece_place(device), 0)
        start = (place, distant.shape[1] - width, lane)
        edge = lax.dynamic_slice(distant, start, (1, width, panels))[0]
        sides.append(jnp.where(present, edge, 0.0))
    return jnp.concatenate([sides[0], cells, sides[1]], axis=0)


def on_device(
    right_side, self_term, proj_tiles, owner_dev, cube_slot, near_src, near_tiles, kernel_hat
):
    members = lax.axis_size("px")
    blocks = proj_tiles.shape[0]
    extent = kernel_hat.shape[0]
    cubes_dev = extent // members * (extent // CUBE_ROWS) * (extent // CUBE_COLS)
    self_local = self_term.reshape(blocks, 64)
    cubes = owner_dev[:, 0] * cubes_dev + cube_slot
    *late, first, last = spectral_tables(kernel_hat)

    rhs = right_side.reshape(blocks, 64)
    note_shape = (blocks + NOTE_ROWS + blocks // RIM_PART, LANES)

    def base_of(values, extended):
        sources = extended[near_src].reshape(blocks, near_tiles.shape[2])
        return self_local * values + jnp.sum(near_tiles * sources[:, None, :], axis=2)

    def far(places, gathered, values):
        extended = halo(values, gathered[1])
        shares = spectral(places, extent, blocks, gathered, tables)
        picked, extended = scatter_pieces(*shares, extended)
        return picked, base_of(values, extended)

    note = jnp.pad(cubes.astype(jnp.float32)[None, :], ((0, 0), (0, LANES - blocks)))
    (payload,) = local_call(project_kernel, "project", proj_tiles, [rhs], [note], [note_shape])
    gathered, (edge, cube_tables, filters) = gather_pieces(payload, late)
    tables = (*cube_tables, (*first, filters, *last, edge))
    all_cubes = jnp.concatenate([half[:, blocks, :blocks] for half in gathered], axis=0)
    places = cube_places(all_cubes.astype(jnp.int32).reshape(members * blocks), extent)
    image_one, payload = local_call(
        complete_kernel,
        "complete",
        proj_tiles,
        [*far(places, gathered, rhs), rhs],
        [],
        [(blocks, 64), note_shape],
    )
    gathered, _ = gather_pieces(payload, ())
    sums = sum(jnp.sum(half[:, blocks, :], axis=0, keepdims=True) for half in gathered)
    image, weights = local_call(
        close_kernel,
        "close",
        proj_tiles,
        [*far(places, gathered, image_one), rhs, image_one],
        [sums],
        [(blocks, 64), (NOTE_ROWS, LANES)],
    )
    weights = total(weights)
    out = jax.ShapeDtypeStruct((blocks // 2, 128), jnp.float32)
    answer, residual = pl.pallas_call(
        finish_kernel,
        out_shape=(out, out),
        scratch_shapes=[pltpu.VMEM((blocks, 64), jnp.float32)],
        name="finish",
    )(rhs, image_one, image, sums, weights)
    return (answer.reshape(blocks * 64), residual.reshape(blocks * 64))


def solution(mesh):
    return jax.shard_map(
        on_device,
        mesh=mesh,
        in_specs=(
            P(("groups", "px")),
            P(("groups", "px")),
            P(("groups", "px"), None, None),
            P(("groups", "px"), None),
            P(("groups", "px")),
            P(("groups", "px"), None),
            P(("groups", "px"), None, None),
            P(None, "px", None),
        ),
        out_specs=(P(("groups", "px")), P(("groups", "px"))),
        check_vma=False,
    )
```
